32 devices in a mesh: gx: 4 (over y, core), gy: 4 (over z), gz: 2 (over x).
Axes of the slice: x: 2, y: 2, z: 4, core: 2. Of those that a mesh axis runs over, the one named last changes fastest.
Arguments:
- residual_in: float32 [32, 128, 512], P('gz', 'gy', 'gx'), may hold values from -6 to 6
- labels: int32 [32, 128, 512], P('gz', 'gy', 'gx'), may hold values 0 or 1
- factor: float32 [3, 32, 128, 512], P(None, 'gz', 'gy', 'gx'), may hold values from 0.5 to 2
- basis: float32 [4, 8, 8, 8], replicated, may hold values from 0.05 to 0.25
- basis_index: int32 [4, 16, 64], P('gz', 'gy', 'gx'), may hold values from 0 to 3
Outputs:
- preconditioned: float32 [32, 128, 512], P('gz', 'gy', 'gx')
- coarse_correction: float32 [4, 16, 64], P('gz', 'gy', 'gx')
The draws below stay inside these ranges and needn't reach their ends.
All inputs are finite; a program needn't handle non-finite values. No bound on the sum of `labels` on one device may be relied on, other than what follows from the above.
Results may differ from the reference program's by a relative error of at most 0.0003.
Values sent between devices are 32-bit elements; how exact they have to be, the bound alone decides.
No kernel may reach another device: no remote copies, remote signals or barrier semaphores. Data moves between devices by JAX's collectives and lax.ppermute only.
A program may use at most 64 MiB of HBM per device.

```python
import math
import jax
import jax.numpy as jnp
from jax import lax

BLK = 8
NBASIS = 4
CITERS = 4
NX = 512
NY = 128
NZ = 32
NXC = 64
NYC = 16
NZC = 4


def with_ends(drawn, own_key, least, largest):
    longest = drawn.shape.index(max(drawn.shape))
    spots = []
    for shift in (0, 1):
        where = [jax.random.randint(jax.random.fold_in(own_key, axis), (), 0, length) for axis, length in enumerate(drawn.shape)]
        where[longest] = (where[longest] + shift) % drawn.shape[longest]
        spots.append(tuple(where))
    return drawn.at[spots[0]].set(least).at[spots[1]].set(largest)


def block_scale(key, dims, pieces, least, largest):
    def one(axis_at, shards_of):
        draws = jax.random.uniform(jax.random.fold_in(jax.random.fold_in(key, 6), axis_at), (shards_of,), jnp.float32, least / len(pieces), largest / len(pieces))
        return jnp.repeat(jnp.exp(draws), dims[axis_at] // shards_of).reshape((-1,) + (1,) * (len(dims) - axis_at - 1))

    loudness = one(*pieces[0])
    for cut in pieces[1:]:
        loudness = loudness * one(*cut)
    return loudness


def scatter_about(stream_key, shape, scale, reach, split=(), held_as=jnp.bfloat16):
    factor_of = block_scale(stream_key, shape, split, -0.22, 0.18) if split else 1.0
    entries = jax.random.normal(stream_key, shape, jnp.float32) * scale * factor_of
    return jnp.minimum(jnp.maximum(entries, -reach), reach).astype(held_as)


def setup_inputs(seed: int = 0) -> dict:
    keys = jax.random.split(jax.random.key(seed), 6)
    return {
        "residual_in": scatter_about(keys[0], (NZ, NY, NX), 1.0, 6.0, ((0, 2), (1, 4), (2, 4)), jnp.float32),
        "labels": with_ends((jax.random.randint(keys[1], (NZ, NY, NX), 0, 4) < 1).astype(jnp.int32), jax.random.fold_in(keys[1], 1), 0, 1),
        "factor": jnp.clip(jnp.exp(math.log(2.0) - 1.3862944 * jax.random.uniform(keys[2], (3, NZ, NY, NX), jnp.float32) ** block_scale(keys[2], (3, NZ, NY, NX), ((1, 2), (2, 4), (3, 4)), -0.2, 0.2)), 0.5, 2.0),
        "basis": jnp.clip(jax.random.uniform(keys[3], (NBASIS, BLK, BLK, BLK), jnp.float32, 0.05, 0.25), 0.05, 0.25),
        "basis_index": with_ends(jax.random.randint(keys[4], (NZC, NYC, NXC), 0, NBASIS), jax.random.fold_in(keys[4], 1), 0, NBASIS - 1).astype(jnp.int32),
    }


BRICK = (0.6, 1.0, 1.0)
MORTAR = (0.25, 0.3, 0.3)
MASS = 0.05
OMEGA = 0.8
WEIGHT_ONE = 1.0 / (1.05 - 0.95 * math.cos(math.pi / 4))
WEIGHT_TWO = 1.0 / (1.05 + 0.95 * math.cos(math.pi / 4))
STENCIL_W = {1: 1.0, 2: 0.5, 3: 0.25}
OFFSETS = [(i, j, k) for i in (-1, 0, 1) for j in (-1, 0, 1) for k in (-1, 0, 1) if (i, j, k) != (0, 0, 0)]


def material(labels, factor):
    rows = [jnp.where(labels == 1, MORTAR[axis_id], BRICK[axis_id]).astype(jnp.float32) * factor[axis_id] for axis_id in range(3)]
    return jnp.stack(rows)


def subset_means(padded):
    means = {}
    for offset in OFFSETS:
        subset = tuple(axis_id for axis_id in range(3) if offset[axis_id] != 0)
        if subset not in means:
            total = padded[subset[0]]
            for axis_id in subset[1:]:
                total = total + padded[axis_id]
            means[subset] = total / float(len(subset))
    return means


def window(values, lead, offset, extent):
    return values[lead + offset[0]:lead + offset[0] + extent[0], lead + offset[1]:lead + offset[1] + extent[1], lead + offset[2]:lead + offset[2] + extent[2]]


def couplings(padded, lead, extent, field):
    means = subset_means(padded)
    if field is None:
        full = (padded[0] + padded[1] + padded[2]) / 3.0
        total = MASS * window(full, lead, (0, 0, 0), extent)
    else:
        total = jnp.zeros(extent, jnp.float32)
    for offset in OFFSETS:
        subset = tuple(axis_id for axis_id in range(3) if offset[axis_id] != 0)
        values = means[subset]
        coupling = (0.5 * STENCIL_W[len(subset)]) * (window(values, lead, (0, 0, 0), extent) + window(values, lead, offset, extent))
        if field is None:
            total = total + coupling
        else:
            total = total + coupling * window(field, 1, offset, extent)
    return total


def coarse_terms(padded, field):
    center = padded[:, 1:-1, 1:-1, 1:-1]
    extent = center.shape[1:]
    if field is None:
        total = MASS * (center[0] + center[1] + center[2]) / 3.0
    else:
        total = jnp.zeros(extent, jnp.float32)
    for axis_id in range(3):
        for step in (-1, 1):
            offset = tuple(step if d == axis_id else 0 for d in range(3))
            coupling = 0.5 * (center[axis_id] + window(padded[axis_id], 1, offset, extent))
            if field is None:
                total = total + coupling
            else:
                total = total + coupling * window(field, 1, offset, extent)
    return total


def restrict(residual, basis, basis_index):
    zc, yc, xc = basis_index.shape
    blocks = residual.reshape(zc, BLK, yc, BLK, xc, BLK)
    terms = jnp.einsum("aibjck,nijk->abcn", blocks, basis, precision=lax.Precision.HIGHEST)
    onehot = (basis_index[..., None] == jnp.arange(basis.shape[0], dtype=jnp.int32)).astype(jnp.float32)
    return jnp.sum(terms * onehot, axis=-1), onehot


def prolong(coarse, onehot, basis):
    zc, yc, xc = coarse.shape
    weighted = coarse[..., None] * onehot
    fine = jnp.einsum("abcn,nijk->aibjck", weighted, basis, precision=lax.Precision.HIGHEST)
    return fine.reshape(zc * BLK, yc * BLK, xc * BLK)


def block_mean(kappa):
    comps, zn, yn, xn = kappa.shape
    return kappa.reshape(comps, zn // BLK, BLK, yn // BLK, BLK, xn // BLK, BLK).mean(axis=(2, 4, 6))


def reference(residual_in, labels, factor, basis, basis_index):
    kappa = material(labels, factor)
    extent = residual_in.shape
    padded = jnp.pad(kappa, ((0, 0), (1, 1), (1, 1), (1, 1)))
    diag = couplings(padded, 1, extent, None)
    first = WEIGHT_ONE * residual_in / diag
    off = couplings(padded, 1, extent, jnp.pad(first, 1))
    image = diag * first - off
    smooth = first + WEIGHT_TWO * (residual_in - image) / diag
    coarse_rhs, onehot = restrict(residual_in, basis, basis_index)
    coarse_pad = jnp.pad(block_mean(kappa), ((0, 0), (1, 1), (1, 1), (1, 1)))
    coarse_diag = coarse_terms(coarse_pad, None)
    estimate = OMEGA * coarse_rhs / coarse_diag
    for sweep in range(CITERS - 1):
        off_coarse = coarse_terms(coarse_pad, jnp.pad(estimate, 1))
        estimate = estimate + OMEGA * (coarse_rhs - (coarse_diag * estimate - off_coarse)) / coarse_diag
    preconditioned = smooth + prolong(estimate, onehot, basis)
    return preconditioned, estimate
```

```python
import math

import jax
import jax.numpy as jnp
from jax import lax
from jax.experimental import pallas as pl
from jax.experimental.pallas import tpu as pltpu
from jax.sharding import PartitionSpec as P

BLK = 8
CITERS = 4
BRICK = (0.6, 1.0, 1.0)
MORTAR = (0.25, 0.3, 0.3)
MASS = 0.05
OMEGA = 0.8
WEIGHT_ONE = 1.0 / (1.05 - 0.95 * math.cos(math.pi / 4))
WEIGHT_TWO = 1.0 / (1.05 + 0.95 * math.cos(math.pi / 4))
SELF = 1.0 + 1.0 + 1.0 / 3.0 + MASS / 3.0
KEEP = 1.0 + WEIGHT_TWO / WEIGHT_ONE - WEIGHT_TWO

NZ, NY, NX = 16, 32, 128
CZ, CY, CX = 2, 4, 16
F32 = jnp.float32
HIGHEST = lax.Precision.HIGHEST

ZPAY = 7 * NY + 8
KROWS = 36
RROW = 3 * KROWS
YCO = 128
YPAY = YCO + 8
XPAY = 40 + 8
RLANE = 110


def iota(shape, dim):
    return lax.broadcasted_iota(jnp.int32, shape, dim)


def roll(values, shift, axis):
    size = values.shape[axis]
    shift = shift % size
    return values if shift == 0 else pltpu.roll(values, shift, axis)


def both(values, step, axis):
    return roll(values, step, axis) + roll(values, -step, axis)


def take(values, lanes):
    return jnp.take_along_axis(values, lanes, axis=1, mode="promise_in_bounds")


def pair_stiffness(own, below, above):
    k0, k1, k2 = own
    d0, d1, d2 = (a + b if a is not None else b for a, b in zip(below, above))
    part_y = 0.5 * k1 + 0.125 * (d0 + d1)
    part_yx = 0.125 * (k1 + k2) + (1.0 / 24.0) * (d0 + d1 + d2)
    part_0 = 0.5 * d0
    part_x = 0.5 * k2 + 0.125 * (d0 + d2)
    return part_0, part_y, part_x, part_yx


def first_kernel(r_ref, lab_ref, fac_ref, bas_ref, bix_ref, kap_ref, rr_ref, sel_ref, zpay_ref, tile_ref, sum_ref):
    gz = lax.axis_index("gz")
    tiled = lax.dot_general(
        bas_ref[...].reshape(4 * BLK * BLK, BLK),
        (iota((BLK, NX), 1) % BLK == iota((BLK, NX), 0)).astype(F32),
        (((1,), (0,)), ((), ())),
        precision=HIGHEST,
        preferred_element_type=F32,
    )
    tile_ref[...] = tiled.reshape(4, BLK, BLK, NX)
    sum_ref[...] = jnp.zeros(sum_ref.shape, F32)
    spread = (iota((CX, NX), 1) // BLK == iota((CX, NX), 0)).astype(F32)
    for zc in range(CZ):
        index = lax.dot_general(
            bix_ref[jnp.where(gz == 0, zc, CZ - 1 - zc)].astype(F32),
            spread,
            (((1,), (0,)), ((), ())),
            precision=HIGHEST,
            preferred_element_type=F32,
        )
        index = jnp.concatenate([jnp.broadcast_to(index[y : y + 1], (BLK, NX)) for y in range(CY)], axis=0)
        sums = [None] * 4
        for i in range(BLK):
            zp = zc * BLK + i
            z = jnp.where(gz == 0, zp, NZ - 1 - zp)
            zi = jnp.where(gz == 0, i, BLK - 1 - i)
            mortar = lab_ref[z] == 1
            b0, b1, b2, b3 = (jnp.concatenate([tile_ref[n, zi]] * CY, axis=0) for n in range(4))
            basis = jnp.where(index < 1.5, jnp.where(index < 0.5, b0, b1), jnp.where(index < 2.5, b2, b3))
            res = r_ref[z]
            rr_ref[zp] = res
            sel_ref[zp] = basis
            terms = []
            for a in range(3):
                k = jnp.where(mortar, MORTAR[a], BRICK[a]) * fac_ref[a, z]
                kap_ref[a, zp] = k
                terms.append(k)
                if zp == NZ - 1:
                    zpay_ref[2 * a * NY : (2 * a + 1) * NY] = k
                if zp == NZ - 2:
                    zpay_ref[(2 * a + 1) * NY : (2 * a + 2) * NY] = k
            if zp == NZ - 1:
                zpay_ref[6 * NY : 7 * NY] = res
            terms.append(basis * res)
            sums = [t if s is None else s + t for s, t in zip(sums, terms)]
        for q in range(4):
            total = sums[q].reshape(CY, BLK, NX).sum(axis=1)
            sum_ref[(q * 2 + zc) * 8 : (q * 2 + zc) * 8 + CY] = total if q == 3 else total * (1.0 / BLK**3)
    bricks = lax.dot_general(
        sum_ref[...],
        (iota((NX, NX), 0) // BLK == iota((NX, NX), 1) % CX).astype(F32),
        (((1,), (0,)), ((), ())),
        precision=HIGHEST,
        preferred_element_type=F32,
    )
    group = iota((8, NX), 1) // CX
    coarse = bricks[0:8]
    for g in range(1, 8):
        coarse = jnp.where(group == g, bricks[g * 8 : g * 8 + 8], coarse)
    zpay_ref[7 * NY : 7 * NY + 8] = coarse


def rows_kernel(kap_ref, rr_ref, ya_ref, yb_ref):
    even = lax.axis_index("gy") % 2 == 0

    def put(at, low, high):
        ya_ref[at : at + low.shape[0]] = jnp.where(even, high, low)
        yb_ref[at : at + low.shape[0]] = jnp.where(even, low, high)

    for zp in range(NZ):
        for a in range(3):
            put(a * KROWS + 2 * zp, kap_ref[a, zp, 0:2], kap_ref[a, zp, NY - 2 : NY])
        put(RROW + zp, rr_ref[zp, 0:1], rr_ref[zp, NY - 1 : NY])


def rows_more_kernel(za_ref, zpay_ref, ya_in, yb_in, ya_ref, yb_ref):
    even = lax.axis_index("gy") % 2 == 0
    ya_ref[0:YCO] = ya_in[0:YCO]
    yb_ref[0:YCO] = yb_in[0:YCO]

    def put(at, low, high):
        ya_ref[at : at + low.shape[0]] = jnp.where(even, high, low)
        yb_ref[at : at + low.shape[0]] = jnp.where(even, low, high)

    for a in range(3):
        for s in range(2):
            base = (2 * a + s) * NY
            put(a * KROWS + 2 * (NZ + s), za_ref[base : base + 2], za_ref[base + NY - 2 : base + NY])
    put(RROW + NZ, za_ref[6 * NY : 6 * NY + 1], za_ref[7 * NY - 1 : 7 * NY])
    coarse = jnp.concatenate([zpay_ref[7 * NY : 7 * NY + CY], za_ref[7 * NY : 7 * NY + CY]], axis=0)
    ya_ref[YCO : YCO + 8] = coarse
    yb_ref[YCO : YCO + 8] = coarse


def pack_columns(planes, residuals, rows):
    lane = iota((rows, NX), 1)
    left = jnp.zeros((rows, NX), F32)
    right = jnp.zeros((rows, NX), F32)
    for a in range(3):
        for zp in range(NZ + 2):
            at = 2 + a * KROWS + 2 * zp
            moved = roll(planes(a, zp), at, 1)
            left = jnp.where((lane == at) | (lane == at + 1), moved, left)
            right = jnp.where((lane == at - 2) | (lane == at - 1), moved, right)
    for zp in range(NZ + 1):
        at = RLANE + zp
        moved = roll(residuals(zp), at, 1)
        left = jnp.where(lane == at, moved, left)
        right = jnp.where(lane == at - 1, moved, right)
    return left, right


def columns_kernel(kap_ref, rr_ref, za_ref, left_ref, right_ref):
    def plane(a, zp):
        if zp < NZ:
            return kap_ref[a, zp]
        base = (2 * a + zp - NZ) * NY
        return za_ref[base : base + NY]

    def residual(zp):
        return rr_ref[zp] if zp < NZ else za_ref[6 * NY : 7 * NY]

    left_ref[...], right_ref[...] = pack_columns(plane, residual, NY)


def columns_more_kernel(
    ra_ref, rb_ref, yb_ref, left_in, right_in, xa_ref, xb_ref, left_ref, right_ref, hal_ref, hr_ref, cor_ref, lo_ref, hi_ref
):
    gx, gy = lax.axis_index("gx"), lax.axis_index("gy")
    even = gy % 2 == 0
    zero = jnp.zeros((YPAY, NX), F32)
    hi_ref[...] = jnp.where(gy < lax.axis_size("gy") - 1, jnp.where(even, ra_ref[...], rb_ref[...]), zero)
    lo_ref[...] = jnp.where(gy > 0, jnp.where(even, rb_ref[...], ra_ref[...]), zero)
    hal_ref[...] = jnp.zeros(hal_ref.shape, F32)
    hr_ref[...] = jnp.zeros(hr_ref.shape, F32)
    for zp in range(NZ + 2):
        for a in range(3):
            at = a * KROWS + 2 * zp
            hal_ref[a, zp, 0:2] = hi_ref[at : at + 2]
            hal_ref[a, zp, 6:8] = lo_ref[at : at + 2]
        if zp <= NZ:
            hr_ref[zp, 0:1] = hi_ref[RROW + zp : RROW + zp + 1]
            hr_ref[zp, 7:8] = lo_ref[RROW + zp : RROW + zp + 1]
    more_left, more_right = pack_columns(lambda a, zp: hal_ref[a, zp], lambda zp: hr_ref[zp], 8)
    left_ref[0:NY] = left_in[...]
    right_ref[0:NY] = right_in[...]
    left_ref[NY : NY + 8] = more_left
    right_ref[NY : NY + 8] = more_right
    even_x = gx % 2 == 0
    xa_ref[0:40] = jnp.where(even_x, right_ref[...], left_ref[...])
    xb_ref[0:40] = jnp.where(even_x, left_ref[...], right_ref[...])
    tiles = [yb_ref[YCO : YCO + 8], lo_ref[YCO : YCO + 8], hi_ref[YCO : YCO + 8]]
    lane = iota((8, NX), 1)
    source = (lane % 32) // 4 * CX + lane % 4
    sides = []
    for shift in (0, CX - 4):
        parts = [take(t, source + shift) for t in tiles]
        sides.append(jnp.where(lane < 32, parts[0], jnp.where(lane < 64, parts[1], parts[2])))
    xa_ref[40:48] = jnp.where(even_x, sides[1], sides[0])
    xb_ref[40:48] = jnp.where(even_x, sides[0], sides[1])
    for i in range(3):
        cor_ref[i] = tiles[i]


def interior_kernel(kap_ref, rr_ref, za_ref, hal_ref, hr_ref, s1_ref, s2_ref, f_ref):
    rows = NY + 8
    lane = iota((rows, NX), 1)
    inner = (lane > 0) & (lane < NX - 1)
    not_first, not_last = lane > 0, lane < NX - 1

    def stiff(zp):
        if zp < 0:
            return (None, None, None)
        own = []
        for a in range(3):
            if zp < NZ:
                plane = kap_ref[a, zp]
            else:
                base = (2 * a + zp - NZ) * NY
                plane = za_ref[base : base + NY]
            own.append(jnp.concatenate([plane, hal_ref[a, zp]], axis=0))
        return own

    def along_x(values):
        n = values.shape[0]
        back = jnp.where(not_first[:n], roll(values, 1, 1), 0.0)
        return back + jnp.where(not_last[:n], roll(values, -1, 1), 0.0)

    def residual(zp):
        own = rr_ref[zp] if zp < NZ else za_ref[6 * NY : 7 * NY]
        return jnp.concatenate([own, hr_ref[zp]], axis=0)

    def first(zp):
        k = stiff(zp)
        part_0, part_y, part_x, part_yx = pair_stiffness(k, stiff(zp - 1), stiff(zp + 1))
        diag = SELF * (k[0] + k[1] + k[2]) + part_0 + both(part_y, 1, 0)
        diag = diag + along_x(part_x + both(part_yx, 1, 0))
        inv = 1.0 / diag
        return jnp.where(inner, WEIGHT_ONE * residual(zp) * inv, 0.0), inv

    def image(zp, inv):
        k = [v[:NY] for v in stiff(zp)]
        f = f_ref[zp]
        fz = f_ref[zp + 1]
        p = [v * f for v in stiff(zp)]
        above = [v * f_ref[zp + 1] for v in stiff(zp + 1)]
        if zp > 0:
            fz = fz + f_ref[zp - 1]
            above = [u + v * f_ref[zp - 1] for u, v in zip(above, stiff(zp - 1))]
        own_y = 0.5 * p[1] + 0.125 * (above[0] + above[1])
        own_yx = 0.125 * (p[1] + p[2]) + (1.0 / 24.0) * (above[0] + above[1] + above[2])
        own_x = 0.5 * p[2] + 0.125 * (above[0] + above[2])
        dy = lambda v: both(v, 1, 0)[:NY]
        fy, fyz = dy(f), dy(fz)
        fc, fz = f[:NY], fz[:NY]
        total = 0.5 * above[0][:NY] + dy(own_y) + along_x(own_x[:NY] + dy(own_yx))
        t24 = (1.0 / 24.0) * fyz
        t8 = 0.125 * fyz
        total = total + k[0] * (0.5 * fz + t8 + along_x(0.125 * fz + t24))
        total = total + k[1] * (0.5 * fy + t8 + along_x(0.125 * fy + t24))
        total = total + k[2] * along_x(0.5 * fc + 0.125 * (fz + fy) + t24)
        scaled = WEIGHT_TWO * inv
        s1_ref[zp] = jnp.where(inner[:NY], scaled, total)
        s2_ref[zp] = jnp.where(inner[:NY], KEEP * fc + scaled * total, 0.0)

    waiting = None
    for zp in range(NZ + 1):
        f, inv = first(zp)
        f_ref[zp] = f
        if zp > 0:
            image(zp - 1, waiting)
        waiting = inv[:NY]


def slab_terms(mine, other, left):
    rows = NY + 8
    lane = iota((rows, NX), 1)
    zp, c = lane // 4, lane % 4
    real = zp < NZ + 2
    outer = c < 2 if left else c >= 2
    offset_k = jnp.where(outer, 0, 2) if left else jnp.where(outer, 2, 0)
    k = []
    for a in range(3):
        at = jnp.where(real, a * KROWS + 2 * zp + c % 2 + offset_k, 0)
        k.append(jnp.where(real, jnp.where(outer, take(other, at), take(mine, at)), 0.0))
    near = (c == 1) | (c == 2)
    near = near & (zp < NZ + 1)
    offset_r = jnp.where(outer, RLANE - 1, RLANE) if left else jnp.where(outer, RLANE, RLANE - 1)
    at = jnp.where(near, zp + offset_r, 0)
    res = jnp.where(outer, take(other, at), take(mine, at))

    dz = [both(v, 4, 1) for v in k]
    part_0, part_y, part_x, part_yx = pair_stiffness(k, (None, None, None), dz)
    diag = SELF * (k[0] + k[1] + k[2]) + part_0 + both(part_y, 1, 0)
    diag = diag + both(part_x + both(part_yx, 1, 0), 1, 1)
    inv = 1.0 / diag
    f = jnp.where(near, WEIGHT_ONE * res * inv, 0.0)

    p = [v * f for v in k]
    d0, d1, d2 = (both(v, 4, 1) for v in p)
    own_y = 0.5 * p[1] + 0.125 * (d0 + d1)
    own_yx = 0.125 * (p[1] + p[2]) + (1.0 / 24.0) * (d0 + d1 + d2)
    own_x = 0.5 * p[2] + 0.125 * (d0 + d2)
    fz = both(f, 4, 1)
    fy, fyz = both(f, 1, 0), both(fz, 1, 0)
    t24, t8 = (1.0 / 24.0) * fyz, 0.125 * fyz
    total = 0.5 * d0 + both(own_y, 1, 0) + both(own_x + both(own_yx, 1, 0), 1, 1)
    total = total + k[0] * (0.5 * fz + t8 + both(0.125 * fz + t24, 1, 1))
    total = total + k[1] * (0.5 * fy + t8 + both(0.125 * fy + t24, 1, 1))
    total = total + k[2] * both(0.5 * f + 0.125 * (fz + fy) + t24, 1, 1)
    face = c == 2 if left else c == 1
    scaled = WEIGHT_TWO * inv
    times = jnp.where(face, scaled, total)
    plus = jnp.where(face, KEEP * f + scaled * total, 0.0)
    return times[:NY], plus[:NY]


def coarse_solve(tiles, lower, upper):
    lane = iota((8, NX), 1)
    row = iota((8, NX), 0)
    zc, xs = lane // 32, lane % 32
    pair = jnp.where(zc < 2, zc, 3 - zc)
    arrays = []
    for q in range(4):
        at_own = (q * 2 + pair) * CX + jnp.clip(xs - 4, 0, CX - 1)
        blocks = []
        for b in range(3):
            at_low = b * 32 + (q * 2 + pair) * 4 + jnp.clip(xs, 0, 3)
            at_high = b * 32 + (q * 2 + pair) * 4 + jnp.clip(xs - 20, 0, 3)
            far = jnp.where(xs < 4, take(lower, at_low), jnp.where(xs < 24, take(upper, at_high), 0.0))
            whole = jnp.where((xs >= 4) & (xs < 20), take(tiles[b], at_own), far)
            blocks.append((whole, roll(whole, 4, 0)))
        own, below, above = blocks
        first_half = jnp.where(row < 4, jnp.where(lane < 64, below[0], below[1]), jnp.where(lane < 64, own[1], own[0]))
        second_half = jnp.where(row < 4, jnp.where(lane < 64, above[0], above[1]), 0.0)
        arrays.append(jnp.concatenate([first_half, second_half], axis=0))
    kc, rhs = arrays[:3], arrays[3]
    lane = iota((16, NX), 1)

    def sides(values, axis):
        if axis == 0:
            return (
                jnp.where(lane >= 32, roll(values, 32, 1), 0.0),
                jnp.where(lane < 96, roll(values, -32, 1), 0.0),
            )
        if axis == 1:
            return roll(values, 1, 0), roll(values, -1, 0)
        return roll(values, 1, 1), roll(values, -1, 1)

    couple = [[0.5 * (kc[a] + v) for v in sides(kc[a], a)] for a in range(3)]
    diag = (MASS / 3.0) * (kc[0] + kc[1] + kc[2])
    for a in range(3):
        diag = diag + (couple[a][0] + couple[a][1])
    inside = kc[0] > 0.0
    scaled = jnp.where(inside, OMEGA / jnp.where(inside, diag, 1.0), 0.0)
    estimate = scaled * rhs
    for _ in range(CITERS - 1):
        off = None
        for a in range(3):
            low, high = sides(estimate, a)
            term = couple[a][0] * low + couple[a][1] * high
            off = term if off is None else off + term
        estimate = estimate + scaled * (rhs - (diag * estimate - off))
    return estimate[0:8]


def last_kernel(ra_ref, rb_ref, left_ref, right_ref, cor_ref, s1_ref, s2_ref, sel_ref, out_ref, est_ref):
    gx, gz = lax.axis_index("gx"), lax.axis_index("gz")
    even = gx % 2 == 0
    zero = jnp.zeros((XPAY, NX), F32)
    right = jnp.where(gx < lax.axis_size("gx") - 1, jnp.where(even, ra_ref[...], rb_ref[...]), zero)
    left = jnp.where(gx > 0, jnp.where(even, rb_ref[...], ra_ref[...]), zero)
    left_times, left_plus = slab_terms(left_ref[...], left[:40], True)
    right_times, right_plus = slab_terms(right_ref[...], right[:40], False)
    lane = iota((NY, NX), 1)
    times = jnp.where(lane % 4 < 2, right_times, left_times)
    plus = jnp.where(lane % 4 < 2, right_plus, left_plus)

    estimate = coarse_solve([cor_ref[0], cor_ref[1], cor_ref[2]], left[40:48], right[40:48])
    lane8 = iota((8, NX), 1)
    rim = (lane < 2) | (lane >= NX - 2)
    for zc in range(CZ):
        z_out = jnp.where(gz == 0, zc, CZ - 1 - zc)
        est_ref[z_out] = roll(estimate, -(zc * 32 + 4), 1)[4:8, 0:CX]
        wide = take(estimate, zc * 32 + 4 + lane8 // BLK)
        fine = jnp.concatenate([jnp.broadcast_to(wide[4 + y : 5 + y], (BLK, NX)) for y in range(CY)], axis=0)
        for i in range(BLK):
            zp = zc * BLK + i
            z = jnp.where(gz == 0, zp, NZ - 1 - zp)
            x_times = jnp.where(rim, roll(times, -(4 * zp + 2), 1), 0.0)
            x_plus = jnp.where(rim, roll(plus, -(4 * zp + 2), 1), 0.0)
            out_ref[z] = s2_ref[zp] + x_plus + s1_ref[zp] * x_times + sel_ref[zp] * fine


def near(values):
    return pltpu.with_memory_space_constraint(values, pltpu.VMEM)


def call(kernel, inputs, outputs, scratch=(), aliases=None, cost=0, name=None):
    space = pl.BlockSpec(memory_space=pltpu.VMEM)
    return pl.pallas_call(
        kernel,
        out_shape=outputs,
        in_specs=[space] * len(inputs),
        out_specs=[space] * len(outputs),
        scratch_shapes=list(scratch),
        input_output_aliases=aliases or {},
        cost_estimate=pl.CostEstimate(flops=cost, bytes_accessed=cost, transcendentals=0),
        compiler_params=pltpu.CompilerParams(vmem_limit_bytes=32 * 2**20),
        name=name,
    )(*inputs)


def vmem(*shape):
    return pltpu.VMEM(shape, F32)


def exchange(values, sizes, move):
    nx, ny, nz = sizes
    pairs = []
    for x in range(nx):
        for y in range(ny):
            for z in range(nz):
                a, b, c = move(x, y, z)
                pairs.append(((x * ny + y) * nz + z, (a * ny + b) * nz + c))
    return lax.ppermute(values, ("gx", "gy", "gz"), pairs)


def solution(mesh):
    sizes = (mesh.shape["gx"], mesh.shape["gy"], mesh.shape["gz"])
    nx, ny, nz = sizes

    def swap_z(values):
        return exchange(values, sizes, lambda x, y, z: (x, y, nz - 1 - z))

    def swap_y(values, odd):
        def move(x, y, z):
            b = y + 1 if y % 2 == odd else y - 1
            return (x, b, z) if 0 <= b < ny else (x ^ 1, y, z)

        return exchange(values, sizes, move)

    def swap_x(values, odd):
        return exchange(values, sizes, lambda x, y, z: ((x + 1 if x % 2 == odd else x - 1) % nx, y, z))

    def body(residual_in, labels, factor, basis, basis_index):
        kap, rr, sel, zpay = call(
            first_kernel,
            [residual_in, labels, factor, basis, basis_index],
            [vmem(3, NZ, NY, NX), vmem(NZ, NY, NX), vmem(NZ, NY, NX), vmem(ZPAY, NX)],
            [pltpu.VMEM((4, BLK, BLK, NX), F32), pltpu.VMEM((64, NX), F32)],
            name="stiffness",
        )
        kap, rr, sel, zpay = near(kap), near(rr), near(sel), near(zpay)
        za = near(swap_z(zpay))
        ya, yb = call(rows_kernel, [kap, rr], [vmem(YPAY, NX), vmem(YPAY, NX)], name="rows")
        ya, yb = call(
            rows_more_kernel,
            [za, zpay, near(ya), near(yb)],
            [vmem(YPAY, NX), vmem(YPAY, NX)],
            name="rows_more",
        )
        ya, yb = near(ya), near(yb)
        ra, rb = near(swap_y(ya, 0)), near(swap_y(yb, 1))
        left, right = call(columns_kernel, [kap, rr, za], [vmem(NY, NX), vmem(NY, NX)], name="columns")
        xa, xb, left, right, hal, hr, cor = call(
            columns_more_kernel,
            [ra, rb, yb, near(left), near(right)],
            [vmem(XPAY, NX), vmem(XPAY, NX), vmem(40, NX), vmem(40, NX), vmem(3, NZ + 2, 8, NX), vmem(NZ + 1, 8, NX), vmem(3, 8, NX)],
            [pltpu.VMEM((YPAY, NX), F32), pltpu.VMEM((YPAY, NX), F32)],
            name="columns_more",
        )
        xa, xb = near(xa), near(xb)
        wb, wa = near(swap_x(xb, 1)), near(swap_x(xa, 0))
        s1, s2 = call(
            interior_kernel,
            [kap, rr, za, near(hal), near(hr)],
            [vmem(NZ, NY, NX), vmem(NZ, NY, NX)],
            [pltpu.VMEM((NZ + 1, 40, NX), F32)],
            name="interior",
        )
        out, estimate = call(
            last_kernel,
            [wa, wb, near(left), near(right), near(cor), near(s1), near(s2), sel],
            [jax.ShapeDtypeStruct((NZ, NY, NX), F32), jax.ShapeDtypeStruct((CZ, CY, CX), F32)],
            name="last",
        )
        return out, estimate

    in_specs = (
        P("gz", "gy", "gx"),
        P("gz", "gy", "gx"),
        P(None, "gz", "gy", "gx"),
        P(),
        P("gz", "gy", "gx"),
    )
    out_specs = (P("gz", "gy", "gx"), P("gz", "gy", "gx"))
    return jax.shard_map(body, mesh=mesh, in_specs=in_specs, out_specs=out_specs, check_vma=False)
```

```python
import math

import jax
import jax.numpy as jnp
from jax import lax
from jax.experimental import pallas as pl
from jax.experimental.pallas import tpu as pltpu
from jax.sharding import PartitionSpec as P

BLK = 8
CITERS = 4
BRICK = (0.6, 1.0, 1.0)
MORTAR = (0.25, 0.3, 0.3)
MASS = 0.05
OMEGA = 0.8
WEIGHT_ONE = 1.0 / (1.05 - 0.95 * math.cos(math.pi / 4))
WEIGHT_TWO = 1.0 / (1.05 + 0.95 * math.cos(math.pi / 4))
SELF = 1.0 + 1.0 + 1.0 / 3.0 + MASS / 3.0
KEEP = 1.0 + WEIGHT_TWO / WEIGHT_ONE - WEIGHT_TWO

NZ, NY, NX = 16, 32, 128
CZ, CY, CX = 2, 4, 16
F32 = jnp.float32
HIGHEST = lax.Precision.HIGHEST

BULK = 7 * NY
UCOL = 40
URGENT = UCOL + NY
KROWS = 36
GROUP = NZ + 2
RROW = 3 * KROWS
YCO = 128
YPAY = YCO + 8
XPAY = 40 + 16
RLANE = 110


def iota(shape, dim):
    return lax.broadcasted_iota(jnp.int32, shape, dim)


def roll(values, shift, axis):
    size = values.shape[axis]
    shift = shift % size
    return values if shift == 0 else pltpu.roll(values, shift, axis)


def both(values, step, axis):
    return roll(values, step, axis) + roll(values, -step, axis)


def take(values, lanes):
    return jnp.take_along_axis(values, lanes, axis=1, mode="promise_in_bounds")


def pair_stiffness(own, below, above):
    k0, k1, k2 = own
    d0, d1, d2 = (a + b if a is not None else b for a, b in zip(below, above))
    part_y = 0.5 * k1 + 0.125 * (d0 + d1)
    part_yx = 0.125 * (k1 + k2) + (1.0 / 24.0) * (d0 + d1 + d2)
    part_0 = 0.5 * d0
    part_x = 0.5 * k2 + 0.125 * (d0 + d2)
    return part_0, part_y, part_x, part_yx


def first_kernel(
    r_hbm, lab_hbm, fac_hbm, bas_hbm, bix_hbm, kap_ref, rr_ref, sel_ref, urgent_ref,
    lab_ref, fac_ref, bas_ref, bix_ref, tile_ref, sum_ref, sems, more_sems
):
    gz = lax.axis_index("gz")
    halves = []
    small = [
        pltpu.make_async_copy(bas_hbm, bas_ref, sems.at[0]),
        pltpu.make_async_copy(bix_hbm, bix_ref, sems.at[1]),
    ]
    for copy in small:
        copy.start()
    for zc in range(CZ):
        planes = pl.ds(jnp.where(gz == 0, zc * BLK, (CZ - 1 - zc) * BLK), BLK)
        halves.append(
            [
                pltpu.make_async_copy(lab_hbm.at[planes], lab_ref.at[planes], more_sems.at[zc, 0]),
                pltpu.make_async_copy(fac_hbm.at[:, planes], fac_ref.at[:, planes], more_sems.at[zc, 1]),
                pltpu.make_async_copy(r_hbm.at[planes], rr_ref.at[planes], more_sems.at[zc, 2]),
            ]
        )
        for copy in halves[zc]:
            copy.start()
    sum_ref[...] = jnp.zeros(sum_ref.shape, F32)
    kap_ref[:, 0] = jnp.zeros((3, NY, NX), F32)
    for copy in small:
        copy.wait()
    tiled = lax.dot_general(
        bas_ref[...].reshape(4 * BLK * BLK, BLK),
        ((iota((BLK, NX), 1) & (BLK - 1)) == iota((BLK, NX), 0)).astype(F32),
        (((1,), (0,)), ((), ())),
        precision=HIGHEST,
        preferred_element_type=F32,
    )
    tile_ref[...] = tiled.reshape(4, BLK, BLK, NX)
    edges = [None] * 7
    spread = ((iota((CX, NX), 1) >> 3) == iota((CX, NX), 0)).astype(F32)
    for zc in range(CZ):
        index = lax.dot_general(
            bix_ref[jnp.where(gz == 0, zc, CZ - 1 - zc)].astype(F32),
            spread,
            (((1,), (0,)), ((), ())),
            precision=HIGHEST,
            preferred_element_type=F32,
        )
        index = jnp.concatenate([jnp.broadcast_to(index[y : y + 1], (BLK, NX)) for y in range(CY)], axis=0)
        for copy in halves[zc]:
            copy.wait()
        sums = [None] * 4
        for i in range(BLK):
            zp = zc * BLK + i
            z = jnp.where(gz == 0, zp, NZ - 1 - zp)
            zi = jnp.where(gz == 0, i, BLK - 1 - i)
            mortar = lab_ref[z] == 1
            b0, b1, b2, b3 = (jnp.concatenate([tile_ref[n, zi]] * CY, axis=0) for n in range(4))
            basis = jnp.where(index < 1.5, jnp.where(index < 0.5, b0, b1), jnp.where(index < 2.5, b2, b3))
            res = rr_ref[z]
            sel_ref[z] = basis
            terms = []
            for a in range(3):
                k = jnp.where(mortar, MORTAR[a], BRICK[a]) * fac_ref[a, z]
                kap_ref[a, zp + 1] = k
                terms.append(k)
                if zp >= NZ - 2:
                    plane = 2 * a + NZ - 1 - zp
                    edges[plane] = k
                    urgent_ref[plane * 4 : plane * 4 + 2] = k[0:2]
                    urgent_ref[plane * 4 + 2 : plane * 4 + 4] = k[NY - 2 : NY]
            if zp == NZ - 1:
                edges[6] = res
                urgent_ref[24:25] = res[0:1]
                urgent_ref[25:26] = res[NY - 1 : NY]
            terms.append(basis * res)
            sums = [t if s is None else s + t for s, t in zip(sums, terms)]
        for q in range(4):
            total = sums[q].reshape(CY, BLK, NX).sum(axis=1)
            sum_ref[(q * 2 + zc) * 8 : (q * 2 + zc) * 8 + CY] = total if q == 3 else total * (1.0 / BLK**3)
    bricks = lax.dot_general(
        sum_ref[...],
        ((iota((NX, NX), 0) >> 3) == (iota((NX, NX), 1) & (CX - 1))).astype(F32),
        (((1,), (0,)), ((), ())),
        precision=HIGHEST,
        preferred_element_type=F32,
    )
    group = iota((8, NX), 1) >> 4
    coarse = bricks[0:8]
    for g in range(1, 8):
        coarse = jnp.where(group == g, bricks[g * 8 : g * 8 + 8], coarse)
    urgent_ref[26:32] = jnp.zeros((6, NX), F32)
    urgent_ref[32:40] = coarse
    lane = iota((NY, NX), 1)
    columns = jnp.zeros((NY, NX), F32)
    for g, plane in enumerate(edges):
        columns = jnp.where(lane >= 4 * g, roll(plane, 4 * g + 2, 1), columns)
    urgent_ref[UCOL:URGENT] = columns


def place(zp):
    return jnp.where(lax.axis_index("gz") == 0, zp, NZ - 1 - zp)


def rows_kernel(kap_ref, rr_ref, ya_ref, yb_ref, bulk_ref):
    even = lax.axis_index("gy") % 2 == 0

    def put(at, low, high):
        ya_ref[at : at + 1] = jnp.where(even, high, low)
        yb_ref[at : at + 1] = jnp.where(even, low, high)

    for zp in range(NZ):
        for a in range(3):
            at = a * KROWS + zp
            put(at, kap_ref[a, zp + 1, 1:2], kap_ref[a, zp + 1, NY - 2 : NY - 1])
            put(at + GROUP, kap_ref[a, zp + 1, 0:1], kap_ref[a, zp + 1, NY - 1 : NY])
        put(RROW + zp, rr_ref[place(zp), 0:1], rr_ref[place(zp), NY - 1 : NY])
    for a in range(3):
        for s in range(2):
            bulk_ref[(2 * a + s) * NY : (2 * a + s + 1) * NY] = kap_ref[a, NZ - s]
    bulk_ref[6 * NY : 7 * NY] = rr_ref[place(NZ - 1)]


def rows_more_kernel(za_ref, mine_ref, ya_in, yb_in, after_ref, ya_ref, yb_ref):
    even = lax.axis_index("gy") % 2 == 0
    ya_ref[0:YCO] = ya_in[0:YCO]
    yb_ref[0:YCO] = yb_in[0:YCO]

    def put(at, low, high):
        ya_ref[at : at + low.shape[0]] = jnp.where(even, high, low)
        yb_ref[at : at + low.shape[0]] = jnp.where(even, low, high)

    for a in range(3):
        for s in range(2):
            base, at = (2 * a + s) * 4, a * KROWS + NZ + s
            put(at, za_ref[base + 1 : base + 2], za_ref[base + 2 : base + 3])
            put(at + GROUP, za_ref[base : base + 1], za_ref[base + 3 : base + 4])
    put(RROW + NZ, za_ref[24:25], za_ref[25:26])
    coarse = jnp.concatenate([mine_ref[32 : 32 + CY], za_ref[32 : 32 + CY]], axis=0)
    ya_ref[YCO : YCO + 8] = coarse
    yb_ref[YCO : YCO + 8] = coarse


def columns_kernel(kap_ref, rr_ref, urgent_ref, after_ref, left_ref, right_ref):
    lane = iota((NY, NX), 1)
    left = jnp.zeros((NY, NX), F32)
    right = jnp.zeros((NY, NX), F32)
    far = urgent_ref[UCOL:URGENT]
    for a in range(3):
        for zp in range(NZ + 2):
            at = 2 + a * KROWS + 2 * zp
            if zp < NZ:
                moved = roll(kap_ref[a, zp + 1], at, 1)
            else:
                moved = roll(far, at - 4 * (2 * a + zp - NZ) - 2, 1)
            left = jnp.where(lane >= at, moved, left)
            right = jnp.where(lane >= at - 2, moved, right)
    for zp in range(NZ + 1):
        at = RLANE + zp
        moved = roll(rr_ref[place(zp)], at, 1) if zp < NZ else roll(far, at - 26, 1)
        left = jnp.where(lane >= at, moved, left)
        right = jnp.where(lane >= at - 1, moved, right)
    left_ref[...] = left
    right_ref[...] = right


def columns_more_kernel(
    ra_ref, rb_ref, yb_ref, left_in, right_in, xa_ref, xb_ref, left_ref, right_ref, cor_ref, lo_ref, hi_ref
):
    gx, gy = lax.axis_index("gx"), lax.axis_index("gy")
    even = gy % 2 == 0
    zero = jnp.zeros((YPAY, NX), F32)
    hi = jnp.where(gy < lax.axis_size("gy") - 1, jnp.where(even, ra_ref[...], rb_ref[...]), zero)
    lo = jnp.where(gy > 0, jnp.where(even, rb_ref[...], ra_ref[...]), zero)
    hi_ref[...] = hi
    lo_ref[...] = lo

    lane, row = iota((8, NX), 1), iota((8, NX), 0)
    inner = (row == 0) | (row == 7)
    turned_hi, turned_lo = jnp.transpose(hi[:YCO]), jnp.transpose(lo[:YCO])
    part = (lane >= KROWS).astype(jnp.int32) + (lane >= 2 * KROWS).astype(jnp.int32)
    low_k = part * KROWS + ((lane - part * KROWS) >> 1)
    source = jnp.where(lane < RROW, low_k + jnp.where(inner, GROUP, 0), jnp.where(lane < YCO - 2, lane, 0))

    def column(x):
        values = jnp.where(
            row < 4,
            jnp.broadcast_to(turned_hi[x : x + 1], (8, NX)),
            jnp.broadcast_to(turned_lo[x : x + 1], (8, NX)),
        )
        return jnp.where((row < 2) | (row >= 6), take(values, source), 0.0)

    odd = (lane & 1) == 1
    more_left = jnp.where(odd & (lane < RROW), column(1), column(0))
    more_right = jnp.where(odd | (lane >= RROW), column(NX - 1), column(NX - 2))
    left_ref[0:NY] = left_in[...]
    right_ref[0:NY] = right_in[...]
    left_ref[NY : NY + 8] = roll(more_left, 2, 1)
    right_ref[NY : NY + 8] = jnp.where(lane < RROW, more_right, roll(more_right, 1, 1))
    even_x = gx % 2 == 0
    xa_ref[0:40] = jnp.where(even_x, right_ref[...], left_ref[...])
    xb_ref[0:40] = jnp.where(even_x, left_ref[...], right_ref[...])

    tiles = [lo[YCO:YPAY], yb_ref[YCO:YPAY], hi[YCO:YPAY]]
    zc, xs = lane >> 5, lane & 31
    pair = jnp.where(zc < 2, zc, 3 - zc)
    own = (xs >= 4) & (xs < 20)
    low_half, xs16 = lane < 64, iota((16, NX), 1) & 31
    sides = [jnp.zeros((16, NX), F32), jnp.zeros((16, NX), F32)]
    for q in range(4):
        at = (q * 2 + pair) * CX + jnp.clip(xs - 4, 0, CX - 1)
        below, mine, above = ((v, roll(v, 4, 0)) for v in (jnp.where(own, take(t, at), 0.0) for t in tiles))
        first = jnp.where(row < 4, jnp.where(low_half, below[0], below[1]), jnp.where(low_half, mine[1], mine[0]))
        second = jnp.where(row < 4, jnp.where(low_half, above[0], above[1]), 0.0)
        whole = jnp.concatenate([first, second], axis=0)
        cor_ref[q] = whole
        for i, start in enumerate((4, CX)):
            sides[i] = jnp.where((xs16 >= 4 * q) & (xs16 < 4 * q + 4), roll(whole, 4 * q - start, 1), sides[i])
    xa_ref[40:XPAY] = jnp.where(even_x, sides[1], sides[0])
    xb_ref[40:XPAY] = jnp.where(even_x, sides[0], sides[1])


def first_plane(to, zp, kap_ref, res, f_ref, p_ref, s1_ref, rim):
    below, k, above = ([kap_ref[a, zp + i] for a in range(3)] for i in range(3))
    part_0, part_y, part_x, part_yx = pair_stiffness(k, below, above)
    diag = SELF * (k[0] + k[1] + k[2]) + part_0 + both(part_y, 1, 0)
    inv = 1.0 / (diag + both(part_x + both(part_yx, 1, 0), 1, 1))
    f = jnp.where(rim, 0.0, WEIGHT_ONE * res * inv)
    f_ref[zp + 1] = f
    for a in range(3):
        p_ref[a, zp + 1] = k[a] * f
    if to < NZ if isinstance(to, int) else True:
        s1_ref[to] = WEIGHT_TWO * inv


def image_plane(to, zp, kap_ref, f_ref, p_ref, s1_ref, s2_ref, rim):
    k = [kap_ref[a, zp + 1] for a in range(3)]
    p = [p_ref[a, zp + 1] for a in range(3)]
    d0, d1, d2 = (p_ref[a, zp] + p_ref[a, zp + 2] for a in range(3))
    f, fz = f_ref[zp + 1], f_ref[zp] + f_ref[zp + 2]
    own_y = 0.5 * p[1] + 0.125 * (d0 + d1)
    own_yx = 0.125 * (p[1] + p[2]) + (1.0 / 24.0) * (d0 + d1 + d2)
    own_x = 0.5 * p[2] + 0.125 * (d0 + d2)
    fy, fyz = both(f, 1, 0), both(fz, 1, 0)
    t24, t8 = (1.0 / 24.0) * fyz, 0.125 * fyz
    total = 0.5 * d0 + both(own_y, 1, 0) + both(own_x + both(own_yx, 1, 0), 1, 1)
    total = total + k[0] * (0.5 * fz + t8 + both(0.125 * fz + t24, 1, 1))
    total = total + k[1] * (0.5 * fy + t8 + both(0.125 * fy + t24, 1, 1))
    total = total + k[2] * both(0.5 * f + 0.125 * (fz + fy) + t24, 1, 1)
    scaled = s1_ref[to]
    s1_ref[to] = jnp.where(rim, total, scaled)
    s2_ref[to] = jnp.where(rim, 0.0, KEEP * f + scaled * total)


def plane_rim():
    row, lane = iota((NY, NX), 0), iota((NY, NX), 1)
    return (row == 0) | (row == NY - 1) | (lane == 0) | (lane == NX - 1)


def inner_kernel(kap_ref, rr_ref, s1_ref, s2_ref, f_ref, p_ref):
    rim = plane_rim()
    f_ref[0] = jnp.zeros((NY, NX), F32)
    p_ref[:, 0] = jnp.zeros((3, NY, NX), F32)

    @pl.loop(0, 3)
    def _(i):
        for j in range(5):
            zp = i * 5 + j
            first_plane(zp, zp, kap_ref, rr_ref[place(zp)], f_ref, p_ref, s1_ref, rim)

    @pl.loop(0, 2)
    def _(i):
        for j in range(7):
            image_plane(i * 7 + j, i * 7 + j, kap_ref, f_ref, p_ref, s1_ref, s2_ref, rim)


def outer_kernel(kap_ref, rr_ref, bulk_ref, f_in, p_in, s1_in, s2_in, after_ref, s1_ref, s2_ref, k_ref, f_ref, p_ref):
    rim = plane_rim()
    for a in range(3):
        for i in range(3):
            k_ref[a, i] = kap_ref[a, NZ - 2 + i]
        for i in range(2):
            k_ref[a, 3 + i] = bulk_ref[(2 * a + i) * NY : (2 * a + i + 1) * NY]
            p_ref[a, i] = p_in[a, NZ - 2 + i]
    for i in range(2):
        f_ref[i] = f_in[NZ - 2 + i]
    first_plane(NZ - 1, 1, k_ref, rr_ref[place(NZ - 1)], f_ref, p_ref, s1_ref, rim)
    first_plane(NZ, 2, k_ref, bulk_ref[6 * NY : 7 * NY], f_ref, p_ref, s1_ref, rim)
    for i in range(2):
        image_plane(NZ - 2 + i, i, k_ref, f_ref, p_ref, s1_ref, s2_ref, rim)


def along_x(values):
    return both(values, 1, 1)


def edge_rows_kernel(ya_ref, yb_ref, lo_ref, hi_ref, s1_in, s2_in, s1_ref, s2_ref):
    even = lax.axis_index("gy") % 2 == 0
    size = 24
    row, lane = iota((size, NX), 0), iota((size, NX), 1)
    inner = (lane > 0) & (lane < NX - 1)
    near = inner & (row < NZ + 1)
    inner16 = inner[:NZ]
    for other, mine, face, second in (
        (lo_ref, jnp.where(even, yb_ref[...], ya_ref[...]), 0, 1),
        (hi_ref, jnp.where(even, ya_ref[...], yb_ref[...]), NY - 1, NY - 2),
    ):

        def group(source, at):
            return jnp.where(row < GROUP, source[at : at + size], 0.0)

        k = [[group(other, a * KROWS + s * GROUP) for a in range(3)] for s in (0, 1)]
        k += [[group(mine, a * KROWS + s * GROUP) for a in range(3)] for s in (1, 0)]
        parts = [pair_stiffness(v, (None, None, None), [both(u, 1, 0) for u in v]) for v in k]
        res = [None, other[RROW : RROW + size], mine[RROW : RROW + size]]
        f, inv = [None] * 3, [None] * 3
        for c in (1, 2):
            diag = SELF * (k[c][0] + k[c][1] + k[c][2]) + parts[c][0] + parts[c - 1][1] + parts[c + 1][1]
            inv[c] = 1.0 / (diag + along_x(parts[c][2] + parts[c - 1][3] + parts[c + 1][3]))
            f[c] = jnp.where(near, WEIGHT_ONE * res[c] * inv[c], 0.0)
        p = [None] + [[v * f[c] for v in k[c]] for c in (1, 2)]
        d = [None] + [[both(v, 1, 0) for v in p[c]] for c in (1, 2)]
        fz = [None] + [both(f[c], 1, 0) for c in (1, 2)]

        def row_parts(c):
            return (
                0.5 * p[c][1] + 0.125 * (d[c][0] + d[c][1]),
                0.125 * (p[c][1] + p[c][2]) + (1.0 / 24.0) * (d[c][0] + d[c][1] + d[c][2]),
            )

        own_y, own_yx = row_parts(1)
        own_x = 0.5 * p[2][2] + 0.125 * (d[2][0] + d[2][2])
        t24, t8 = (1.0 / 24.0) * fz[1], 0.125 * fz[1]
        total = 0.5 * d[2][0] + own_y + along_x(own_x + own_yx)
        total = total + k[2][0] * (0.5 * fz[2] + t8 + along_x(0.125 * fz[2] + t24))
        total = total + k[2][1] * (0.5 * f[1] + t8 + along_x(0.125 * f[1] + t24))
        total = total + k[2][2] * along_x(0.5 * f[2] + 0.125 * (fz[2] + f[1]) + t24)
        total = total[:NZ] + s1_ref[:, face, :]
        scaled = WEIGHT_TWO * inv[2][:NZ]
        s1_ref[:, face, :] = jnp.where(inner16, scaled, total)
        s2_ref[:, face, :] = jnp.where(inner16, KEEP * f[2][:NZ] + scaled * total, 0.0)

        own_y, own_yx = row_parts(2)
        t24, t8 = (1.0 / 24.0) * fz[2], 0.125 * fz[2]
        total = own_y + along_x(own_yx) + k[3][0] * (t8 + along_x(t24))
        total = total + k[3][1] * (0.5 * f[2] + t8 + along_x(0.125 * f[2] + t24))
        total = (total + k[3][2] * along_x(0.125 * f[2] + t24))[:NZ]
        scaled = s1_ref[:, second, :]
        s1_ref[:, second, :] = jnp.where(inner16, scaled, scaled + total)
        s2_ref[:, second, :] = s2_ref[:, second, :] + jnp.where(inner16, scaled * total, 0.0)


def slab_terms(mine, other, left):
    rows = NY + 8
    lane = iota((8, NX), 1)
    zp, c = lane >> 2, lane & 3
    real = zp < NZ + 2
    outer = c < 2 if left else c >= 2
    offset = jnp.where(outer, 0, 2) if left else jnp.where(outer, 2, 0)
    near = ((c == 1) | (c == 2)) & (zp < NZ + 1)
    offset_r = jnp.where(outer, RLANE - 1, RLANE) if left else jnp.where(outer, RLANE, RLANE - 1)
    at_r = jnp.where(near, zp + offset_r, 0)
    at_k = [jnp.where(real, a * KROWS + 2 * zp + (c & 1) + offset, 0) for a in range(3)]

    def spread(at, keep):
        pieces = []
        for i in range(0, rows, 8):
            piece = jnp.where(outer, take(other[i : i + 8], at), take(mine[i : i + 8], at))
            pieces.append(jnp.where(keep, piece, 0.0))
        return jnp.concatenate(pieces, axis=0)

    k = [spread(at, real) for at in at_k]
    res = spread(at_r, near)
    near = jnp.concatenate([near] * (rows // 8), axis=0)
    face = c == 2 if left else c == 1
    face = jnp.concatenate([face] * (rows // 8), axis=0)

    dz = [both(v, 4, 1) for v in k]
    part_0, part_y, part_x, part_yx = pair_stiffness(k, (None, None, None), dz)
    diag = SELF * (k[0] + k[1] + k[2]) + part_0 + both(part_y, 1, 0)
    diag = diag + both(part_x + both(part_yx, 1, 0), 1, 1)
    inv = 1.0 / diag
    f = jnp.where(near, WEIGHT_ONE * res * inv, 0.0)

    p = [v * f for v in k]
    d0, d1, d2 = (both(v, 4, 1) for v in p)
    own_y = 0.5 * p[1] + 0.125 * (d0 + d1)
    own_yx = 0.125 * (p[1] + p[2]) + (1.0 / 24.0) * (d0 + d1 + d2)
    own_x = 0.5 * p[2] + 0.125 * (d0 + d2)
    fz = both(f, 4, 1)
    fy, fyz = both(f, 1, 0), both(fz, 1, 0)
    t24, t8 = (1.0 / 24.0) * fyz, 0.125 * fyz
    total = 0.5 * d0 + both(own_y, 1, 0) + both(own_x + both(own_yx, 1, 0), 1, 1)
    total = total + k[0] * (0.5 * fz + t8 + both(0.125 * fz + t24, 1, 1))
    total = total + k[1] * (0.5 * fy + t8 + both(0.125 * fy + t24, 1, 1))
    total = total + k[2] * both(0.5 * f + 0.125 * (fz + fy) + t24, 1, 1)
    scaled = WEIGHT_TWO * inv
    times = jnp.where(face, scaled, total)
    plus = jnp.where(face, KEEP * f + scaled * total, 0.0)
    return times[:NY], plus[:NY]


def coarse_solve(cor_ref, lower, upper):
    xs = iota((16, NX), 1) & 31
    arrays = []
    for q in range(4):
        whole = jnp.where(xs < 4, roll(lower, -4 * q, 1), cor_ref[q])
        arrays.append(jnp.where((xs >= 20) & (xs < 24), roll(upper, 20 - 4 * q, 1), whole))
    kc, rhs = arrays[:3], arrays[3]
    lane = iota((16, NX), 1)

    def sides(values, axis):
        if axis == 0:
            return (
                jnp.where(lane >= 32, roll(values, 32, 1), 0.0),
                jnp.where(lane < 96, roll(values, -32, 1), 0.0),
            )
        if axis == 1:
            return roll(values, 1, 0), roll(values, -1, 0)
        return roll(values, 1, 1), roll(values, -1, 1)

    couple = [[0.5 * (kc[a] + v) for v in sides(kc[a], a)] for a in range(3)]
    diag = (MASS / 3.0) * (kc[0] + kc[1] + kc[2])
    for a in range(3):
        diag = diag + (couple[a][0] + couple[a][1])
    inside = kc[0] > 0.0
    scaled = jnp.where(inside, OMEGA / jnp.where(inside, diag, 1.0), 0.0)
    estimate = scaled * rhs
    for _ in range(CITERS - 1):
        off = None
        for a in range(3):
            low, high = sides(estimate, a)
            term = couple[a][0] * low + couple[a][1] * high
            off = term if off is None else off + term
        estimate = estimate + scaled * (rhs - (diag * estimate - off))
    return estimate[0:8]


def last_kernel(
    ra_ref, rb_ref, left_ref, right_ref, cor_ref, s1_ref, s2_ref, sel_ref, out_hbm, est_ref, out_ref, sems
):
    gx, gz = lax.axis_index("gx"), lax.axis_index("gz")
    even = gx % 2 == 0
    zero = jnp.zeros((XPAY, NX), F32)
    right = jnp.where(gx < lax.axis_size("gx") - 1, jnp.where(even, ra_ref[...], rb_ref[...]), zero)
    left = jnp.where(gx > 0, jnp.where(even, rb_ref[...], ra_ref[...]), zero)
    left_times, left_plus = slab_terms(left_ref[...], left[:40], True)
    right_times, right_plus = slab_terms(right_ref[...], right[:40], False)
    lane = iota((NY, NX), 1)
    low_side = (lane & 3) < 2
    times = jnp.where(low_side, right_times, left_times)
    plus = jnp.where(low_side, right_plus, left_plus)

    estimate = coarse_solve(cor_ref, left[40:XPAY], right[40:XPAY])
    lane8 = iota((8, NX), 1)
    rim = (lane < 2) | (lane >= NX - 2)
    copies = []
    step = 4
    for zc in range(CZ):
        z_out = jnp.where(gz == 0, zc, CZ - 1 - zc)
        est_ref[z_out] = roll(estimate, -(zc * 32 + 4), 1)[4:8, 0:CX]
        wide = take(estimate, zc * 32 + 4 + (lane8 >> 3))
        fine = jnp.concatenate([jnp.broadcast_to(wide[4 + y : 5 + y], (BLK, NX)) for y in range(CY)], axis=0)
        for i in range(BLK):
            zp = zc * BLK + i
            z = jnp.where(gz == 0, zp, NZ - 1 - zp)
            x_times = jnp.where(rim, roll(times, -(4 * zp + 2), 1), 0.0)
            x_plus = jnp.where(rim, roll(plus, -(4 * zp + 2), 1), 0.0)
            out_ref[z] = s2_ref[zp] + x_plus + s1_ref[zp] * x_times + sel_ref[z] * fine
            if zp % step == step - 1:
                planes = pl.ds(jnp.where(gz == 0, zp + 1 - step, NZ - 1 - zp), step)
                copies.append(pltpu.make_async_copy(out_ref.at[planes], out_hbm.at[planes], sems.at[zp // step]))
                copies[-1].start()
    for copy in copies:
        copy.wait()


def near(values):
    return pltpu.with_memory_space_constraint(values, pltpu.VMEM)


def call(kernel, inputs, outputs, scratch=(), aliases=None, us=0.1, name=None, in_space=pltpu.VMEM, out_spaces=None):
    return pl.pallas_call(
        kernel,
        out_shape=outputs,
        in_specs=[pl.BlockSpec(memory_space=in_space)] * len(inputs),
        out_specs=[pl.BlockSpec(memory_space=v) for v in out_spaces or [pltpu.VMEM] * len(outputs)],
        scratch_shapes=list(scratch),
        input_output_aliases=aliases or {},
        cost_estimate=pl.CostEstimate(flops=0, bytes_accessed=int(us * 3.6e6), transcendentals=0),
        compiler_params=pltpu.CompilerParams(vmem_limit_bytes=32 * 2**20),
        name=name,
    )(*inputs)


def vmem(*shape):
    return pltpu.VMEM(shape, F32)


def exchange(values, sizes, move):
    nx, ny, nz = sizes
    pairs = []
    for x in range(nx):
        for y in range(ny):
            for z in range(nz):
                a, b, c = move(x, y, z)
                pairs.append(((x * ny + y) * nz + z, (a * ny + b) * nz + c))
    return lax.ppermute(values, ("gx", "gy", "gz"), pairs)


def solution(mesh):
    sizes = (mesh.shape["gx"], mesh.shape["gy"], mesh.shape["gz"])
    nx, ny, nz = sizes

    def swap_z(values):
        return exchange(values, sizes, lambda x, y, z: (x, y, nz - 1 - z))

    def swap_y(values, odd):
        def move(x, y, z):
            b = y + 1 if y % 2 == odd else y - 1
            return (x, b, z) if 0 <= b < ny else (x ^ 1, y, z)

        return exchange(values, sizes, move)

    def swap_x(values, odd):
        return exchange(values, sizes, lambda x, y, z: ((x + 1 if x % 2 == odd else x - 1) % nx, y, z))

    def body(residual_in, labels, factor, basis, basis_index):
        inputs = [residual_in, labels, factor, basis, basis_index]
        kap, rr, sel, urgent = call(
            first_kernel,
            [pltpu.with_memory_space_constraint(v, pltpu.HBM) for v in inputs],
            [vmem(3, NZ + 1, NY, NX), vmem(NZ, NY, NX), vmem(NZ, NY, NX), vmem(URGENT, NX)],
            [
                pltpu.VMEM(labels.shape, jnp.int32),
                pltpu.VMEM(factor.shape, F32),
                pltpu.VMEM(basis.shape, F32),
                pltpu.VMEM(basis_index.shape, jnp.int32),
                pltpu.VMEM((4, BLK, BLK, NX), F32),
                pltpu.VMEM((64, NX), F32),
                pltpu.SemaphoreType.DMA((2,)),
                pltpu.SemaphoreType.DMA((CZ, 3)),
            ],
            us=1.8,
            name="stiffness",
            in_space=pltpu.HBM,
        )
        kap, rr, sel, urgent = near(kap), near(rr), near(sel), near(urgent)
        zu = near(swap_z(urgent))
        ya, yb, bulk = call(rows_kernel, [kap, rr], [vmem(YPAY, NX), vmem(YPAY, NX), vmem(BULK, NX)], name="rows")
        za = near(swap_z(near(bulk)))
        s1, s2, f, p = call(
            inner_kernel,
            [kap, rr],
            [vmem(NZ, NY, NX), vmem(NZ, NY, NX), vmem(NZ, NY, NX), vmem(3, NZ, NY, NX)],
            us=1.1,
            name="inner",
        )
        ya, yb = call(
            rows_more_kernel,
            [zu, urgent, near(ya), near(yb), near(s1)],
            [vmem(YPAY, NX), vmem(YPAY, NX)],
            name="rows_more",
        )
        ya, yb = near(ya), near(yb)
        ra, rb = near(swap_y(ya, 0)), near(swap_y(yb, 1))
        left, right = call(columns_kernel, [kap, rr, zu, ya], [vmem(NY, NX), vmem(NY, NX)], us=0.0, name="columns")
        xa, xb, left, right, cor, lo, hi = call(
            columns_more_kernel,
            [ra, rb, yb, near(left), near(right)],
            [vmem(XPAY, NX), vmem(XPAY, NX), vmem(40, NX), vmem(40, NX), vmem(4, 16, NX), vmem(YPAY, NX), vmem(YPAY, NX)],
            us=0.25,
            name="columns_more",
        )
        xa, xb = near(xa), near(xb)
        wb, wa = near(swap_x(xb, 1)), near(swap_x(xa, 0))
        s1, s2 = call(
            outer_kernel,
            [kap, rr, za, near(f), near(p), near(s1), near(s2), near(lo)],
            [vmem(NZ, NY, NX), vmem(NZ, NY, NX)],
            [pltpu.VMEM((3, 5, NY, NX), F32), pltpu.VMEM((4, NY, NX), F32), pltpu.VMEM((3, 4, NY, NX), F32)],
            aliases={5: 0, 6: 1},
            us=0.25,
            name="outer",
        )
        s1, s2 = call(
            edge_rows_kernel,
            [ya, yb, near(lo), near(hi), near(s1), near(s2)],
            [vmem(NZ, NY, NX), vmem(NZ, NY, NX)],
            aliases={4: 0, 5: 1},
            us=0.4,
            name="edge_rows",
        )
        out, estimate = call(
            last_kernel,
            [wa, wb, near(left), near(right), near(cor), near(s1), near(s2), sel],
            [jax.ShapeDtypeStruct((NZ, NY, NX), F32), jax.ShapeDtypeStruct((CZ, CY, CX), F32)],
            [pltpu.VMEM((NZ, NY, NX), F32), pltpu.SemaphoreType.DMA((4,))],
            us=2.0,
            name="last",
            out_spaces=[pltpu.HBM, pltpu.VMEM],
        )
        return out, estimate

    in_specs = (
        P("gz", "gy", "gx"),
        P("gz", "gy", "gx"),
        P(None, "gz", "gy", "gx"),
        P(),
        P("gz", "gy", "gx"),
    )
    out_specs = (P("gz", "gy", "gx"), P("gz", "gy", "gx"))
    return jax.shard_map(body, mesh=mesh, in_specs=in_specs, out_specs=out_specs, check_vma=False)
```

```python
import math

import jax
import jax.numpy as jnp
from jax import lax
from jax.experimental import pallas as pl
from jax.experimental.pallas import tpu as pltpu
from jax.sharding import PartitionSpec as P

BLK = 8
CITERS = 4
BRICK = (0.6, 1.0, 1.0)
MORTAR = (0.25, 0.3, 0.3)
MASS = 0.05
OMEGA = 0.8
WEIGHT_ONE = 1.0 / (1.05 - 0.95 * math.cos(math.pi / 4))
WEIGHT_TWO = 1.0 / (1.05 + 0.95 * math.cos(math.pi / 4))
SELF = 1.0 + 1.0 + 1.0 / 3.0 + MASS / 3.0
KEEP = 1.0 + WEIGHT_TWO / WEIGHT_ONE - WEIGHT_TWO

NZ, NY, NX = 16, 32, 128
CZ, CY, CX = 2, 4, 16
PARTS = range(2)
F32 = jnp.float32
HIGHEST = lax.Precision.HIGHEST

BULK = 7 * NY
URGENT = 16
ZURGENT = 48
ZROW = 16
KROWS = 36
GROUP = NZ + 2
RROW = 3 * KROWS
YPAY = 128
XPAY = 40 + 16
RLANE = 110


def iota(shape, dim):
    return lax.broadcasted_iota(jnp.int32, shape, dim)


def roll(values, shift, axis):
    size = values.shape[axis]
    shift = shift % size
    return values if shift == 0 else pltpu.roll(values, shift, axis)


def both(values, step, axis):
    return roll(values, step, axis) + roll(values, -step, axis)


def take(values, lanes):
    return jnp.take_along_axis(values, lanes, axis=1, mode="promise_in_bounds")


def pair_stiffness(own, below, above):
    k0, k1, k2 = own
    d0, d1, d2 = (a + b if a is not None else b for a, b in zip(below, above))
    part_y = 0.5 * k1 + 0.125 * (d0 + d1)
    part_yx = 0.125 * (k1 + k2) + (1.0 / 24.0) * (d0 + d1 + d2)
    part_0 = 0.5 * d0
    part_x = 0.5 * k2 + 0.125 * (d0 + d2)
    return part_0, part_y, part_x, part_yx


def first_kernel(
    r_hbm, lab_hbm, fac_hbm, bas_hbm, bix_hbm, kap_ref, rr_ref, sel_ref, urgent_ref,
    lab_ref, fac_ref, bas_ref, bix_ref, tile_ref, sum_ref, sems, more_sems
):
    gz = lax.axis_index("gz")
    parts = []
    small = [
        pltpu.make_async_copy(bas_hbm, bas_ref, sems.at[0]),
        pltpu.make_async_copy(bix_hbm, bix_ref, sems.at[1]),
    ]
    for copy in small:
        copy.start()
    step = NZ // len(PARTS)
    for part in PARTS:
        planes = pl.ds(jnp.where(gz == 0, part * step, NZ - step - part * step), step)
        parts.append(
            [
                pltpu.make_async_copy(lab_hbm.at[planes], lab_ref.at[planes], more_sems.at[part, 0]),
                pltpu.make_async_copy(fac_hbm.at[:, planes], fac_ref.at[:, planes], more_sems.at[part, 1]),
                pltpu.make_async_copy(r_hbm.at[planes], rr_ref.at[planes], more_sems.at[part, 2]),
            ]
        )
        for copy in parts[part]:
            copy.start()
    sum_ref[...] = jnp.zeros(sum_ref.shape, F32)
    kap_ref[:, 0] = jnp.zeros((3, NY, NX), F32)
    for copy in small:
        copy.wait()
    tiled = lax.dot_general(
        bas_ref[...].reshape(4 * BLK * BLK, BLK),
        ((iota((BLK, NX), 1) & (BLK - 1)) == iota((BLK, NX), 0)).astype(F32),
        (((1,), (0,)), ((), ())),
        precision=HIGHEST,
        preferred_element_type=F32,
    )
    tile_ref[...] = tiled.reshape(4, BLK, BLK, NX)
    edges = [None] * 7
    spread = ((iota((CX, NX), 1) >> 3) == iota((CX, NX), 0)).astype(F32)
    for zc in range(CZ):
        index = lax.dot_general(
            bix_ref[jnp.where(gz == 0, zc, CZ - 1 - zc)].astype(F32),
            spread,
            (((1,), (0,)), ((), ())),
            precision=HIGHEST,
            preferred_element_type=F32,
        )
        index = jnp.concatenate([jnp.broadcast_to(index[y : y + 1], (BLK, NX)) for y in range(CY)], axis=0)
        sums = [None] * 4
        for i in range(BLK):
            zp = zc * BLK + i
            if zp % step == 0:
                for copy in parts[zp // step]:
                    copy.wait()
            z = jnp.where(gz == 0, zp, NZ - 1 - zp)
            zi = jnp.where(gz == 0, i, BLK - 1 - i)
            mortar = lab_ref[z] == 1
            b0, b1, b2, b3 = (jnp.concatenate([tile_ref[n, zi]] * CY, axis=0) for n in range(4))
            basis = jnp.where(index < 1.5, jnp.where(index < 0.5, b0, b1), jnp.where(index < 2.5, b2, b3))
            res = rr_ref[z]
            sel_ref[z] = basis
            terms = []
            for a in range(3):
                k = jnp.where(mortar, MORTAR[a], BRICK[a]) * fac_ref[a, z]
                kap_ref[a, zp + 1] = k
                terms.append(k)
                if zp >= NZ - 2:
                    plane = 2 * a + NZ - 1 - zp
                    edges[plane] = k
            if zp == NZ - 1:
                edges[6] = res
            terms.append(basis * res)
            sums = [t if s is None else s + t for s, t in zip(sums, terms)]
        for q in range(4):
            total = sums[q].reshape(CY, BLK, NX).sum(axis=1)
            sum_ref[(q * 2 + zc) * 8 : (q * 2 + zc) * 8 + CY] = total if q == 3 else total * (1.0 / BLK**3)
    bricks = lax.dot_general(
        sum_ref[...],
        ((iota((NX, NX), 0) >> 3) == (iota((NX, NX), 1) & (CX - 1))).astype(F32),
        (((1,), (0,)), ((), ())),
        precision=HIGHEST,
        preferred_element_type=F32,
    )
    group = iota((8, NX), 1) >> 4
    coarse = bricks[0:8]
    for g in range(1, 8):
        coarse = jnp.where(group == g, bricks[g * 8 : g * 8 + 8], coarse)
    urgent_ref[0:8] = coarse
    lane = iota((NY, NX), 1)
    columns = jnp.zeros((NY, NX), F32)
    for g, plane in enumerate(edges):
        columns = jnp.where(lane >= 4 * g, roll(plane, 4 * g + 2, 1), columns)
    lane = iota((8, NX), 1)
    folded = columns[:8]
    for i in range(1, NY // 8):
        folded = jnp.where(lane >= 32 * i, roll(columns[8 * i : 8 * i + 8], 32 * i, 1), folded)
    urgent_ref[8:16] = folded
    for g, plane in enumerate(edges[:6]):
        urgent_ref[ZROW + 4 * g : ZROW + 4 * g + 2] = plane[0:2]
        urgent_ref[ZROW + 4 * g + 2 : ZROW + 4 * g + 4] = plane[NY - 2 : NY]
    urgent_ref[ZROW + 24 : ZROW + 25] = edges[6][0:1]
    urgent_ref[ZROW + 25 : ZROW + 26] = edges[6][NY - 1 : NY]
    urgent_ref[ZROW + 26 : ZURGENT] = jnp.zeros((6, NX), F32)


def place(zp):
    return jnp.where(lax.axis_index("gz") == 0, zp, NZ - 1 - zp)


def rows_kernel(kap_ref, rr_ref, ya_ref, yb_ref, bulk_ref):
    even = lax.axis_index("gy") % 2 == 0

    def put(at, low, high):
        ya_ref[at : at + 1] = jnp.where(even, high, low)
        yb_ref[at : at + 1] = jnp.where(even, low, high)

    for zp in range(NZ):
        for a in range(3):
            at = a * KROWS + zp
            put(at, kap_ref[a, zp + 1, 1:2], kap_ref[a, zp + 1, NY - 2 : NY - 1])
            put(at + GROUP, kap_ref[a, zp + 1, 0:1], kap_ref[a, zp + 1, NY - 1 : NY])
        put(RROW + zp, rr_ref[place(zp), 0:1], rr_ref[place(zp), NY - 1 : NY])
    for a in range(3):
        for s in range(2):
            bulk_ref[(2 * a + s) * NY : (2 * a + s + 1) * NY] = kap_ref[a, NZ - s]
    bulk_ref[6 * NY : 7 * NY] = rr_ref[place(NZ - 1)]


def columns_kernel(kap_ref, rr_ref, left_ref, right_ref):
    lane = iota((NY, NX), 1)
    left = jnp.zeros((NY, NX), F32)
    right = jnp.zeros((NY, NX), F32)
    for a in range(3):
        for zp in range(NZ):
            at = 2 + a * KROWS + 2 * zp
            moved = roll(kap_ref[a, zp + 1], at, 1)
            left = jnp.where(lane >= at, moved, left)
            right = jnp.where(lane >= at - 2, moved, right)
    for zp in range(NZ):
        at = RLANE + zp
        moved = roll(rr_ref[place(zp)], at, 1)
        left = jnp.where(lane >= at, moved, left)
        right = jnp.where(lane >= at - 1, moved, right)
    left_ref[...] = left
    right_ref[...] = right


def columns_beyond(left, right, moved):
    lane = iota(left.shape, 1)
    for a in range(3):
        for s in range(2):
            at = 2 + a * KROWS + 2 * (NZ + s)
            values = moved(2 * a + s, at)
            left = jnp.where((lane == at) | (lane == at + 1), values, left)
            right = jnp.where((lane == at - 2) | (lane == at - 1), values, right)
    at = RLANE + NZ
    values = moved(6, at)
    return jnp.where(lane == at, values, left), jnp.where(lane == at - 1, values, right)


def columns_beyond_kernel(left_in, right_in, far_ref, left_ref, right_ref):
    folded = far_ref[8:16]
    columns = jnp.concatenate([roll(folded, -32 * i, 1) for i in range(NY // 8)], axis=0)
    left_ref[...], right_ref[...] = columns_beyond(
        left_in[...], right_in[...], lambda g, x0: roll(columns, x0 - 4 * g - 2, 1)
    )


def send_rows_kernel(far_ref, mine_ref, left_ref, right_ref, ya_in, yb_in, after_ref, ya_ref, yb_ref, ub_ref):
    even = lax.axis_index("gy") % 2 == 0

    def put(at, low, high):
        ya_ref[at : at + 1] = jnp.where(even, high, low)
        yb_ref[at : at + 1] = jnp.where(even, low, high)

    for a in range(3):
        for s in range(2):
            base, at = ZROW + (2 * a + s) * 4, a * KROWS + NZ + s
            put(at, far_ref[base + 1 : base + 2], far_ref[base + 2 : base + 3])
            put(at + GROUP, far_ref[base : base + 1], far_ref[base + 3 : base + 4])
    put(RROW + NZ, far_ref[ZROW + 24 : ZROW + 25], far_ref[ZROW + 25 : ZROW + 26])
    row = iota((8, NX), 0)
    folded = far_ref[8:16]
    corners = jnp.where(row < 2, folded, roll(roll(folded, -96, 1), 4, 0))

    def ends(ref):
        return jnp.where(row < 2, ref[0:8], roll(ref[NY - 8 : NY], 4, 0))

    left, right = columns_beyond(ends(left_ref), ends(right_ref), lambda g, x0: roll(corners, x0 - 4 * g - 2, 1))
    low = jnp.where(row < 2, left, roll(right, 2, 0))
    high = jnp.where(row < 2, roll(left, -2, 0), right)
    ya_ref[YPAY + 8 :] = jnp.where(even, high, low)
    ub_ref[8:16] = jnp.where(even, low, high)
    coarse = jnp.concatenate([mine_ref[0:CY], far_ref[0:CY]], axis=0)
    ya_ref[YPAY : YPAY + 8] = coarse
    ub_ref[0:8] = coarse


def columns_more_kernel(ra_ref, rb_ref, mine_ref, left_in, right_in, xa_ref, xb_ref, left_ref, right_ref, cor_ref):
    gx, gy = lax.axis_index("gx"), lax.axis_index("gy")
    even = gy % 2 == 0
    zero = jnp.zeros((URGENT, NX), F32)
    ra = ra_ref[YPAY:]
    hi = jnp.where(gy < lax.axis_size("gy") - 1, jnp.where(even, ra, rb_ref[...]), zero)
    lo = jnp.where(gy > 0, jnp.where(even, rb_ref[...], ra), zero)
    lane, row = iota((8, NX), 1), iota((8, NX), 0)

    def halo(shift):
        above, below = roll(hi[8:16], -shift, 0), roll(lo[8:16], 6 - shift, 0)
        return jnp.where(row < 2, above, jnp.where(row >= 6, below, 0.0))

    left_ref[0:NY] = left_in[...]
    right_ref[0:NY] = right_in[...]
    left_ref[NY : NY + 8] = halo(0)
    right_ref[NY : NY + 8] = halo(2)
    even_x = gx % 2 == 0
    xa_ref[0:40] = jnp.where(even_x, right_ref[...], left_ref[...])
    xb_ref[0:40] = jnp.where(even_x, left_ref[...], right_ref[...])

    tiles = [lo[0:8], mine_ref[0:8], hi[0:8]]
    zc, xs = lane >> 5, lane & 31
    pair = jnp.where(zc < 2, zc, 3 - zc)
    own = (xs >= 4) & (xs < 20)
    low_half, xs16 = lane < 64, iota((16, NX), 1) & 31
    sides = [jnp.zeros((16, NX), F32), jnp.zeros((16, NX), F32)]
    for q in range(4):
        at = (q * 2 + pair) * CX + jnp.clip(xs - 4, 0, CX - 1)
        below, mine, above = ((v, roll(v, 4, 0)) for v in (jnp.where(own, take(t, at), 0.0) for t in tiles))
        first = jnp.where(row < 4, jnp.where(low_half, below[0], below[1]), jnp.where(low_half, mine[1], mine[0]))
        second = jnp.where(row < 4, jnp.where(low_half, above[0], above[1]), 0.0)
        whole = jnp.concatenate([first, second], axis=0)
        cor_ref[q] = whole
        for i, start in enumerate((4, CX)):
            sides[i] = jnp.where((xs16 >= 4 * q) & (xs16 < 4 * q + 4), roll(whole, 4 * q - start, 1), sides[i])
    xa_ref[40:XPAY] = jnp.where(even_x, sides[1], sides[0])
    xb_ref[40:XPAY] = jnp.where(even_x, sides[0], sides[1])


def first_plane(to, zp, kap_ref, res, f_ref, p_ref, s1_ref, rim):
    below, k, above = ([kap_ref[a, zp + i] for a in range(3)] for i in range(3))
    part_0, part_y, part_x, part_yx = pair_stiffness(k, below, above)
    diag = SELF * (k[0] + k[1] + k[2]) + part_0 + both(part_y, 1, 0)
    inv = 1.0 / (diag + both(part_x + both(part_yx, 1, 0), 1, 1))
    f = jnp.where(rim, 0.0, WEIGHT_ONE * res * inv)
    f_ref[zp + 1] = f
    for a in range(3):
        p_ref[a, zp + 1] = k[a] * f
    if to < NZ if isinstance(to, int) else True:
        s1_ref[to] = WEIGHT_TWO * inv


def image_plane(to, zp, kap_ref, f_ref, p_ref, s1_ref, s2_ref, rim):
    k = [kap_ref[a, zp + 1] for a in range(3)]
    p = [p_ref[a, zp + 1] for a in range(3)]
    d0, d1, d2 = (p_ref[a, zp] + p_ref[a, zp + 2] for a in range(3))
    f, fz = f_ref[zp + 1], f_ref[zp] + f_ref[zp + 2]
    own_y = 0.5 * p[1] + 0.125 * (d0 + d1)
    own_yx = 0.125 * (p[1] + p[2]) + (1.0 / 24.0) * (d0 + d1 + d2)
    own_x = 0.5 * p[2] + 0.125 * (d0 + d2)
    fy, fyz = both(f, 1, 0), both(fz, 1, 0)
    t24, t8 = (1.0 / 24.0) * fyz, 0.125 * fyz
    total = 0.5 * d0 + both(own_y, 1, 0) + both(own_x + both(own_yx, 1, 0), 1, 1)
    total = total + k[0] * (0.5 * fz + t8 + both(0.125 * fz + t24, 1, 1))
    total = total + k[1] * (0.5 * fy + t8 + both(0.125 * fy + t24, 1, 1))
    total = total + k[2] * both(0.5 * f + 0.125 * (fz + fy) + t24, 1, 1)
    scaled = s1_ref[to]
    s1_ref[to] = jnp.where(rim, total, scaled)
    s2_ref[to] = jnp.where(rim, 0.0, KEEP * f + scaled * total)


def plane_rim():
    row, lane = iota((NY, NX), 0), iota((NY, NX), 1)
    return (row == 0) | (row == NY - 1) | (lane == 0) | (lane == NX - 1)


def inner_first_kernel(kap_ref, rr_ref, s1_ref, f_ref, p_ref):
    rim = plane_rim()
    f_ref[0] = jnp.zeros((NY, NX), F32)
    p_ref[:, 0] = jnp.zeros((3, NY, NX), F32)

    @pl.loop(0, 3)
    def _(i):
        for j in range(5):
            zp = i * 5 + j
            first_plane(zp, zp, kap_ref, rr_ref[place(zp)], f_ref, p_ref, s1_ref, rim)


def inner_image_kernel(kap_ref, f_ref, p_ref, s1_in, after_ref, s1_ref, s2_ref):
    rim = plane_rim()

    @pl.loop(0, 2)
    def _(i):
        for j in range(7):
            image_plane(i * 7 + j, i * 7 + j, kap_ref, f_ref, p_ref, s1_ref, s2_ref, rim)


def outer_kernel(kap_ref, rr_ref, bulk_ref, f_in, p_in, s1_in, s2_in, s1_ref, s2_ref, k_ref, f_ref, p_ref):
    rim = plane_rim()
    for a in range(3):
        for i in range(3):
            k_ref[a, i] = kap_ref[a, NZ - 2 + i]
        for i in range(2):
            k_ref[a, 3 + i] = bulk_ref[(2 * a + i) * NY : (2 * a + i + 1) * NY]
            p_ref[a, i] = p_in[a, NZ - 2 + i]
    for i in range(2):
        f_ref[i] = f_in[NZ - 2 + i]
    first_plane(NZ - 1, 1, k_ref, rr_ref[place(NZ - 1)], f_ref, p_ref, s1_ref, rim)
    first_plane(NZ, 2, k_ref, bulk_ref[6 * NY : 7 * NY], f_ref, p_ref, s1_ref, rim)
    for i in range(2):
        image_plane(NZ - 2 + i, i, k_ref, f_ref, p_ref, s1_ref, s2_ref, rim)


def along_x(values):
    return both(values, 1, 1)


def edge_rows_kernel(ya_ref, yb_ref, ra_ref, rb_ref, s1_in, s2_in, s1_ref, s2_ref):
    even = lax.axis_index("gy") % 2 == 0
    size = 24
    row, lane = iota((size, NX), 0), iota((size, NX), 1)
    inner = (lane > 0) & (lane < NX - 1)
    near = inner & (row < NZ + 1)
    inner16 = inner[:NZ]
    gy = lax.axis_index("gy")
    zero = jnp.zeros((YPAY, NX), F32)
    ya, yb, ra, rb = ya_ref[0:YPAY], yb_ref[...], ra_ref[0:YPAY], rb_ref[...]
    hi = jnp.where(gy < lax.axis_size("gy") - 1, jnp.where(even, ra, rb), zero)
    lo = jnp.where(gy > 0, jnp.where(even, rb, ra), zero)
    for other, mine, face, second in (
        (lo, jnp.where(even, yb, ya), 0, 1),
        (hi, jnp.where(even, ya, yb), NY - 1, NY - 2),
    ):

        def group(source, at):
            return jnp.where(row < GROUP, source[at : at + size], 0.0)

        k = [[group(other, a * KROWS + s * GROUP) for a in range(3)] for s in (0, 1)]
        k += [[group(mine, a * KROWS + s * GROUP) for a in range(3)] for s in (1, 0)]
        parts = [pair_stiffness(v, (None, None, None), [both(u, 1, 0) for u in v]) for v in k]
        res = [None] + [jnp.where(row < NZ + 1, v[YPAY - size :], 0.0) for v in (roll(other, 4 - 8, 0), roll(mine, 4 - 8, 0))]
        f, inv = [None] * 3, [None] * 3
        for c in (1, 2):
            diag = SELF * (k[c][0] + k[c][1] + k[c][2]) + parts[c][0] + parts[c - 1][1] + parts[c + 1][1]
            inv[c] = 1.0 / (diag + along_x(parts[c][2] + parts[c - 1][3] + parts[c + 1][3]))
            f[c] = jnp.where(near, WEIGHT_ONE * res[c] * inv[c], 0.0)
        p = [None] + [[v * f[c] for v in k[c]] for c in (1, 2)]
        d = [None] + [[both(v, 1, 0) for v in p[c]] for c in (1, 2)]
        fz = [None] + [both(f[c], 1, 0) for c in (1, 2)]

        def row_parts(c):
            return (
                0.5 * p[c][1] + 0.125 * (d[c][0] + d[c][1]),
                0.125 * (p[c][1] + p[c][2]) + (1.0 / 24.0) * (d[c][0] + d[c][1] + d[c][2]),
            )

        own_y, own_yx = row_parts(1)
        own_x = 0.5 * p[2][2] + 0.125 * (d[2][0] + d[2][2])
        t24, t8 = (1.0 / 24.0) * fz[1], 0.125 * fz[1]
        total = 0.5 * d[2][0] + own_y + along_x(own_x + own_yx)
        total = total + k[2][0] * (0.5 * fz[2] + t8 + along_x(0.125 * fz[2] + t24))
        total = total + k[2][1] * (0.5 * f[1] + t8 + along_x(0.125 * f[1] + t24))
        total = total + k[2][2] * along_x(0.5 * f[2] + 0.125 * (fz[2] + f[1]) + t24)
        total = total[:NZ] + s1_ref[:, face, :]
        scaled = WEIGHT_TWO * inv[2][:NZ]
        s1_ref[:, face, :] = jnp.where(inner16, scaled, total)
        s2_ref[:, face, :] = jnp.where(inner16, KEEP * f[2][:NZ] + scaled * total, 0.0)

        own_y, own_yx = row_parts(2)
        t24, t8 = (1.0 / 24.0) * fz[2], 0.125 * fz[2]
        total = own_y + along_x(own_yx) + k[3][0] * (t8 + along_x(t24))
        total = total + k[3][1] * (0.5 * f[2] + t8 + along_x(0.125 * f[2] + t24))
        total = (total + k[3][2] * along_x(0.125 * f[2] + t24))[:NZ]
        scaled = s1_ref[:, second, :]
        s1_ref[:, second, :] = jnp.where(inner16, scaled, scaled + total)
        s2_ref[:, second, :] = s2_ref[:, second, :] + jnp.where(inner16, scaled * total, 0.0)


def slab_terms(mine, other, left):
    rows = NY + 8
    lane = iota((8, NX), 1)
    zp, c = lane >> 2, lane & 3
    real = zp < NZ + 2
    outer = c < 2 if left else c >= 2
    offset = jnp.where(outer, 0, 2) if left else jnp.where(outer, 2, 0)
    near = ((c == 1) | (c == 2)) & (zp < NZ + 1)
    offset_r = jnp.where(outer, RLANE - 1, RLANE) if left else jnp.where(outer, RLANE, RLANE - 1)
    at_r = jnp.where(near, zp + offset_r, 0)
    at_k = [jnp.where(real, a * KROWS + 2 * zp + (c & 1) + offset, 0) for a in range(3)]

    def spread(at, keep):
        pieces = []
        for i in range(0, rows, 8):
            piece = jnp.where(outer, take(other[i : i + 8], at), take(mine[i : i + 8], at))
            pieces.append(jnp.where(keep, piece, 0.0))
        return jnp.concatenate(pieces, axis=0)

    k = [spread(at, real) for at in at_k]
    res = spread(at_r, near)
    near = jnp.concatenate([near] * (rows // 8), axis=0)
    face = c == 2 if left else c == 1
    face = jnp.concatenate([face] * (rows // 8), axis=0)

    dz = [both(v, 4, 1) for v in k]
    part_0, part_y, part_x, part_yx = pair_stiffness(k, (None, None, None), dz)
    diag = SELF * (k[0] + k[1] + k[2]) + part_0 + both(part_y, 1, 0)
    diag = diag + both(part_x + both(part_yx, 1, 0), 1, 1)
    inv = 1.0 / diag
    f = jnp.where(near, WEIGHT_ONE * res * inv, 0.0)

    p = [v * f for v in k]
    d0, d1, d2 = (both(v, 4, 1) for v in p)
    own_y = 0.5 * p[1] + 0.125 * (d0 + d1)
    own_yx = 0.125 * (p[1] + p[2]) + (1.0 / 24.0) * (d0 + d1 + d2)
    own_x = 0.5 * p[2] + 0.125 * (d0 + d2)
    fz = both(f, 4, 1)
    fy, fyz = both(f, 1, 0), both(fz, 1, 0)
    t24, t8 = (1.0 / 24.0) * fyz, 0.125 * fyz
    total = 0.5 * d0 + both(own_y, 1, 0) + both(own_x + both(own_yx, 1, 0), 1, 1)
    total = total + k[0] * (0.5 * fz + t8 + both(0.125 * fz + t24, 1, 1))
    total = total + k[1] * (0.5 * fy + t8 + both(0.125 * fy + t24, 1, 1))
    total = total + k[2] * both(0.5 * f + 0.125 * (fz + fy) + t24, 1, 1)
    scaled = WEIGHT_TWO * inv
    times = jnp.where(face, scaled, total)
    plus = jnp.where(face, KEEP * f + scaled * total, 0.0)
    return times[:NY], plus[:NY]


def coarse_solve(cor_ref, lower, upper):
    xs = iota((16, NX), 1) & 31
    arrays = []
    for q in range(4):
        whole = jnp.where(xs < 4, roll(lower, -4 * q, 1), cor_ref[q])
        arrays.append(jnp.where((xs >= 20) & (xs < 24), roll(upper, 20 - 4 * q, 1), whole))
    kc, rhs = arrays[:3], arrays[3]
    lane = iota((16, NX), 1)

    def sides(values, axis):
        if axis == 0:
            return (
                jnp.where(lane >= 32, roll(values, 32, 1), 0.0),
                jnp.where(lane < 96, roll(values, -32, 1), 0.0),
            )
        if axis == 1:
            return roll(values, 1, 0), roll(values, -1, 0)
        return roll(values, 1, 1), roll(values, -1, 1)

    couple = [[0.5 * (kc[a] + v) for v in sides(kc[a], a)] for a in range(3)]
    diag = (MASS / 3.0) * (kc[0] + kc[1] + kc[2])
    for a in range(3):
        diag = diag + (couple[a][0] + couple[a][1])
    inside = kc[0] > 0.0
    scaled = jnp.where(inside, OMEGA / jnp.where(inside, diag, 1.0), 0.0)
    estimate = scaled * rhs
    for _ in range(CITERS - 1):
        off = None
        for a in range(3):
            low, high = sides(estimate, a)
            term = couple[a][0] * low + couple[a][1] * high
            off = term if off is None else off + term
        estimate = estimate + scaled * (rhs - (diag * estimate - off))
    return estimate[0:8]


def last_kernel(
    rb_ref, ra_ref, left_ref, right_ref, cor_ref, s1_ref, s2_ref, sel_ref, out_hbm, est_hbm, out_ref, est_ref, sems
):
    gx, gz = lax.axis_index("gx"), lax.axis_index("gz")
    even = gx % 2 == 0
    zero = jnp.zeros((XPAY, NX), F32)
    right = jnp.where(gx < lax.axis_size("gx") - 1, jnp.where(even, ra_ref[...], rb_ref[...]), zero)
    left = jnp.where(gx > 0, jnp.where(even, rb_ref[...], ra_ref[...]), zero)
    left_times, left_plus = slab_terms(left_ref[...], left[:40], True)
    right_times, right_plus = slab_terms(right_ref[...], right[:40], False)
    lane = iota((NY, NX), 1)
    low_side = (lane & 3) < 2
    times = jnp.where(low_side, right_times, left_times)
    plus = jnp.where(low_side, right_plus, left_plus)

    estimate = coarse_solve(cor_ref, left[40:XPAY], right[40:XPAY])
    lane8 = iota((8, NX), 1)
    rim = (lane < 2) | (lane >= NX - 2)
    step = 4
    for zc in range(CZ):
        z_out = jnp.where(gz == 0, zc, CZ - 1 - zc)
        est_ref[z_out] = roll(estimate, -(zc * 32 + 4), 1)[4:8, 0:CX]
    copies = [pltpu.make_async_copy(est_ref, est_hbm, sems.at[NZ // step])]
    copies[0].start()
    for zc in range(CZ):
        wide = take(estimate, zc * 32 + 4 + (lane8 >> 3))
        fine = jnp.concatenate([jnp.broadcast_to(wide[4 + y : 5 + y], (BLK, NX)) for y in range(CY)], axis=0)
        for i in range(BLK):
            zp = zc * BLK + i
            z = jnp.where(gz == 0, zp, NZ - 1 - zp)
            x_times = jnp.where(rim, roll(times, -(4 * zp + 2), 1), 0.0)
            x_plus = jnp.where(rim, roll(plus, -(4 * zp + 2), 1), 0.0)
            out_ref[z] = s2_ref[zp] + x_plus + s1_ref[zp] * x_times + sel_ref[z] * fine
            if zp % step == step - 1:
                planes = pl.ds(jnp.where(gz == 0, zp + 1 - step, NZ - 1 - zp), step)
                copies.append(pltpu.make_async_copy(out_ref.at[planes], out_hbm.at[planes], sems.at[zp // step]))
                copies[-1].start()
    for copy in copies:
        copy.wait()


def near(values):
    return pltpu.with_memory_space_constraint(values, pltpu.VMEM)


def call(kernel, inputs, outputs, scratch=(), aliases=None, us=0.1, name=None, in_space=pltpu.VMEM, out_spaces=None):
    return pl.pallas_call(
        kernel,
        out_shape=outputs,
        in_specs=[pl.BlockSpec(memory_space=in_space)] * len(inputs),
        out_specs=[pl.BlockSpec(memory_space=v) for v in out_spaces or [pltpu.VMEM] * len(outputs)],
        scratch_shapes=list(scratch),
        input_output_aliases=aliases or {},
        cost_estimate=pl.CostEstimate(flops=int(us * 1e9), bytes_accessed=0, transcendentals=0),
        compiler_params=pltpu.CompilerParams(vmem_limit_bytes=32 * 2**20),
        name=name,
    )(*inputs)


def vmem(*shape):
    return pltpu.VMEM(shape, F32)


def exchange(values, sizes, move):
    nx, ny, nz = sizes
    pairs = []
    for x in range(nx):
        for y in range(ny):
            for z in range(nz):
                a, b, c = move(x, y, z)
                pairs.append(((x * ny + y) * nz + z, (a * ny + b) * nz + c))
    return lax.ppermute(values, ("gx", "gy", "gz"), pairs)


def solution(mesh):
    sizes = (mesh.shape["gx"], mesh.shape["gy"], mesh.shape["gz"])
    nx, ny, nz = sizes

    def swap_z(values):
        return exchange(values, sizes, lambda x, y, z: (x, y, nz - 1 - z))

    def swap_y(values, odd):
        def move(x, y, z):
            b = y + 1 if y % 2 == odd else y - 1
            return (x, b, z) if 0 <= b < ny else (x ^ 1, y, z)

        return exchange(values, sizes, move)

    def swap_x(values, odd):
        return exchange(values, sizes, lambda x, y, z: ((x + 1 if x % 2 == odd else x - 1) % nx, y, z))

    def body(residual_in, labels, factor, basis, basis_index):
        inputs = [residual_in, labels, factor, basis, basis_index]
        kap, rr, sel, urgent = call(
            first_kernel,
            [pltpu.with_memory_space_constraint(v, pltpu.HBM) for v in inputs],
            [vmem(3, NZ + 1, NY, NX), vmem(NZ, NY, NX), vmem(NZ, NY, NX), vmem(ZURGENT, NX)],
            [
                pltpu.VMEM(labels.shape, jnp.int32),
                pltpu.VMEM(factor.shape, F32),
                pltpu.VMEM(basis.shape, F32),
                pltpu.VMEM(basis_index.shape, jnp.int32),
                pltpu.VMEM((4, BLK, BLK, NX), F32),
                pltpu.VMEM((64, NX), F32),
                pltpu.SemaphoreType.DMA((2,)),
                pltpu.SemaphoreType.DMA((len(PARTS), 3)),
            ],
            us=1.8,
            name="stiffness",
            in_space=pltpu.HBM,
        )
        kap, rr, sel, urgent = near(kap), near(rr), near(sel), near(urgent)
        zu = near(swap_z(urgent))
        ya, yb, bulk = call(rows_kernel, [kap, rr], [vmem(YPAY + URGENT, NX), vmem(YPAY, NX), vmem(BULK, NX)], name="rows")
        zb = near(swap_z(near(bulk)))
        left, right = call(columns_kernel, [kap, rr], [vmem(NY, NX), vmem(NY, NX)], us=0.4, name="columns")
        left, right = near(left), near(right)
        s1, f, p = call(
            inner_first_kernel,
            [kap, rr],
            [vmem(NZ, NY, NX), vmem(NZ, NY, NX), vmem(3, NZ, NY, NX)],
            us=0.6,
            name="inner_first",
        )
        s1, f, p = near(s1), near(f), near(p)
        ya, yb, ub = call(
            send_rows_kernel,
            [zu, urgent, left, right, near(ya), near(yb), f],
            [vmem(YPAY + URGENT, NX), vmem(YPAY, NX), vmem(URGENT, NX)],
            aliases={4: 0, 5: 1},
            us=10.0,
            name="send_rows",
        )
        ya, yb, ub = near(ya), near(yb), near(ub)
        wa, rb, wb = near(swap_y(ya, 0)), near(swap_y(ub, 1)), near(swap_y(yb, 1))
        left, right = call(columns_beyond_kernel, [left, right, zu], [vmem(NY, NX), vmem(NY, NX)], us=100.0, name="columns_beyond")
        xa, xb, left, right, cor = call(
            columns_more_kernel,
            [wa, rb, ub, near(left), near(right)],
            [vmem(XPAY, NX), vmem(XPAY, NX), vmem(40, NX), vmem(40, NX), vmem(4, 16, NX)],
            us=1.0,
            name="columns_more",
        )
        xa, xb = near(xa), near(xb)
        vb, va = near(swap_x(xb, 1)), near(swap_x(xa, 0))
        s1, s2 = call(
            inner_image_kernel,
            [kap, f, p, s1, xa],
            [vmem(NZ, NY, NX), vmem(NZ, NY, NX)],
            aliases={3: 0},
            us=0.6,
            name="inner_image",
        )
        s1, s2 = call(
            outer_kernel,
            [kap, rr, zb, f, p, near(s1), near(s2)],
            [vmem(NZ, NY, NX), vmem(NZ, NY, NX)],
            [pltpu.VMEM((3, 5, NY, NX), F32), pltpu.VMEM((4, NY, NX), F32), pltpu.VMEM((3, 4, NY, NX), F32)],
            aliases={5: 0, 6: 1},
            us=0.25,
            name="outer",
        )
        s1, s2 = call(
            edge_rows_kernel,
            [ya, yb, wa, wb, near(s1), near(s2)],
            [vmem(NZ, NY, NX), vmem(NZ, NY, NX)],
            aliases={4: 0, 5: 1},
            us=0.4,
            name="edge_rows",
        )
        out, estimate = call(
            last_kernel,
            [vb, va, near(left), near(right), near(cor), near(s1), near(s2), sel],
            [jax.ShapeDtypeStruct((NZ, NY, NX), F32), jax.ShapeDtypeStruct((CZ, CY, CX), F32)],
            [pltpu.VMEM((NZ, NY, NX), F32), pltpu.VMEM((CZ, CY, CX), F32), pltpu.SemaphoreType.DMA((5,))],
            us=1.5,
            name="last",
            out_spaces=[pltpu.HBM, pltpu.HBM],
        )
        return out, estimate

    in_specs = (
        P("gz", "gy", "gx"),
        P("gz", "gy", "gx"),
        P(None, "gz", "gy", "gx"),
        P(),
        P("gz", "gy", "gx"),
    )
    out_specs = (P("gz", "gy", "gx"), P("gz", "gy", "gx"))
    return jax.shard_map(body, mesh=mesh, in_specs=in_specs, out_specs=out_specs, check_vma=False)
```

```python
import math

import jax
import jax.numpy as jnp
from jax import lax
from jax.experimental import pallas as pl
from jax.experimental.pallas import tpu as pltpu
from jax.sharding import PartitionSpec as P

BLK = 8
CITERS = 4
BRICK = (0.6, 1.0, 1.0)
MORTAR = (0.25, 0.3, 0.3)
MASS = 0.05
OMEGA = 0.8
WEIGHT_ONE = 1.0 / (1.05 - 0.95 * math.cos(math.pi / 4))
WEIGHT_TWO = 1.0 / (1.05 + 0.95 * math.cos(math.pi / 4))
SELF = 1.0 + 1.0 + 1.0 / 3.0 + MASS / 3.0
KEEP = 1.0 + WEIGHT_TWO / WEIGHT_ONE - WEIGHT_TWO

NZ, NY, NX = 16, 32, 128
CZ, CY, CX = 2, 4, 16
PARTS = range(2)
F32 = jnp.float32
HIGHEST = lax.Precision.HIGHEST

BULK = 7 * NY
URGENT = 16
ZURGENT = 48
ZROW = 16
KROWS = 36
GROUP = NZ + 2
RROW = 3 * KROWS
YPAY = 128
XPAY = 40 + 16
RLANE = 110


def iota(shape, dim):
    return lax.broadcasted_iota(jnp.int32, shape, dim)


def roll(values, shift, axis):
    size = values.shape[axis]
    shift = shift % size
    return values if shift == 0 else pltpu.roll(values, shift, axis)


def both(values, step, axis):
    return roll(values, step, axis) + roll(values, -step, axis)


def take(values, lanes):
    return jnp.take_along_axis(values, lanes, axis=1, mode="promise_in_bounds")


def pair_stiffness(own, below, above):
    k0, k1, k2 = own
    d0, d1, d2 = (a + b if a is not None else b for a, b in zip(below, above))
    part_y = 0.5 * k1 + 0.125 * (d0 + d1)
    part_yx = 0.125 * (k1 + k2) + (1.0 / 24.0) * (d0 + d1 + d2)
    part_0 = 0.5 * d0
    part_x = 0.5 * k2 + 0.125 * (d0 + d2)
    return part_0, part_y, part_x, part_yx


def first_kernel(
    r_hbm, lab_hbm, fac_hbm, bas_hbm, bix_hbm, kap_ref, rr_ref, sel_ref, urgent_ref,
    lab_ref, fac_ref, bas_ref, bix_ref, tile_ref, sum_ref, sems, more_sems
):
    gz = lax.axis_index("gz")
    parts = []
    small = [
        pltpu.make_async_copy(bas_hbm, bas_ref, sems.at[0]),
        pltpu.make_async_copy(bix_hbm, bix_ref, sems.at[1]),
    ]
    for copy in small:
        copy.start()
    step = NZ // len(PARTS)
    for part in PARTS:
        planes = pl.ds(jnp.where(gz == 0, part * step, NZ - step - part * step), step)
        parts.append(
            [
                pltpu.make_async_copy(lab_hbm.at[planes], lab_ref.at[planes], more_sems.at[part, 0]),
                pltpu.make_async_copy(fac_hbm.at[:, planes], fac_ref.at[:, planes], more_sems.at[part, 1]),
                pltpu.make_async_copy(r_hbm.at[planes], rr_ref.at[planes], more_sems.at[part, 2]),
            ]
        )
        for copy in parts[part]:
            copy.start()
    sum_ref[...] = jnp.zeros(sum_ref.shape, F32)
    kap_ref[:, 0] = jnp.zeros((3, NY, NX), F32)
    for copy in small:
        copy.wait()
    tiled = lax.dot_general(
        bas_ref[...].reshape(4 * BLK * BLK, BLK),
        ((iota((BLK, NX), 1) & (BLK - 1)) == iota((BLK, NX), 0)).astype(F32),
        (((1,), (0,)), ((), ())),
        precision=HIGHEST,
        preferred_element_type=F32,
    )
    tile_ref[...] = tiled.reshape(4, BLK, BLK, NX)
    edges = [None] * 7
    spread = ((iota((CX, NX), 1) >> 3) == iota((CX, NX), 0)).astype(F32)
    for zc in range(CZ):
        index = lax.dot_general(
            bix_ref[jnp.where(gz == 0, zc, CZ - 1 - zc)].astype(F32),
            spread,
            (((1,), (0,)), ((), ())),
            precision=HIGHEST,
            preferred_element_type=F32,
        )
        index = jnp.concatenate([jnp.broadcast_to(index[y : y + 1], (BLK, NX)) for y in range(CY)], axis=0)
        sums = [None] * 4
        for i in range(BLK):
            zp = zc * BLK + i
            if zp % step == 0:
                for copy in parts[zp // step]:
                    copy.wait()
            z = jnp.where(gz == 0, zp, NZ - 1 - zp)
            zi = jnp.where(gz == 0, i, BLK - 1 - i)
            mortar = lab_ref[z] == 1
            b0, b1, b2, b3 = (jnp.concatenate([tile_ref[n, zi]] * CY, axis=0) for n in range(4))
            basis = jnp.where(index < 1.5, jnp.where(index < 0.5, b0, b1), jnp.where(index < 2.5, b2, b3))
            res = rr_ref[z]
            sel_ref[z] = basis
            terms = []
            for a in range(3):
                k = jnp.where(mortar, MORTAR[a], BRICK[a]) * fac_ref[a, z]
                kap_ref[a, zp + 1] = k
                terms.append(k)
                if zp >= NZ - 2:
                    plane = 2 * a + NZ - 1 - zp
                    edges[plane] = k
            if zp == NZ - 1:
                edges[6] = res
            terms.append(basis * res)
            sums = [t if s is None else s + t for s, t in zip(sums, terms)]
        for q in range(4):
            total = sums[q].reshape(CY, BLK, NX).sum(axis=1)
            sum_ref[(q * 2 + zc) * 8 : (q * 2 + zc) * 8 + CY] = total if q == 3 else total * (1.0 / BLK**3)
    bricks = lax.dot_general(
        sum_ref[...],
        ((iota((NX, NX), 0) >> 3) == (iota((NX, NX), 1) & (CX - 1))).astype(F32),
        (((1,), (0,)), ((), ())),
        precision=HIGHEST,
        preferred_element_type=F32,
    )
    group = iota((8, NX), 1) >> 4
    coarse = bricks[0:8]
    for g in range(1, 8):
        coarse = jnp.where(group == g, bricks[g * 8 : g * 8 + 8], coarse)
    urgent_ref[0:8] = coarse
    lane = iota((NY, NX), 1)
    columns = jnp.zeros((NY, NX), F32)
    for g, plane in enumerate(edges):
        columns = jnp.where(lane >= 4 * g, roll(plane, 4 * g + 2, 1), columns)
    lane = iota((8, NX), 1)
    folded = columns[:8]
    for i in range(1, NY // 8):
        folded = jnp.where(lane >= 32 * i, roll(columns[8 * i : 8 * i + 8], 32 * i, 1), folded)
    urgent_ref[8:16] = folded
    for g, plane in enumerate(edges[:6]):
        urgent_ref[ZROW + 4 * g : ZROW + 4 * g + 2] = plane[0:2]
        urgent_ref[ZROW + 4 * g + 2 : ZROW + 4 * g + 4] = plane[NY - 2 : NY]
    urgent_ref[ZROW + 24 : ZROW + 25] = edges[6][0:1]
    urgent_ref[ZROW + 25 : ZROW + 26] = edges[6][NY - 1 : NY]
    urgent_ref[ZROW + 26 : ZURGENT] = jnp.zeros((6, NX), F32)


def place(zp):
    return jnp.where(lax.axis_index("gz") == 0, zp, NZ - 1 - zp)


def rows_kernel(kap_ref, rr_ref, ya_ref, yb_ref, bulk_ref):
    even = lax.axis_index("gy") % 2 == 0

    def put(at, low, high):
        ya_ref[at : at + 1] = jnp.where(even, high, low)
        yb_ref[at : at + 1] = jnp.where(even, low, high)

    for zp in range(NZ):
        for a in range(3):
            at = a * KROWS + zp
            put(at, kap_ref[a, zp + 1, 1:2], kap_ref[a, zp + 1, NY - 2 : NY - 1])
            put(at + GROUP, kap_ref[a, zp + 1, 0:1], kap_ref[a, zp + 1, NY - 1 : NY])
        put(RROW + zp, rr_ref[place(zp), 0:1], rr_ref[place(zp), NY - 1 : NY])
    for a in range(3):
        for s in range(2):
            bulk_ref[(2 * a + s) * NY : (2 * a + s + 1) * NY] = kap_ref[a, NZ - s]
    bulk_ref[6 * NY : 7 * NY] = rr_ref[place(NZ - 1)]


def columns_kernel(kap_ref, rr_ref, left_ref, right_ref):
    lane = iota((NY, NX), 1)
    left = jnp.zeros((NY, NX), F32)
    right = jnp.zeros((NY, NX), F32)
    for a in range(3):
        for zp in range(NZ):
            at = 2 + a * KROWS + 2 * zp
            moved = roll(kap_ref[a, zp + 1], at, 1)
            left = jnp.where(lane >= at, moved, left)
            right = jnp.where(lane >= at - 2, moved, right)
    for zp in range(NZ):
        at = RLANE + zp
        moved = roll(rr_ref[place(zp)], at, 1)
        left = jnp.where(lane >= at, moved, left)
        right = jnp.where(lane >= at - 1, moved, right)
    left_ref[...] = left
    right_ref[...] = right


def columns_beyond(left, right, moved):
    lane = iota(left.shape, 1)
    for a in range(3):
        for s in range(2):
            at = 2 + a * KROWS + 2 * (NZ + s)
            values = moved(2 * a + s, at)
            left = jnp.where((lane == at) | (lane == at + 1), values, left)
            right = jnp.where((lane == at - 2) | (lane == at - 1), values, right)
    at = RLANE + NZ
    values = moved(6, at)
    return jnp.where(lane == at, values, left), jnp.where(lane == at - 1, values, right)


def columns_beyond_kernel(left_in, right_in, far_ref, left_ref, right_ref):
    folded = far_ref[8:16]
    columns = jnp.concatenate([roll(folded, -32 * i, 1) for i in range(NY // 8)], axis=0)
    left_ref[...], right_ref[...] = columns_beyond(
        left_in[...], right_in[...], lambda g, x0: roll(columns, x0 - 4 * g - 2, 1)
    )


def send_rows_kernel(far_ref, mine_ref, left_ref, right_ref, ya_in, yb_in, after_ref, ya_ref, yb_ref, ub_ref):
    even = lax.axis_index("gy") % 2 == 0

    def put(at, low, high):
        ya_ref[at : at + 1] = jnp.where(even, high, low)
        yb_ref[at : at + 1] = jnp.where(even, low, high)

    for a in range(3):
        for s in range(2):
            base, at = ZROW + (2 * a + s) * 4, a * KROWS + NZ + s
            put(at, far_ref[base + 1 : base + 2], far_ref[base + 2 : base + 3])
            put(at + GROUP, far_ref[base : base + 1], far_ref[base + 3 : base + 4])
    put(RROW + NZ, far_ref[ZROW + 24 : ZROW + 25], far_ref[ZROW + 25 : ZROW + 26])
    row = iota((8, NX), 0)
    folded = far_ref[8:16]
    corners = jnp.where(row < 2, folded, roll(roll(folded, -96, 1), 4, 0))

    def ends(ref):
        return jnp.where(row < 2, ref[0:8], roll(ref[NY - 8 : NY], 4, 0))

    left, right = columns_beyond(ends(left_ref), ends(right_ref), lambda g, x0: roll(corners, x0 - 4 * g - 2, 1))
    low = jnp.where(row < 2, left, roll(right, 2, 0))
    high = jnp.where(row < 2, roll(left, -2, 0), right)
    ya_ref[YPAY + 8 :] = jnp.where(even, high, low)
    ub_ref[8:16] = jnp.where(even, low, high)
    coarse = jnp.concatenate([mine_ref[0:CY], far_ref[0:CY]], axis=0)
    ya_ref[YPAY : YPAY + 8] = coarse
    ub_ref[0:8] = coarse


def columns_more_kernel(ra_ref, rb_ref, mine_ref, left_in, right_in, xa_ref, xb_ref, left_ref, right_ref, cor_ref):
    gx, gy = lax.axis_index("gx"), lax.axis_index("gy")
    even = gy % 2 == 0
    zero = jnp.zeros((URGENT, NX), F32)
    ra = ra_ref[YPAY:]
    hi = jnp.where(gy < lax.axis_size("gy") - 1, jnp.where(even, ra, rb_ref[...]), zero)
    lo = jnp.where(gy > 0, jnp.where(even, rb_ref[...], ra), zero)
    lane, row = iota((8, NX), 1), iota((8, NX), 0)

    def halo(shift):
        above, below = roll(hi[8:16], -shift, 0), roll(lo[8:16], 6 - shift, 0)
        return jnp.where(row < 2, above, jnp.where(row >= 6, below, 0.0))

    left_ref[0:NY] = left_in[...]
    right_ref[0:NY] = right_in[...]
    left_ref[NY : NY + 8] = halo(0)
    right_ref[NY : NY + 8] = halo(2)
    even_x = gx % 2 == 0
    xa_ref[0:40] = jnp.where(even_x, right_ref[...], left_ref[...])
    xb_ref[0:40] = jnp.where(even_x, left_ref[...], right_ref[...])

    tiles = [lo[0:8], mine_ref[0:8], hi[0:8]]
    zc, xs = lane >> 5, lane & 31
    pair = jnp.where(zc < 2, zc, 3 - zc)
    own = (xs >= 4) & (xs < 20)
    low_half, xs16 = lane < 64, iota((16, NX), 1) & 31
    sides = [jnp.zeros((16, NX), F32), jnp.zeros((16, NX), F32)]
    for q in range(4):
        at = (q * 2 + pair) * CX + jnp.clip(xs - 4, 0, CX - 1)
        below, mine, above = ((v, roll(v, 4, 0)) for v in (jnp.where(own, take(t, at), 0.0) for t in tiles))
        first = jnp.where(row < 4, jnp.where(low_half, below[0], below[1]), jnp.where(low_half, mine[1], mine[0]))
        second = jnp.where(row < 4, jnp.where(low_half, above[0], above[1]), 0.0)
        whole = jnp.concatenate([first, second], axis=0)
        cor_ref[q] = whole
        for i, start in enumerate((4, CX)):
            sides[i] = jnp.where((xs16 >= 4 * q) & (xs16 < 4 * q + 4), roll(whole, 4 * q - start, 1), sides[i])
    xa_ref[40:XPAY] = jnp.where(even_x, sides[1], sides[0])
    xb_ref[40:XPAY] = jnp.where(even_x, sides[0], sides[1])


def first_plane(to, zp, kap_ref, res, f_ref, p_ref, s1_ref, rim):
    below, k, above = ([kap_ref[a, zp + i] for a in range(3)] for i in range(3))
    part_0, part_y, part_x, part_yx = pair_stiffness(k, below, above)
    diag = SELF * (k[0] + k[1] + k[2]) + part_0 + both(part_y, 1, 0)
    inv = 1.0 / (diag + both(part_x + both(part_yx, 1, 0), 1, 1))
    f = jnp.where(rim, 0.0, WEIGHT_ONE * res * inv)
    f_ref[zp + 1] = f
    for a in range(3):
        p_ref[a, zp + 1] = k[a] * f
    if to < NZ if isinstance(to, int) else True:
        s1_ref[to] = WEIGHT_TWO * inv


def image_plane(to, zp, kap_ref, f_ref, p_ref, s1_ref, s2_ref, rim):
    k = [kap_ref[a, zp + 1] for a in range(3)]
    p = [p_ref[a, zp + 1] for a in range(3)]
    d0, d1, d2 = (p_ref[a, zp] + p_ref[a, zp + 2] for a in range(3))
    f, fz = f_ref[zp + 1], f_ref[zp] + f_ref[zp + 2]
    own_y = 0.5 * p[1] + 0.125 * (d0 + d1)
    own_yx = 0.125 * (p[1] + p[2]) + (1.0 / 24.0) * (d0 + d1 + d2)
    own_x = 0.5 * p[2] + 0.125 * (d0 + d2)
    fy, fyz = both(f, 1, 0), both(fz, 1, 0)
    t24, t8 = (1.0 / 24.0) * fyz, 0.125 * fyz
    total = 0.5 * d0 + both(own_y, 1, 0) + both(own_x + both(own_yx, 1, 0), 1, 1)
    total = total + k[0] * (0.5 * fz + t8 + both(0.125 * fz + t24, 1, 1))
    total = total + k[1] * (0.5 * fy + t8 + both(0.125 * fy + t24, 1, 1))
    total = total + k[2] * both(0.5 * f + 0.125 * (fz + fy) + t24, 1, 1)
    scaled = s1_ref[to]
    s1_ref[to] = jnp.where(rim, total, scaled)
    s2_ref[to] = jnp.where(rim, 0.0, KEEP * f + scaled * total)


def plane_rim():
    row, lane = iota((NY, NX), 0), iota((NY, NX), 1)
    return (row == 0) | (row == NY - 1) | (lane == 0) | (lane == NX - 1)


def inner_first_kernel(kap_ref, rr_ref, s1_ref, f_ref, p_ref):
    rim = plane_rim()
    f_ref[0] = jnp.zeros((NY, NX), F32)
    p_ref[:, 0] = jnp.zeros((3, NY, NX), F32)

    @pl.loop(0, 3)
    def _(i):
        for j in range(5):
            zp = i * 5 + j
            first_plane(zp, zp, kap_ref, rr_ref[place(zp)], f_ref, p_ref, s1_ref, rim)


def inner_image_kernel(kap_ref, f_ref, p_ref, s1_in, after_ref, s1_ref, s2_ref):
    rim = plane_rim()

    @pl.loop(0, 2)
    def _(i):
        for j in range(7):
            image_plane(i * 7 + j, i * 7 + j, kap_ref, f_ref, p_ref, s1_ref, s2_ref, rim)


def outer_kernel(kap_ref, rr_ref, bulk_ref, f_in, p_in, s1_in, s2_in, s1_ref, s2_ref, k_ref, f_ref, p_ref):
    rim = plane_rim()
    for a in range(3):
        for i in range(3):
            k_ref[a, i] = kap_ref[a, NZ - 2 + i]
        for i in range(2):
            k_ref[a, 3 + i] = bulk_ref[(2 * a + i) * NY : (2 * a + i + 1) * NY]
            p_ref[a, i] = p_in[a, NZ - 2 + i]
    for i in range(2):
        f_ref[i] = f_in[NZ - 2 + i]
    first_plane(NZ - 1, 1, k_ref, rr_ref[place(NZ - 1)], f_ref, p_ref, s1_ref, rim)
    first_plane(NZ, 2, k_ref, bulk_ref[6 * NY : 7 * NY], f_ref, p_ref, s1_ref, rim)
    for i in range(2):
        image_plane(NZ - 2 + i, i, k_ref, f_ref, p_ref, s1_ref, s2_ref, rim)


def along_x(values):
    return both(values, 1, 1)


def edge_rows_kernel(ya_ref, yb_ref, ra_ref, rb_ref, s1_in, s2_in, s1_ref, s2_ref):
    even = lax.axis_index("gy") % 2 == 0
    size = 24
    row, lane = iota((size, NX), 0), iota((size, NX), 1)
    inner = (lane > 0) & (lane < NX - 1)
    near = inner & (row < NZ + 1)
    inner16 = inner[:NZ]
    gy = lax.axis_index("gy")
    zero = jnp.zeros((YPAY, NX), F32)
    ya, yb, ra, rb = ya_ref[0:YPAY], yb_ref[...], ra_ref[0:YPAY], rb_ref[...]
    hi = jnp.where(gy < lax.axis_size("gy") - 1, jnp.where(even, ra, rb), zero)
    lo = jnp.where(gy > 0, jnp.where(even, rb, ra), zero)
    for other, mine, face, second in (
        (lo, jnp.where(even, yb, ya), 0, 1),
        (hi, jnp.where(even, ya, yb), NY - 1, NY - 2),
    ):

        def group(source, at):
            return jnp.where(row < GROUP, source[at : at + size], 0.0)

        k = [[group(other, a * KROWS + s * GROUP) for a in range(3)] for s in (0, 1)]
        k += [[group(mine, a * KROWS + s * GROUP) for a in range(3)] for s in (1, 0)]
        parts = [pair_stiffness(v, (None, None, None), [both(u, 1, 0) for u in v]) for v in k]
        res = [None] + [jnp.where(row < NZ + 1, v[YPAY - size :], 0.0) for v in (roll(other, 4 - 8, 0), roll(mine, 4 - 8, 0))]
        f, inv = [None] * 3, [None] * 3
        for c in (1, 2):
            diag = SELF * (k[c][0] + k[c][1] + k[c][2]) + parts[c][0] + parts[c - 1][1] + parts[c + 1][1]
            inv[c] = 1.0 / (diag + along_x(parts[c][2] + parts[c - 1][3] + parts[c + 1][3]))
            f[c] = jnp.where(near, WEIGHT_ONE * res[c] * inv[c], 0.0)
        p = [None] + [[v * f[c] for v in k[c]] for c in (1, 2)]
        d = [None] + [[both(v, 1, 0) for v in p[c]] for c in (1, 2)]
        fz = [None] + [both(f[c], 1, 0) for c in (1, 2)]

        def row_parts(c):
            return (
                0.5 * p[c][1] + 0.125 * (d[c][0] + d[c][1]),
                0.125 * (p[c][1] + p[c][2]) + (1.0 / 24.0) * (d[c][0] + d[c][1] + d[c][2]),
            )

        own_y, own_yx = row_parts(1)
        own_x = 0.5 * p[2][2] + 0.125 * (d[2][0] + d[2][2])
        t24, t8 = (1.0 / 24.0) * fz[1], 0.125 * fz[1]
        total = 0.5 * d[2][0] + own_y + along_x(own_x + own_yx)
        total = total + k[2][0] * (0.5 * fz[2] + t8 + along_x(0.125 * fz[2] + t24))
        total = total + k[2][1] * (0.5 * f[1] + t8 + along_x(0.125 * f[1] + t24))
        total = total + k[2][2] * along_x(0.5 * f[2] + 0.125 * (fz[2] + f[1]) + t24)
        total = total[:NZ] + s1_ref[:, face, :]
        scaled = WEIGHT_TWO * inv[2][:NZ]
        s1_ref[:, face, :] = jnp.where(inner16, scaled, total)
        s2_ref[:, face, :] = jnp.where(inner16, KEEP * f[2][:NZ] + scaled * total, 0.0)

        own_y, own_yx = row_parts(2)
        t24, t8 = (1.0 / 24.0) * fz[2], 0.125 * fz[2]
        total = own_y + along_x(own_yx) + k[3][0] * (t8 + along_x(t24))
        total = total + k[3][1] * (0.5 * f[2] + t8 + along_x(0.125 * f[2] + t24))
        total = (total + k[3][2] * along_x(0.125 * f[2] + t24))[:NZ]
        scaled = s1_ref[:, second, :]
        s1_ref[:, second, :] = jnp.where(inner16, scaled, scaled + total)
        s2_ref[:, second, :] = s2_ref[:, second, :] + jnp.where(inner16, scaled * total, 0.0)


def slab_lanes(left):
    lane = iota((8, NX), 1)
    zp, c = lane >> 2, lane & 3
    outer = c < 2 if left else c >= 2
    real = zp < GROUP
    near = ((c == 1) | (c == 2)) & (zp < NZ + 1)
    offset = jnp.where(outer, 0, 2) if left else jnp.where(outer, 2, 0)
    offset_r = jnp.where(outer, RLANE - 1, RLANE) if left else jnp.where(outer, RLANE, RLANE - 1)
    sources = [jnp.where(real, a * KROWS + 2 * zp + (c & 1) + offset, 0) for a in range(3)]
    sources.append(jnp.where(near, zp + offset_r, 0))
    return outer, [real] * 3 + [near], sources


def slab_kernel(left_ref, right_ref, after_ref, slab_ref):
    for side, pack in enumerate((left_ref, right_ref)):
        outer, keeps, sources = slab_lanes(side == 0)
        for q in range(4):
            for i in range(0, NY + 8, 8):
                piece = take(pack[i : i + 8], sources[q])
                slab_ref[side, q, i : i + 8] = jnp.where(keeps[q] & ~outer, piece, 0.0)


def rim_kernel(s1_ref, s2_ref, rim1_ref, rim2_ref):
    lane = iota((NY, NX), 1)
    for source, rim in ((s1_ref, rim1_ref), (s2_ref, rim2_ref)):
        values = jnp.zeros((NY, NX), F32)
        for zp in range(NZ):
            values = jnp.where(lane >= 4 * zp, roll(source[zp], 4 * zp + 2, 1), values)
        rim[...] = values


def slab_terms(mine, other, rim1, rim2, left):
    rows = NY + 8
    outer, keeps, sources = slab_lanes(left)

    def spread(q):
        pieces = []
        for i in range(0, rows, 8):
            pieces.append(jnp.where(keeps[q] & outer, take(other[i : i + 8], sources[q]), mine[q, i : i + 8]))
        return jnp.concatenate(pieces, axis=0)

    k = [spread(a) for a in range(3)]
    res = spread(3)
    c = iota((rows, NX), 1) & 3
    near = jnp.concatenate([keeps[3]] * (rows // 8), axis=0)

    dz = [both(v, 4, 1) for v in k]
    part_0, part_y, part_x, part_yx = pair_stiffness(k, (None, None, None), dz)
    diag = SELF * (k[0] + k[1] + k[2]) + part_0 + both(part_y, 1, 0)
    inv = 1.0 / (diag + both(part_x + both(part_yx, 1, 0), 1, 1))
    f = jnp.where(near, WEIGHT_ONE * res * inv, 0.0)

    def from_outer(values):
        return roll(values, 1 if left else -1, 1)

    p = [v * f for v in k]
    d0, d1, d2 = (both(v, 4, 1) for v in p)
    own_y = 0.5 * p[1] + 0.125 * (d0 + d1)
    own_yx = 0.125 * (p[1] + p[2]) + (1.0 / 24.0) * (d0 + d1 + d2)
    own_x = 0.5 * p[2] + 0.125 * (d0 + d2)
    fz = both(f, 4, 1)
    fy, fyz = both(f, 1, 0)[:NY], both(fz, 1, 0)[:NY]
    fc, fz = f[:NY], fz[:NY]
    k = [v[:NY] for v in k]
    t24, t8 = (1.0 / 24.0) * fyz, 0.125 * fyz
    total = 0.5 * d0[:NY] + both(own_y, 1, 0)[:NY] + from_outer(own_x[:NY] + both(own_yx, 1, 0)[:NY])
    total = total + k[0] * (0.5 * fz + t8 + from_outer(0.125 * fz + t24))
    total = total + k[1] * (0.5 * fy + t8 + from_outer(0.125 * fy + t24))
    total = total + k[2] * from_outer(0.5 * fc + 0.125 * (fz + fy) + t24)
    face = (c == 2 if left else c == 1)[:NY]
    return jnp.where(face, KEEP * fc + WEIGHT_TWO * inv[:NY] * (total + rim1), rim2 + rim1 * total)


def coarse_solve(cor_ref, lower, upper):
    xs = iota((16, NX), 1) & 31
    arrays = []
    for q in range(4):
        whole = jnp.where(xs < 4, roll(lower, -4 * q, 1), cor_ref[q])
        arrays.append(jnp.where((xs >= 20) & (xs < 24), roll(upper, 20 - 4 * q, 1), whole))
    kc, rhs = arrays[:3], arrays[3]
    lane = iota((16, NX), 1)

    def sides(values, axis):
        if axis == 0:
            return roll(values, 32, 1), roll(values, -32, 1)
        return roll(values, 1, axis - 1), roll(values, -1, axis - 1)

    within = [(lane >= 32, lane < 96), (None, None), (None, None)]
    diag = (1.0 + MASS / 3.0) * (kc[0] + kc[1] + kc[2])
    couple = []
    for a in range(3):
        for v, real in zip(sides(kc[a], a), within[a]):
            half = 0.5 * v if real is None else jnp.where(real, 0.5 * v, 0.0)
            diag = diag + half
            half = 0.5 * kc[a] + half
            couple.append(half if real is None else jnp.where(real, half, 0.0))
    inside = kc[0] > 0.0
    scaled = jnp.where(inside, OMEGA / jnp.where(inside, diag, 1.0), 0.0)
    couple = [scaled * v for v in couple]
    start = scaled * rhs
    estimate = start
    for _ in range(CITERS - 1):
        t = [v * u for v, u in zip(couple, [u for a in range(3) for u in sides(estimate, a)])]
        estimate = (start + (1.0 - OMEGA) * estimate) + (((t[0] + t[1]) + (t[2] + t[3])) + (t[4] + t[5]))
    return estimate[0:8]


def last_kernel(
    rb_ref, ra_ref, slab_ref, cor_ref, rim1_ref, rim2_ref, s2_ref, sel_ref, out_hbm, est_hbm, out_ref, est_ref, sems
):
    gx, gz = lax.axis_index("gx"), lax.axis_index("gz")
    even = gx % 2 == 0
    zero = jnp.zeros((XPAY, NX), F32)
    right = jnp.where(gx < lax.axis_size("gx") - 1, jnp.where(even, ra_ref[...], rb_ref[...]), zero)
    left = jnp.where(gx > 0, jnp.where(even, rb_ref[...], ra_ref[...]), zero)
    rim1, rim2 = rim1_ref[...], rim2_ref[...]
    from_left = slab_terms(slab_ref[0], left[:40], rim1, rim2, True)
    from_right = slab_terms(slab_ref[1], right[:40], rim1, rim2, False)
    lane = iota((NY, NX), 1)
    faces = jnp.where((lane & 3) < 2, from_right, from_left)

    estimate = coarse_solve(cor_ref, left[40:XPAY], right[40:XPAY])
    lane8 = iota((8, NX), 1)
    rim = (lane < 2) | (lane >= NX - 2)
    step = 4
    for zc in range(CZ):
        z_out = jnp.where(gz == 0, zc, CZ - 1 - zc)
        est_ref[z_out] = roll(estimate, -(zc * 32 + 4), 1)[4:8, 0:CX]
    copies = [pltpu.make_async_copy(est_ref, est_hbm, sems.at[NZ // step])]
    copies[0].start()
    for zc in range(CZ):
        wide = take(estimate, zc * 32 + 4 + (lane8 >> 3))
        fine = jnp.concatenate([jnp.broadcast_to(wide[4 + y : 5 + y], (BLK, NX)) for y in range(CY)], axis=0)
        for i in range(BLK):
            zp = zc * BLK + i
            z = jnp.where(gz == 0, zp, NZ - 1 - zp)
            out_ref[z] = jnp.where(rim, roll(faces, -(4 * zp + 2), 1), s2_ref[zp]) + sel_ref[z] * fine
            if zp % step == step - 1:
                planes = pl.ds(jnp.where(gz == 0, zp + 1 - step, NZ - 1 - zp), step)
                copies.append(pltpu.make_async_copy(out_ref.at[planes], out_hbm.at[planes], sems.at[zp // step]))
                copies[-1].start()
    for copy in copies:
        copy.wait()


def near(values):
    return pltpu.with_memory_space_constraint(values, pltpu.VMEM)


def call(kernel, inputs, outputs, scratch=(), aliases=None, us=0.1, name=None, in_space=pltpu.VMEM, out_spaces=None):
    return pl.pallas_call(
        kernel,
        out_shape=outputs,
        in_specs=[pl.BlockSpec(memory_space=in_space)] * len(inputs),
        out_specs=[pl.BlockSpec(memory_space=v) for v in out_spaces or [pltpu.VMEM] * len(outputs)],
        scratch_shapes=list(scratch),
        input_output_aliases=aliases or {},
        cost_estimate=pl.CostEstimate(flops=int(us * 1e9), bytes_accessed=0, transcendentals=0),
        compiler_params=pltpu.CompilerParams(vmem_limit_bytes=32 * 2**20),
        name=name,
    )(*inputs)


def vmem(*shape):
    return pltpu.VMEM(shape, F32)


def exchange(values, sizes, move):
    nx, ny, nz = sizes
    pairs = []
    for x in range(nx):
        for y in range(ny):
            for z in range(nz):
                a, b, c = move(x, y, z)
                pairs.append(((x * ny + y) * nz + z, (a * ny + b) * nz + c))
    return lax.ppermute(values, ("gx", "gy", "gz"), pairs)


def solution(mesh):
    sizes = (mesh.shape["gx"], mesh.shape["gy"], mesh.shape["gz"])
    nx, ny, nz = sizes

    def swap_z(values):
        return exchange(values, sizes, lambda x, y, z: (x, y, nz - 1 - z))

    def swap_y(values, odd):
        def move(x, y, z):
            b = y + 1 if y % 2 == odd else y - 1
            return (x, b, z) if 0 <= b < ny else (x ^ 1, y, z)

        return exchange(values, sizes, move)

    def swap_x(values, odd):
        return exchange(values, sizes, lambda x, y, z: ((x + 1 if x % 2 == odd else x - 1) % nx, y, z))

    def body(residual_in, labels, factor, basis, basis_index):
        inputs = [residual_in, labels, factor, basis, basis_index]
        kap, rr, sel, urgent = call(
            first_kernel,
            [pltpu.with_memory_space_constraint(v, pltpu.HBM) for v in inputs],
            [vmem(3, NZ + 1, NY, NX), vmem(NZ, NY, NX), vmem(NZ, NY, NX), vmem(ZURGENT, NX)],
            [
                pltpu.VMEM(labels.shape, jnp.int32),
                pltpu.VMEM(factor.shape, F32),
                pltpu.VMEM(basis.shape, F32),
                pltpu.VMEM(basis_index.shape, jnp.int32),
                pltpu.VMEM((4, BLK, BLK, NX), F32),
                pltpu.VMEM((64, NX), F32),
                pltpu.SemaphoreType.DMA((2,)),
                pltpu.SemaphoreType.DMA((len(PARTS), 3)),
            ],
            us=1.8,
            name="stiffness",
            in_space=pltpu.HBM,
        )
        kap, rr, sel, urgent = near(kap), near(rr), near(sel), near(urgent)
        zu = near(swap_z(urgent))
        ya, yb, bulk = call(rows_kernel, [kap, rr], [vmem(YPAY + URGENT, NX), vmem(YPAY, NX), vmem(BULK, NX)], name="rows")
        zb = near(swap_z(near(bulk)))
        left, right = call(columns_kernel, [kap, rr], [vmem(NY, NX), vmem(NY, NX)], us=0.4, name="columns")
        left, right = near(left), near(right)
        s1, f, p = call(
            inner_first_kernel,
            [kap, rr],
            [vmem(NZ, NY, NX), vmem(NZ, NY, NX), vmem(3, NZ, NY, NX)],
            us=0.6,
            name="inner_first",
        )
        s1, f, p = near(s1), near(f), near(p)
        ya, yb, ub = call(
            send_rows_kernel,
            [zu, urgent, left, right, near(ya), near(yb), f],
            [vmem(YPAY + URGENT, NX), vmem(YPAY, NX), vmem(URGENT, NX)],
            aliases={4: 0, 5: 1},
            us=10.0,
            name="send_rows",
        )
        ya, yb, ub = near(ya), near(yb), near(ub)
        wa, rb, wb = near(swap_y(ya, 0)), near(swap_y(ub, 1)), near(swap_y(yb, 1))
        left, right = call(columns_beyond_kernel, [left, right, zu], [vmem(NY, NX), vmem(NY, NX)], us=100.0, name="columns_beyond")
        xa, xb, left, right, cor = call(
            columns_more_kernel,
            [wa, rb, ub, near(left), near(right)],
            [vmem(XPAY, NX), vmem(XPAY, NX), vmem(40, NX), vmem(40, NX), vmem(4, 16, NX)],
            us=1.0,
            name="columns_more",
        )
        xa, xb = near(xa), near(xb)
        vb, va = near(swap_x(xb, 1)), near(swap_x(xa, 0))
        s1, s2 = call(
            inner_image_kernel,
            [kap, f, p, s1, xa],
            [vmem(NZ, NY, NX), vmem(NZ, NY, NX)],
            aliases={3: 0},
            us=0.6,
            name="inner_image",
        )
        s1, s2 = call(
            outer_kernel,
            [kap, rr, zb, f, p, near(s1), near(s2)],
            [vmem(NZ, NY, NX), vmem(NZ, NY, NX)],
            [pltpu.VMEM((3, 5, NY, NX), F32), pltpu.VMEM((4, NY, NX), F32), pltpu.VMEM((3, 4, NY, NX), F32)],
            aliases={5: 0, 6: 1},
            us=0.25,
            name="outer",
        )
        s1, s2 = call(
            edge_rows_kernel,
            [ya, yb, wa, wb, near(s1), near(s2)],
            [vmem(NZ, NY, NX), vmem(NZ, NY, NX)],
            aliases={4: 0, 5: 1},
            us=0.4,
            name="edge_rows",
        )
        (slab,) = call(slab_kernel, [near(left), near(right), xa], [vmem(2, 4, 40, NX)], us=0.1, name="slab")
        rim1, rim2 = call(rim_kernel, [near(s1), near(s2)], [vmem(NY, NX), vmem(NY, NX)], us=0.2, name="rim")
        out, estimate = call(
            last_kernel,
            [vb, va, near(slab), near(cor), near(rim1), near(rim2), near(s2), sel],
            [jax.ShapeDtypeStruct((NZ, NY, NX), F32), jax.ShapeDtypeStruct((CZ, CY, CX), F32)],
            [pltpu.VMEM((NZ, NY, NX), F32), pltpu.VMEM((CZ, CY, CX), F32), pltpu.SemaphoreType.DMA((5,))],
            us=1.5,
            name="last",
            out_spaces=[pltpu.HBM, pltpu.HBM],
        )
        return out, estimate

    in_specs = (
        P("gz", "gy", "gx"),
        P("gz", "gy", "gx"),
        P(None, "gz", "gy", "gx"),
        P(),
        P("gz", "gy", "gx"),
    )
    out_specs = (P("gz", "gy", "gx"), P("gz", "gy", "gx"))
    return jax.shard_map(body, mesh=mesh, in_specs=in_specs, out_specs=out_specs, check_vma=False)
```

```python
import math

import jax
import jax.numpy as jnp
from jax import lax
from jax.experimental import pallas as pl
from jax.experimental.pallas import tpu as pltpu
from jax.sharding import PartitionSpec as P

BLK = 8
CITERS = 4
BRICK = (0.6, 1.0, 1.0)
MORTAR = (0.25, 0.3, 0.3)
MASS = 0.05
OMEGA = 0.8
WEIGHT_ONE = 1.0 / (1.05 - 0.95 * math.cos(math.pi / 4))
WEIGHT_TWO = 1.0 / (1.05 + 0.95 * math.cos(math.pi / 4))
SELF = 1.0 + 1.0 + 1.0 / 3.0 + MASS / 3.0
KEEP = 1.0 + WEIGHT_TWO / WEIGHT_ONE - WEIGHT_TWO

NZ, NY, NX = 16, 32, 128
CZ, CY, CX = 2, 4, 16
PARTS = range(2)
F32 = jnp.float32
HIGHEST = lax.Precision.HIGHEST

BULK = 7 * NY + 24
BCOL, BROW = 7 * NY, 7 * NY + 8
URGENT = 16
ZURGENT = 32
KROWS = 36
GROUP = NZ + 2
RROW = 3 * KROWS
YPAY = 128
XPAY = 40 + 16
RLANE = 110


def iota(shape, dim):
    return lax.broadcasted_iota(jnp.int32, shape, dim)


def roll(values, shift, axis):
    size = values.shape[axis]
    shift = shift % size
    return values if shift == 0 else pltpu.roll(values, shift, axis)


def both(values, step, axis):
    return roll(values, step, axis) + roll(values, -step, axis)


def take(values, lanes):
    return jnp.take_along_axis(values, lanes, axis=1, mode="promise_in_bounds")


def pair_stiffness(own, below, above):
    k0, k1, k2 = own
    d0, d1, d2 = (a + b if a is not None else b for a, b in zip(below, above))
    part_y = 0.5 * k1 + 0.125 * (d0 + d1)
    part_yx = 0.125 * (k1 + k2) + (1.0 / 24.0) * (d0 + d1 + d2)
    part_0 = 0.5 * d0
    part_x = 0.5 * k2 + 0.125 * (d0 + d2)
    return part_0, part_y, part_x, part_yx


def first_kernel(
    r_hbm, lab_hbm, fac_hbm, bas_hbm, bix_hbm, kap_ref, rr_ref, sel_ref, urgent_ref,
    lab_ref, fac_ref, bas_ref, bix_ref, tile_ref, sum_ref, sems, more_sems
):
    gz = lax.axis_index("gz")
    parts = []
    small = [
        pltpu.make_async_copy(bas_hbm, bas_ref, sems.at[0]),
        pltpu.make_async_copy(bix_hbm, bix_ref, sems.at[1]),
    ]
    for copy in small:
        copy.start()
    step = NZ // len(PARTS)
    for part in PARTS:
        planes = pl.ds(jnp.where(gz == 0, part * step, NZ - step - part * step), step)
        parts.append(
            [
                pltpu.make_async_copy(lab_hbm.at[planes], lab_ref.at[planes], more_sems.at[part, 0]),
                pltpu.make_async_copy(fac_hbm.at[:, planes], fac_ref.at[:, planes], more_sems.at[part, 1]),
                pltpu.make_async_copy(r_hbm.at[planes], rr_ref.at[planes], more_sems.at[part, 2]),
            ]
        )
        for copy in parts[part]:
            copy.start()
    kap_ref[:, 0] = jnp.zeros((3, NY, NX), F32)
    for copy in small:
        copy.wait()
    tiled = lax.dot_general(
        bas_ref[...].reshape(4 * BLK * BLK, BLK),
        ((iota((BLK, NX), 1) & (BLK - 1)) == iota((BLK, NX), 0)).astype(F32),
        (((1,), (0,)), ((), ())),
        precision=HIGHEST,
        preferred_element_type=F32,
    )
    tile_ref[...] = tiled.reshape(4, BLK, BLK, NX)
    edges = [None] * 7
    spread = ((iota((CX, NX), 1) >> 3) == iota((CX, NX), 0)).astype(F32)
    indices = []
    for zc in range(CZ):
        index = lax.dot_general(
            bix_ref[jnp.where(gz == 0, zc, CZ - 1 - zc)].astype(F32),
            spread,
            (((1,), (0,)), ((), ())),
            precision=HIGHEST,
            preferred_element_type=F32,
        )
        indices.append(jnp.concatenate([jnp.broadcast_to(index[y : y + 1], (BLK, NX)) for y in range(CY)], axis=0))
    for zc in range(CZ):
        index = indices[zc]
        sums = [None] * 4
        for i in range(BLK):
            zp = zc * BLK + i
            if zp % step == 0:
                for copy in parts[zp // step]:
                    copy.wait()
            z = jnp.where(gz == 0, zp, NZ - 1 - zp)
            zi = jnp.where(gz == 0, i, BLK - 1 - i)
            mortar = lab_ref[z] == 1
            b0, b1, b2, b3 = (jnp.concatenate([tile_ref[n, zi]] * CY, axis=0) for n in range(4))
            basis = jnp.where(index < 1.5, jnp.where(index < 0.5, b0, b1), jnp.where(index < 2.5, b2, b3))
            res = rr_ref[z]
            sel_ref[z] = basis
            terms = []
            for a in range(3):
                k = jnp.where(mortar, MORTAR[a], BRICK[a]) * fac_ref[a, z]
                kap_ref[a, zp + 1] = k
                terms.append(k)
                if zp >= NZ - 2:
                    plane = 2 * a + NZ - 1 - zp
                    edges[plane] = k
            if zp == NZ - 1:
                edges[6] = res
            terms.append(basis * res)
            sums = [t if s is None else s + t for s, t in zip(sums, terms)]
        for q in range(4):
            total = sums[q].reshape(CY, BLK, NX).sum(axis=1)
            total = total if q == 3 else total * (1.0 / BLK**3)
            at = (q * 2 + zc) * 8
            sum_ref[at : at + CY] = total
            sum_ref[at + CY : at + 8] = total
    gather = ((iota((NX, NX), 0) >> 3) == (iota((NX, NX), 1) & (CX - 1))).astype(jnp.bfloat16)
    rest, bricks = sum_ref[...], None
    for _ in range(3):
        part = rest.astype(jnp.bfloat16)
        rest = rest - part.astype(F32)
        term = lax.dot_general(part, gather, (((1,), (0,)), ((), ())), preferred_element_type=F32)
        bricks = term if bricks is None else bricks + term
    group = iota((8, NX), 1) >> 4
    coarse = bricks[0:8]
    for g in range(1, 8):
        coarse = jnp.where(group == g, bricks[g * 8 : g * 8 + 8], coarse)
    urgent_ref[0:8] = coarse
    even = lax.axis_index("gy") % 2 == 0
    row = iota((8, NX), 0)

    def ends(plane):
        return jnp.where(row < 4, plane[:8], plane[NY - 8 :])

    left, right = columns_beyond(
        jnp.zeros((8, NX), F32), jnp.zeros((8, NX), F32), lambda g, x0: roll(ends(edges[g]), x0, 1)
    )
    urgent_ref[8:16] = end_tile(left, right)
    for g, plane in enumerate(edges):
        a, beyond = divmod(g, 2)
        for inner in range(2) if g < 6 else (1,):
            at = 12 if g == 6 else 4 * a + 2 * inner + beyond
            low = plane[0:1] if inner else plane[1:2]
            high = plane[NY - 1 : NY] if inner else plane[NY - 2 : NY - 1]
            urgent_ref[16 + at : 17 + at] = jnp.where(even, high, low)


def end_tile(left, right):
    row = iota((8, NX), 0)
    low = jnp.where(row < 2, left, roll(right, 2, 0))
    high = jnp.where(row < 6, roll(left, -2, 0), right)
    return jnp.where(row < 4, low, high)


def place(zp):
    return jnp.where(lax.axis_index("gz") == 0, zp, NZ - 1 - zp)


def rows_kernel(kap_ref, rr_ref, ya_ref, yb_ref, bulk_ref):
    even = lax.axis_index("gy") % 2 == 0

    def put(at, low, high):
        ya_ref[at : at + 1] = jnp.where(even, high, low)
        yb_ref[at : at + 1] = jnp.where(even, low, high)

    for zp in range(NZ):
        for a in range(3):
            at = a * KROWS + zp
            put(at, kap_ref[a, zp + 1, 1:2], kap_ref[a, zp + 1, NY - 2 : NY - 1])
            put(at + GROUP, kap_ref[a, zp + 1, 0:1], kap_ref[a, zp + 1, NY - 1 : NY])
        put(RROW + zp, rr_ref[place(zp), 0:1], rr_ref[place(zp), NY - 1 : NY])
    for a in range(3):
        for s in range(2):
            bulk_ref[(2 * a + s) * NY : (2 * a + s + 1) * NY] = kap_ref[a, NZ - s]
    bulk_ref[6 * NY : 7 * NY] = rr_ref[place(NZ - 1)]
    planes = [kap_ref[a, NZ - s] for a in range(3) for s in range(2)] + [rr_ref[place(NZ - 1)]]
    lane = iota((NY, NX), 1)
    columns = jnp.zeros((NY, NX), F32)
    for g, plane in enumerate(planes):
        columns = jnp.where(lane >= 4 * g, roll(plane, 4 * g + 2, 1), columns)
    lane = iota((8, NX), 1)
    folded = columns[:8]
    for i in range(1, NY // 8):
        folded = jnp.where(lane >= 32 * i, roll(columns[8 * i : 8 * i + 8], 32 * i, 1), folded)
    bulk_ref[BCOL:BROW] = folded
    bulk_ref[BROW:BULK] = jnp.zeros((16, NX), F32)
    for g, plane in enumerate(planes):
        a, beyond = divmod(g, 2)
        for inner in range(2) if g < 6 else (1,):
            at = BROW + (12 if g == 6 else 4 * a + 2 * inner + beyond)
            low = plane[0:1] if inner else plane[1:2]
            high = plane[NY - 1 : NY] if inner else plane[NY - 2 : NY - 1]
            bulk_ref[at : at + 1] = jnp.where(even, low, high)


def columns_kernel(kap_ref, rr_ref, left_ref, right_ref, ends_ref):
    lane = iota((NY, NX), 1)
    left = jnp.zeros((NY, NX), F32)
    right = jnp.zeros((NY, NX), F32)
    for a in range(3):
        for zp in range(NZ):
            at = 2 + a * KROWS + 2 * zp
            moved = roll(kap_ref[a, zp + 1], at, 1)
            left = jnp.where(lane >= at, moved, left)
            right = jnp.where(lane >= at - 2, moved, right)
    for zp in range(NZ):
        at = RLANE + zp
        moved = roll(rr_ref[place(zp)], at, 1)
        left = jnp.where(lane >= at, moved, left)
        right = jnp.where(lane >= at - 1, moved, right)
    left_ref[...] = left
    right_ref[...] = right
    row = iota((8, NX), 0)
    ends_ref[...] = end_tile(*(jnp.where(row < 4, v[:8], v[NY - 8 :]) for v in (left, right)))


def columns_beyond(left, right, moved):
    lane = iota(left.shape, 1)
    for a in range(3):
        for s in range(2):
            at = 2 + a * KROWS + 2 * (NZ + s)
            values = moved(2 * a + s, at)
            left = jnp.where((lane == at) | (lane == at + 1), values, left)
            right = jnp.where((lane == at - 2) | (lane == at - 1), values, right)
    at = RLANE + NZ
    values = moved(6, at)
    return jnp.where(lane == at, values, left), jnp.where(lane == at - 1, values, right)


def insert_rows(y_ref, far_ref, at):
    for i in range(6):
        y_ref[i * GROUP + NZ : (i + 1) * GROUP] = far_ref[at + 2 * i : at + 2 * i + 2]
    y_ref[RROW + NZ : RROW + NZ + 1] = far_ref[at + 12 : at + 13]


def columns_beyond_kernel(left_in, right_in, bulk_ref, yb_in, after_ref, left_ref, right_ref, yb_ref):
    folded = bulk_ref[BCOL:BROW]
    columns = jnp.concatenate([roll(folded, -32 * i, 1) for i in range(NY // 8)], axis=0)
    left_ref[...], right_ref[...] = columns_beyond(
        left_in[...], right_in[...], lambda g, x0: roll(columns, x0 - 4 * g - 2, 1)
    )
    insert_rows(yb_ref, bulk_ref, BROW)


def send_rows_kernel(far_ref, mine_ref, ends_ref, ya_in, after_ref, ya_ref, ub_ref):
    even = lax.axis_index("gy") % 2 == 0
    row, lane = iota((8, NX), 0), iota((8, NX), 1)
    insert_rows(ya_ref, far_ref, 16)
    is_right = ((row >> 1) & 1) == 1
    at = lane - jnp.where(is_right, 0, 2)
    within = at - jnp.where(at >= 2 * KROWS, 2 * KROWS, jnp.where(at >= KROWS, KROWS, 0))
    beyond = (at < RROW) & (within >= 2 * NZ)
    beyond = beyond | (lane == RLANE + NZ - is_right.astype(jnp.int32))
    tile = jnp.where(beyond, far_ref[8:16], ends_ref[...])
    turned = roll(tile, 4, 0)
    ya_ref[YPAY + 8 :] = jnp.where(even, turned, tile)
    ub_ref[8:16] = jnp.where(even, tile, turned)
    coarse = jnp.where(row < CY, mine_ref[0:8], far_ref[0:8])
    ya_ref[YPAY : YPAY + 8] = coarse
    ub_ref[0:8] = coarse


def columns_more_kernel(ra_ref, rb_ref, mine_ref, left_in, right_in, xa_ref, xb_ref, left_ref, right_ref, cor_ref):
    gx, gy = lax.axis_index("gx"), lax.axis_index("gy")
    even = gy % 2 == 0
    zero = jnp.zeros((URGENT, NX), F32)
    ra = ra_ref[YPAY:]
    hi = jnp.where(gy < lax.axis_size("gy") - 1, jnp.where(even, ra, rb_ref[...]), zero)
    lo = jnp.where(gy > 0, jnp.where(even, rb_ref[...], ra), zero)
    lane, row = iota((8, NX), 1), iota((8, NX), 0)

    def halo(shift):
        above, below = roll(hi[8:16], -shift, 0), roll(lo[8:16], 6 - shift, 0)
        return jnp.where(row < 2, above, jnp.where(row >= 6, below, 0.0))

    left_ref[0:NY] = left_in[...]
    right_ref[0:NY] = right_in[...]
    left_ref[NY : NY + 8] = halo(0)
    right_ref[NY : NY + 8] = halo(2)
    even_x = gx % 2 == 0
    xa_ref[0:40] = jnp.where(even_x, right_ref[...], left_ref[...])
    xb_ref[0:40] = jnp.where(even_x, left_ref[...], right_ref[...])

    tiles = [lo[0:8], mine_ref[0:8], hi[0:8]]
    zc, xs = lane >> 5, lane & 31
    pair = jnp.where(zc < 2, zc, 3 - zc)
    own = (xs >= 4) & (xs < 20)
    low_half, xs16 = lane < 64, iota((16, NX), 1) & 31
    sides = [jnp.zeros((16, NX), F32), jnp.zeros((16, NX), F32)]
    for q in range(4):
        at = (q * 2 + pair) * CX + jnp.clip(xs - 4, 0, CX - 1)
        below, mine, above = ((v, roll(v, 4, 0)) for v in (jnp.where(own, take(t, at), 0.0) for t in tiles))
        first = jnp.where(row < 4, jnp.where(low_half, below[0], below[1]), jnp.where(low_half, mine[1], mine[0]))
        second = jnp.where(row < 4, jnp.where(low_half, above[0], above[1]), 0.0)
        whole = jnp.concatenate([first, second], axis=0)
        cor_ref[q] = whole
        for i, start in enumerate((4, CX)):
            sides[i] = jnp.where((xs16 >= 4 * q) & (xs16 < 4 * q + 4), roll(whole, 4 * q - start, 1), sides[i])
    xa_ref[40:XPAY] = jnp.where(even_x, sides[1], sides[0])
    xb_ref[40:XPAY] = jnp.where(even_x, sides[0], sides[1])


def first_plane(to, zp, kap_ref, res, f_ref, p_ref, s1_ref, rim):
    below, k, above = ([kap_ref[a, zp + i] for a in range(3)] for i in range(3))
    part_0, part_y, part_x, part_yx = pair_stiffness(k, below, above)
    diag = SELF * (k[0] + k[1] + k[2]) + part_0 + both(part_y, 1, 0)
    inv = 1.0 / (diag + both(part_x + both(part_yx, 1, 0), 1, 1))
    f = jnp.where(rim, 0.0, WEIGHT_ONE * res * inv)
    f_ref[zp + 1] = f
    for a in range(3):
        p_ref[a, zp + 1] = k[a] * f
    if to < NZ if isinstance(to, int) else True:
        s1_ref[to] = WEIGHT_TWO * inv


def image_plane(to, zp, kap_ref, f_ref, p_ref, s1_ref, s2_ref, rim):
    k = [kap_ref[a, zp + 1] for a in range(3)]
    p = [p_ref[a, zp + 1] for a in range(3)]
    d0, d1, d2 = (p_ref[a, zp] + p_ref[a, zp + 2] for a in range(3))
    f, fz = f_ref[zp + 1], f_ref[zp] + f_ref[zp + 2]
    own_y = 0.5 * p[1] + 0.125 * (d0 + d1)
    own_yx = 0.125 * (p[1] + p[2]) + (1.0 / 24.0) * (d0 + d1 + d2)
    own_x = 0.5 * p[2] + 0.125 * (d0 + d2)
    fy, fyz = both(f, 1, 0), both(fz, 1, 0)
    t24, t8 = (1.0 / 24.0) * fyz, 0.125 * fyz
    total = 0.5 * d0 + both(own_y, 1, 0) + both(own_x + both(own_yx, 1, 0), 1, 1)
    total = total + k[0] * (0.5 * fz + t8 + both(0.125 * fz + t24, 1, 1))
    total = total + k[1] * (0.5 * fy + t8 + both(0.125 * fy + t24, 1, 1))
    total = total + k[2] * both(0.5 * f + 0.125 * (fz + fy) + t24, 1, 1)
    scaled = s1_ref[to]
    s1_ref[to] = jnp.where(rim, total, scaled)
    s2_ref[to] = jnp.where(rim, 0.0, KEEP * f + scaled * total)


def plane_rim():
    row, lane = iota((NY, NX), 0), iota((NY, NX), 1)
    return (row == 0) | (row == NY - 1) | (lane == 0) | (lane == NX - 1)


def inner_first_kernel(kap_ref, rr_ref, s1_ref, f_ref, p_ref):
    rim = plane_rim()
    f_ref[0] = jnp.zeros((NY, NX), F32)
    p_ref[:, 0] = jnp.zeros((3, NY, NX), F32)

    @pl.loop(0, 3)
    def _(i):
        for j in range(5):
            zp = i * 5 + j
            first_plane(zp, zp, kap_ref, rr_ref[place(zp)], f_ref, p_ref, s1_ref, rim)


def inner_image_kernel(kap_ref, f_ref, p_ref, s1_in, after_ref, s1_ref, s2_ref):
    rim = plane_rim()

    @pl.loop(0, 2)
    def _(i):
        for j in range(7):
            image_plane(i * 7 + j, i * 7 + j, kap_ref, f_ref, p_ref, s1_ref, s2_ref, rim)


def outer_kernel(kap_ref, rr_ref, bulk_ref, f_in, p_in, s1_in, s2_in, s1_ref, s2_ref, k_ref, f_ref, p_ref):
    rim = plane_rim()
    for a in range(3):
        for i in range(3):
            k_ref[a, i] = kap_ref[a, NZ - 2 + i]
        for i in range(2):
            k_ref[a, 3 + i] = bulk_ref[(2 * a + i) * NY : (2 * a + i + 1) * NY]
            p_ref[a, i] = p_in[a, NZ - 2 + i]
    for i in range(2):
        f_ref[i] = f_in[NZ - 2 + i]
    first_plane(NZ - 1, 1, k_ref, rr_ref[place(NZ - 1)], f_ref, p_ref, s1_ref, rim)
    first_plane(NZ, 2, k_ref, bulk_ref[6 * NY : 7 * NY], f_ref, p_ref, s1_ref, rim)
    for i in range(2):
        image_plane(NZ - 2 + i, i, k_ref, f_ref, p_ref, s1_ref, s2_ref, rim)


def along_x(values):
    return both(values, 1, 1)


def edge_rows_kernel(ya_ref, yb_ref, ra_ref, rb_ref, s1_in, s2_in, s1_ref, s2_ref):
    even = lax.axis_index("gy") % 2 == 0
    size = 24
    row, lane = iota((size, NX), 0), iota((size, NX), 1)
    inner = (lane > 0) & (lane < NX - 1)
    near = inner & (row < NZ + 1)
    inner16 = inner[:NZ]
    gy = lax.axis_index("gy")
    zero = jnp.zeros((YPAY, NX), F32)
    ya, yb, ra, rb = ya_ref[0:YPAY], yb_ref[...], ra_ref[0:YPAY], rb_ref[...]
    hi = jnp.where(gy < lax.axis_size("gy") - 1, jnp.where(even, ra, rb), zero)
    lo = jnp.where(gy > 0, jnp.where(even, rb, ra), zero)
    for other, mine, face, second in (
        (lo, jnp.where(even, yb, ya), 0, 1),
        (hi, jnp.where(even, ya, yb), NY - 1, NY - 2),
    ):

        def group(source, at):
            return jnp.where(row < GROUP, source[at : at + size], 0.0)

        k = [[group(other, a * KROWS + s * GROUP) for a in range(3)] for s in (0, 1)]
        k += [[group(mine, a * KROWS + s * GROUP) for a in range(3)] for s in (1, 0)]
        parts = [pair_stiffness(v, (None, None, None), [both(u, 1, 0) for u in v]) for v in k]
        res = [None] + [jnp.where(row < NZ + 1, v[YPAY - size :], 0.0) for v in (roll(other, 4 - 8, 0), roll(mine, 4 - 8, 0))]
        f, inv = [None] * 3, [None] * 3
        for c in (1, 2):
            diag = SELF * (k[c][0] + k[c][1] + k[c][2]) + parts[c][0] + parts[c - 1][1] + parts[c + 1][1]
            inv[c] = 1.0 / (diag + along_x(parts[c][2] + parts[c - 1][3] + parts[c + 1][3]))
            f[c] = jnp.where(near, WEIGHT_ONE * res[c] * inv[c], 0.0)
        p = [None] + [[v * f[c] for v in k[c]] for c in (1, 2)]
        d = [None] + [[both(v, 1, 0) for v in p[c]] for c in (1, 2)]
        fz = [None] + [both(f[c], 1, 0) for c in (1, 2)]

        def row_parts(c):
            return (
                0.5 * p[c][1] + 0.125 * (d[c][0] + d[c][1]),
                0.125 * (p[c][1] + p[c][2]) + (1.0 / 24.0) * (d[c][0] + d[c][1] + d[c][2]),
            )

        own_y, own_yx = row_parts(1)
        own_x = 0.5 * p[2][2] + 0.125 * (d[2][0] + d[2][2])
        t24, t8 = (1.0 / 24.0) * fz[1], 0.125 * fz[1]
        total = 0.5 * d[2][0] + own_y + along_x(own_x + own_yx)
        total = total + k[2][0] * (0.5 * fz[2] + t8 + along_x(0.125 * fz[2] + t24))
        total = total + k[2][1] * (0.5 * f[1] + t8 + along_x(0.125 * f[1] + t24))
        total = total + k[2][2] * along_x(0.5 * f[2] + 0.125 * (fz[2] + f[1]) + t24)
        total = total[:NZ] + s1_ref[:, face, :]
        scaled = WEIGHT_TWO * inv[2][:NZ]
        s1_ref[:, face, :] = jnp.where(inner16, scaled, total)
        s2_ref[:, face, :] = jnp.where(inner16, KEEP * f[2][:NZ] + scaled * total, 0.0)

        own_y, own_yx = row_parts(2)
        t24, t8 = (1.0 / 24.0) * fz[2], 0.125 * fz[2]
        total = own_y + along_x(own_yx) + k[3][0] * (t8 + along_x(t24))
        total = total + k[3][1] * (0.5 * f[2] + t8 + along_x(0.125 * f[2] + t24))
        total = (total + k[3][2] * along_x(0.125 * f[2] + t24))[:NZ]
        scaled = s1_ref[:, second, :]
        s1_ref[:, second, :] = jnp.where(inner16, scaled, scaled + total)
        s2_ref[:, second, :] = s2_ref[:, second, :] + jnp.where(inner16, scaled * total, 0.0)


def slab_lanes(left):
    lane = iota((8, NX), 1)
    zp, c = lane >> 2, lane & 3
    outer = c < 2 if left else c >= 2
    real = zp < GROUP
    near = ((c == 1) | (c == 2)) & (zp < NZ + 1)
    offset = jnp.where(outer, 0, 2) if left else jnp.where(outer, 2, 0)
    offset_r = jnp.where(outer, RLANE - 1, RLANE) if left else jnp.where(outer, RLANE, RLANE - 1)
    sources = [jnp.where(real, a * KROWS + 2 * zp + (c & 1) + offset, 0) for a in range(3)]
    sources.append(jnp.where(near, zp + offset_r, 0))
    return outer, [real] * 3 + [near], sources


def slab_kernel(left_ref, right_ref, after_ref, slab_ref):
    for side, pack in enumerate((left_ref, right_ref)):
        outer, keeps, sources = slab_lanes(side == 0)
        for q in range(4):
            for i in range(0, NY + 8, 8):
                piece = take(pack[i : i + 8], sources[q])
                slab_ref[side, q, i : i + 8] = jnp.where(keeps[q] & ~outer, piece, 0.0)


def rim_kernel(s1_ref, s2_ref, rim1_ref, rim2_ref):
    lane = iota((NY, NX), 1)
    for source, rim in ((s1_ref, rim1_ref), (s2_ref, rim2_ref)):
        values = jnp.zeros((NY, NX), F32)
        for zp in range(NZ):
            values = jnp.where(lane >= 4 * zp, roll(source[zp], 4 * zp + 2, 1), values)
        rim[...] = values


def slab_terms(mine, other, rim1, rim2, left):
    rows = NY + 8
    outer, keeps, sources = slab_lanes(left)

    def spread(q):
        pieces = []
        for i in range(0, rows, 8):
            pieces.append(jnp.where(keeps[q] & outer, take(other[i : i + 8], sources[q]), mine[q, i : i + 8]))
        return jnp.concatenate(pieces, axis=0)

    k = [spread(a) for a in range(3)]
    res = spread(3)
    c = iota((rows, NX), 1) & 3
    near = jnp.concatenate([keeps[3]] * (rows // 8), axis=0)

    dz = [both(v, 4, 1) for v in k]
    part_0, part_y, part_x, part_yx = pair_stiffness(k, (None, None, None), dz)
    diag = SELF * (k[0] + k[1] + k[2]) + part_0 + both(part_y, 1, 0)
    inv = 1.0 / (diag + both(part_x + both(part_yx, 1, 0), 1, 1))
    f = jnp.where(near, WEIGHT_ONE * res * inv, 0.0)

    def from_outer(values):
        return roll(values, 1 if left else -1, 1)

    p = [v * f for v in k]
    d0, d1, d2 = (both(v, 4, 1) for v in p)
    own_y = 0.5 * p[1] + 0.125 * (d0 + d1)
    own_yx = 0.125 * (p[1] + p[2]) + (1.0 / 24.0) * (d0 + d1 + d2)
    own_x = 0.5 * p[2] + 0.125 * (d0 + d2)
    fz = both(f, 4, 1)
    fy, fyz = both(f, 1, 0)[:NY], both(fz, 1, 0)[:NY]
    fc, fz = f[:NY], fz[:NY]
    k = [v[:NY] for v in k]
    t24, t8 = (1.0 / 24.0) * fyz, 0.125 * fyz
    total = 0.5 * d0[:NY] + both(own_y, 1, 0)[:NY] + from_outer(own_x[:NY] + both(own_yx, 1, 0)[:NY])
    total = total + k[0] * (0.5 * fz + t8 + from_outer(0.125 * fz + t24))
    total = total + k[1] * (0.5 * fy + t8 + from_outer(0.125 * fy + t24))
    total = total + k[2] * from_outer(0.5 * fc + 0.125 * (fz + fy) + t24)
    face = (c == 2 if left else c == 1)[:NY]
    return jnp.where(face, KEEP * fc + WEIGHT_TWO * inv[:NY] * (total + rim1), rim2 + rim1 * total)


def coarse_solve(cor_ref, lower, upper):
    xs = iota((16, NX), 1) & 31
    arrays = []
    for q in range(4):
        whole = jnp.where(xs < 4, roll(lower, -4 * q, 1), cor_ref[q])
        arrays.append(jnp.where((xs >= 20) & (xs < 24), roll(upper, 20 - 4 * q, 1), whole))
    kc, rhs = arrays[:3], arrays[3]
    lane = iota((16, NX), 1)

    def sides(values, axis):
        if axis == 0:
            return roll(values, 32, 1), roll(values, -32, 1)
        return roll(values, 1, axis - 1), roll(values, -1, axis - 1)

    within = [(lane >= 32, lane < 96), (None, None), (None, None)]
    diag = (1.0 + MASS / 3.0) * (kc[0] + kc[1] + kc[2])
    couple = []
    for a in range(3):
        for v, real in zip(sides(kc[a], a), within[a]):
            half = 0.5 * v if real is None else jnp.where(real, 0.5 * v, 0.0)
            diag = diag + half
            half = 0.5 * kc[a] + half
            couple.append(half if real is None else jnp.where(real, half, 0.0))
    inside = kc[0] > 0.0
    scaled = jnp.where(inside, OMEGA / jnp.where(inside, diag, 1.0), 0.0)
    couple = [scaled * v for v in couple]
    start = scaled * rhs
    estimate = start
    for _ in range(CITERS - 1):
        t = [v * u for v, u in zip(couple, [u for a in range(3) for u in sides(estimate, a)])]
        estimate = (start + (1.0 - OMEGA) * estimate) + (((t[0] + t[1]) + (t[2] + t[3])) + (t[4] + t[5]))
    return estimate[0:8]


def last_kernel(
    rb_ref, ra_ref, slab_ref, cor_ref, rim1_ref, rim2_ref, s2_ref, sel_ref, out_hbm, est_hbm, out_ref, est_ref, sems
):
    gx, gz = lax.axis_index("gx"), lax.axis_index("gz")
    even = gx % 2 == 0
    zero = jnp.zeros((XPAY, NX), F32)
    right = jnp.where(gx < lax.axis_size("gx") - 1, jnp.where(even, ra_ref[...], rb_ref[...]), zero)
    left = jnp.where(gx > 0, jnp.where(even, rb_ref[...], ra_ref[...]), zero)
    rim1, rim2 = rim1_ref[...], rim2_ref[...]
    from_left = slab_terms(slab_ref[0], left[:40], rim1, rim2, True)
    from_right = slab_terms(slab_ref[1], right[:40], rim1, rim2, False)
    lane = iota((NY, NX), 1)
    faces = jnp.where((lane & 3) < 2, from_right, from_left)

    estimate = coarse_solve(cor_ref, left[40:XPAY], right[40:XPAY])
    lane8 = iota((8, NX), 1)
    rim = (lane < 2) | (lane >= NX - 2)
    step = 4
    for zc in range(CZ):
        z_out = jnp.where(gz == 0, zc, CZ - 1 - zc)
        est_ref[z_out] = roll(estimate, -(zc * 32 + 4), 1)[4:8, 0:CX]
    copies = [pltpu.make_async_copy(est_ref, est_hbm, sems.at[NZ // step])]
    copies[0].start()
    for zc in range(CZ):
        wide = take(estimate, zc * 32 + 4 + (lane8 >> 3))
        fine = jnp.concatenate([jnp.broadcast_to(wide[4 + y : 5 + y], (BLK, NX)) for y in range(CY)], axis=0)
        for i in range(BLK):
            zp = zc * BLK + i
            z = jnp.where(gz == 0, zp, NZ - 1 - zp)
            out_ref[z] = jnp.where(rim, roll(faces, -(4 * zp + 2), 1), s2_ref[zp]) + sel_ref[z] * fine
            if zp % step == step - 1:
                planes = pl.ds(jnp.where(gz == 0, zp + 1 - step, NZ - 1 - zp), step)
                copies.append(pltpu.make_async_copy(out_ref.at[planes], out_hbm.at[planes], sems.at[zp // step]))
                copies[-1].start()
    for copy in copies:
        copy.wait()


def near(values):
    return pltpu.with_memory_space_constraint(values, pltpu.VMEM)


def call(kernel, inputs, outputs, scratch=(), aliases=None, us=0.1, name=None, in_space=pltpu.VMEM, out_spaces=None):
    return pl.pallas_call(
        kernel,
        out_shape=outputs,
        in_specs=[pl.BlockSpec(memory_space=in_space)] * len(inputs),
        out_specs=[pl.BlockSpec(memory_space=v) for v in out_spaces or [pltpu.VMEM] * len(outputs)],
        scratch_shapes=list(scratch),
        input_output_aliases=aliases or {},
        cost_estimate=pl.CostEstimate(flops=int(us * 1e9), bytes_accessed=0, transcendentals=0),
        compiler_params=pltpu.CompilerParams(vmem_limit_bytes=32 * 2**20),
        name=name,
    )(*inputs)


def vmem(*shape):
    return pltpu.VMEM(shape, F32)


def exchange(values, sizes, move):
    nx, ny, nz = sizes
    pairs = []
    for x in range(nx):
        for y in range(ny):
            for z in range(nz):
                a, b, c = move(x, y, z)
                pairs.append(((x * ny + y) * nz + z, (a * ny + b) * nz + c))
    return lax.ppermute(values, ("gx", "gy", "gz"), pairs)


def solution(mesh):
    sizes = (mesh.shape["gx"], mesh.shape["gy"], mesh.shape["gz"])
    nx, ny, nz = sizes

    def swap_z(values):
        return exchange(values, sizes, lambda x, y, z: (x, y, nz - 1 - z))

    def swap_y(values, odd):
        def move(x, y, z):
            b = y + 1 if y % 2 == odd else y - 1
            return (x, b, z) if 0 <= b < ny else (x ^ 1, y, z)

        return exchange(values, sizes, move)

    def swap_x(values, odd):
        return exchange(values, sizes, lambda x, y, z: ((x + 1 if x % 2 == odd else x - 1) % nx, y, z))

    def body(residual_in, labels, factor, basis, basis_index):
        inputs = [residual_in, labels, factor, basis, basis_index]
        kap, rr, sel, urgent = call(
            first_kernel,
            [pltpu.with_memory_space_constraint(v, pltpu.HBM) for v in inputs],
            [vmem(3, NZ + 1, NY, NX), vmem(NZ, NY, NX), vmem(NZ, NY, NX), vmem(ZURGENT, NX)],
            [
                pltpu.VMEM(labels.shape, jnp.int32),
                pltpu.VMEM(factor.shape, F32),
                pltpu.VMEM(basis.shape, F32),
                pltpu.VMEM(basis_index.shape, jnp.int32),
                pltpu.VMEM((4, BLK, BLK, NX), F32),
                pltpu.VMEM((64, NX), F32),
                pltpu.SemaphoreType.DMA((2,)),
                pltpu.SemaphoreType.DMA((len(PARTS), 3)),
            ],
            us=1.8,
            name="stiffness",
            in_space=pltpu.HBM,
        )
        kap, rr, sel, urgent = near(kap), near(rr), near(sel), near(urgent)
        zu = near(swap_z(urgent))
        ya, yb, bulk = call(rows_kernel, [kap, rr], [vmem(YPAY + URGENT, NX), vmem(YPAY, NX), vmem(BULK, NX)], name="rows")
        zb = near(swap_z(near(bulk)))
        left, right, ends = call(
            columns_kernel, [kap, rr], [vmem(NY, NX), vmem(NY, NX), vmem(8, NX)], us=0.4, name="columns"
        )
        s1, f, p = call(
            inner_first_kernel,
            [kap, rr],
            [vmem(NZ, NY, NX), vmem(NZ, NY, NX), vmem(3, NZ, NY, NX)],
            us=0.6,
            name="inner_first",
        )
        s1, f, p = near(s1), near(f), near(p)
        ya, ub = call(
            send_rows_kernel,
            [zu, urgent, near(ends), near(ya), f],
            [vmem(YPAY + URGENT, NX), vmem(URGENT, NX)],
            aliases={3: 0},
            us=10.0,
            name="send_rows",
        )
        ya, ub = near(ya), near(ub)
        wa, rb = near(swap_y(ya, 0)), near(swap_y(ub, 1))
        left, right, yb = call(
            columns_beyond_kernel,
            [near(left), near(right), zb, near(yb), ub],
            [vmem(NY, NX), vmem(NY, NX), vmem(YPAY, NX)],
            aliases={0: 0, 1: 1, 3: 2},
            us=100.0,
            name="columns_beyond",
        )
        yb = near(yb)
        wb = near(swap_y(yb, 1))
        xa, xb, left, right, cor = call(
            columns_more_kernel,
            [wa, rb, ub, near(left), near(right)],
            [vmem(XPAY, NX), vmem(XPAY, NX), vmem(40, NX), vmem(40, NX), vmem(4, 16, NX)],
            us=1.0,
            name="columns_more",
        )
        xa, xb = near(xa), near(xb)
        vb, va = near(swap_x(xb, 1)), near(swap_x(xa, 0))
        s1, s2 = call(
            inner_image_kernel,
            [kap, f, p, s1, xa],
            [vmem(NZ, NY, NX), vmem(NZ, NY, NX)],
            aliases={3: 0},
            us=0.6,
            name="inner_image",
        )
        s1, s2 = call(
            outer_kernel,
            [kap, rr, zb, f, p, near(s1), near(s2)],
            [vmem(NZ, NY, NX), vmem(NZ, NY, NX)],
            [pltpu.VMEM((3, 5, NY, NX), F32), pltpu.VMEM((4, NY, NX), F32), pltpu.VMEM((3, 4, NY, NX), F32)],
            aliases={5: 0, 6: 1},
            us=0.25,
            name="outer",
        )
        s1, s2 = call(
            edge_rows_kernel,
            [ya, yb, wa, wb, near(s1), near(s2)],
            [vmem(NZ, NY, NX), vmem(NZ, NY, NX)],
            aliases={4: 0, 5: 1},
            us=0.4,
            name="edge_rows",
        )
        (slab,) = call(slab_kernel, [near(left), near(right), xa], [vmem(2, 4, 40, NX)], us=0.1, name="slab")
        rim1, rim2 = call(rim_kernel, [near(s1), near(s2)], [vmem(NY, NX), vmem(NY, NX)], us=0.2, name="rim")
        out, estimate = call(
            last_kernel,
            [vb, va, near(slab), near(cor), near(rim1), near(rim2), near(s2), sel],
            [jax.ShapeDtypeStruct((NZ, NY, NX), F32), jax.ShapeDtypeStruct((CZ, CY, CX), F32)],
            [pltpu.VMEM((NZ, NY, NX), F32), pltpu.VMEM((CZ, CY, CX), F32), pltpu.SemaphoreType.DMA((5,))],
            us=1.5,
            name="last",
            out_spaces=[pltpu.HBM, pltpu.HBM],
        )
        return out, estimate

    in_specs = (
        P("gz", "gy", "gx"),
        P("gz", "gy", "gx"),
        P(None, "gz", "gy", "gx"),
        P(),
        P("gz", "gy", "gx"),
    )
    out_specs = (P("gz", "gy", "gx"), P("gz", "gy", "gx"))
    return jax.shard_map(body, mesh=mesh, in_specs=in_specs, out_specs=out_specs, check_vma=False)
```

```python
import math

import jax
import jax.numpy as jnp
from jax import lax
from jax.experimental import pallas as pl
from jax.experimental.pallas import tpu as pltpu
from jax.sharding import PartitionSpec as P

BLK = 8
CITERS = 4
BRICK = (0.6, 1.0, 1.0)
MORTAR = (0.25, 0.3, 0.3)
MASS = 0.05
OMEGA = 0.8
WEIGHT_ONE = 1.0 / (1.05 - 0.95 * math.cos(math.pi / 4))
WEIGHT_TWO = 1.0 / (1.05 + 0.95 * math.cos(math.pi / 4))
SELF = 1.0 + 1.0 + 1.0 / 3.0 + MASS / 3.0
KEEP = 1.0 + WEIGHT_TWO / WEIGHT_ONE - WEIGHT_TWO

NZ, NY, NX = 16, 32, 128
CZ, CY, CX = 2, 4, 16
PARTS = range(2)
F32 = jnp.float32
HIGHEST = lax.Precision.HIGHEST

BULK = 7 * NY + 8
BCOL = 7 * NY
URGENT = 16
ZURGENT = 48
KROWS = 36
GROUP = NZ + 2
RROW = 3 * KROWS
YPAY = 128
XPAY = 40 + 16
RLANE = 110


def iota(shape, dim):
    return lax.broadcasted_iota(jnp.int32, shape, dim)


def roll(values, shift, axis):
    size = values.shape[axis]
    shift = shift % size
    return values if shift == 0 else pltpu.roll(values, shift, axis)


def both(values, step, axis):
    return roll(values, step, axis) + roll(values, -step, axis)


def take(values, lanes):
    return jnp.take_along_axis(values, lanes, axis=1, mode="promise_in_bounds")


def pair_stiffness(own, below, above):
    k0, k1, k2 = own
    d0, d1, d2 = (a + b if a is not None else b for a, b in zip(below, above))
    part_y = 0.5 * k1 + 0.125 * (d0 + d1)
    part_yx = 0.125 * (k1 + k2) + (1.0 / 24.0) * (d0 + d1 + d2)
    part_0 = 0.5 * d0
    part_x = 0.5 * k2 + 0.125 * (d0 + d2)
    return part_0, part_y, part_x, part_yx


def first_kernel(
    r_hbm, lab_hbm, fac_hbm, bas_hbm, bix_hbm, kap_ref, rr_ref, sel_ref, urgent_ref,
    lab_ref, fac_ref, bas_ref, bix_ref, tile_ref, sum_ref, sems, more_sems
):
    gz = lax.axis_index("gz")
    parts = []
    small = [
        pltpu.make_async_copy(bas_hbm, bas_ref, sems.at[0]),
        pltpu.make_async_copy(bix_hbm, bix_ref, sems.at[1]),
    ]
    for copy in small:
        copy.start()
    step = NZ // len(PARTS)
    for part in PARTS:
        planes = pl.ds(jnp.where(gz == 0, part * step, NZ - step - part * step), step)
        parts.append(
            [
                pltpu.make_async_copy(lab_hbm.at[planes], lab_ref.at[planes], more_sems.at[part, 0]),
                pltpu.make_async_copy(fac_hbm.at[:, planes], fac_ref.at[:, planes], more_sems.at[part, 1]),
                pltpu.make_async_copy(r_hbm.at[planes], rr_ref.at[planes], more_sems.at[part, 2]),
            ]
        )
        for copy in parts[part]:
            copy.start()
    kap_ref[:, 0] = jnp.zeros((3, NY, NX), F32)
    for copy in small:
        copy.wait()
    tiled = lax.dot_general(
        bas_ref[...].reshape(4 * BLK * BLK, BLK),
        ((iota((BLK, NX), 1) & (BLK - 1)) == iota((BLK, NX), 0)).astype(F32),
        (((1,), (0,)), ((), ())),
        precision=HIGHEST,
        preferred_element_type=F32,
    )
    tile_ref[...] = tiled.reshape(4, BLK, BLK, NX)
    edges = [None] * 7
    spread = ((iota((CX, NX), 1) >> 3) == iota((CX, NX), 0)).astype(F32)
    indices = []
    for zc in range(CZ):
        index = lax.dot_general(
            bix_ref[jnp.where(gz == 0, zc, CZ - 1 - zc)].astype(F32),
            spread,
            (((1,), (0,)), ((), ())),
            precision=HIGHEST,
            preferred_element_type=F32,
        )
        indices.append(jnp.concatenate([jnp.broadcast_to(index[y : y + 1], (BLK, NX)) for y in range(CY)], axis=0))
    for zc in range(CZ):
        index = indices[zc]
        sums = [None] * 4
        for i in range(BLK):
            zp = zc * BLK + i
            if zp % step == 0:
                for copy in parts[zp // step]:
                    copy.wait()
            z = jnp.where(gz == 0, zp, NZ - 1 - zp)
            zi = jnp.where(gz == 0, i, BLK - 1 - i)
            mortar = lab_ref[z] == 1
            b0, b1, b2, b3 = (jnp.concatenate([tile_ref[n, zi]] * CY, axis=0) for n in range(4))
            basis = jnp.where(index < 1.5, jnp.where(index < 0.5, b0, b1), jnp.where(index < 2.5, b2, b3))
            res = rr_ref[z]
            sel_ref[z] = basis
            terms = []
            for a in range(3):
                k = jnp.where(mortar, MORTAR[a], BRICK[a]) * fac_ref[a, z]
                kap_ref[a, zp + 1] = k
                terms.append(k)
                if zp >= NZ - 2:
                    plane = 2 * a + NZ - 1 - zp
                    edges[plane] = k
            if zp == NZ - 1:
                edges[6] = res
            terms.append(basis * res)
            sums = [t if s is None else s + t for s, t in zip(sums, terms)]
        for q in range(4):
            total = sums[q].reshape(CY, BLK, NX).sum(axis=1)
            total = total if q == 3 else total * (1.0 / BLK**3)
            at = (q * 2 + zc) * 8
            sum_ref[at : at + CY] = total
            sum_ref[at + CY : at + 8] = total
    gather = ((iota((NX, NX), 0) >> 3) == (iota((NX, NX), 1) & (CX - 1))).astype(jnp.bfloat16)
    rest, bricks = sum_ref[...], None
    for _ in range(3):
        part = rest.astype(jnp.bfloat16)
        rest = rest - part.astype(F32)
        term = lax.dot_general(part, gather, (((1,), (0,)), ((), ())), preferred_element_type=F32)
        bricks = term if bricks is None else bricks + term
    group = iota((8, NX), 1) >> 4
    coarse = bricks[0:8]
    for g in range(1, 8):
        coarse = jnp.where(group == g, bricks[g * 8 : g * 8 + 8], coarse)
    urgent_ref[0:8] = coarse
    row = iota((8, NX), 0)

    def ends(plane):
        return jnp.where(row < 4, plane[:8], plane[NY - 8 :])

    left, right = columns_beyond(
        jnp.zeros((8, NX), F32), jnp.zeros((8, NX), F32), lambda g, x0: roll(ends(edges[g]), x0, 1)
    )
    urgent_ref[8:16] = end_tile(left, right)
    for g, plane in enumerate(edges):
        a, beyond = divmod(g, 2)
        for inner in range(2) if g < 6 else (1,):
            at = 12 if g == 6 else 4 * a + 2 * inner + beyond
            urgent_ref[16 + at : 17 + at] = plane[0:1] if inner else plane[1:2]
            urgent_ref[32 + at : 33 + at] = plane[NY - 1 : NY] if inner else plane[NY - 2 : NY - 1]


def end_tile(left, right):
    row = iota((8, NX), 0)
    low = jnp.where(row < 2, left, roll(right, 2, 0))
    high = jnp.where(row < 6, roll(left, -2, 0), right)
    return jnp.where(row < 4, low, high)


def place(zp):
    return jnp.where(lax.axis_index("gz") == 0, zp, NZ - 1 - zp)


def rows_kernel(kap_ref, rr_ref, y0_ref, y1_ref, y2_ref, bulk_ref):
    phase = lax.rem(lax.axis_index("gy"), 3)

    def put(at, low, high):
        for slot, ref in enumerate((y0_ref, y1_ref, y2_ref)):
            ref[at : at + 1] = jnp.where(phase == slot, high, low)

    for zp in range(NZ):
        for a in range(3):
            at = a * KROWS + zp
            put(at, kap_ref[a, zp + 1, 1:2], kap_ref[a, zp + 1, NY - 2 : NY - 1])
            put(at + GROUP, kap_ref[a, zp + 1, 0:1], kap_ref[a, zp + 1, NY - 1 : NY])
        put(RROW + zp, rr_ref[place(zp), 0:1], rr_ref[place(zp), NY - 1 : NY])
    for a in range(3):
        for s in range(2):
            bulk_ref[(2 * a + s) * NY : (2 * a + s + 1) * NY] = kap_ref[a, NZ - s]
    bulk_ref[6 * NY : 7 * NY] = rr_ref[place(NZ - 1)]
    planes = [kap_ref[a, NZ - s] for a in range(3) for s in range(2)] + [rr_ref[place(NZ - 1)]]
    lane = iota((NY, NX), 1)
    columns = jnp.zeros((NY, NX), F32)
    for g, plane in enumerate(planes):
        columns = jnp.where(lane >= 4 * g, roll(plane, 4 * g + 2, 1), columns)
    lane = iota((8, NX), 1)
    folded = columns[:8]
    for i in range(1, NY // 8):
        folded = jnp.where(lane >= 32 * i, roll(columns[8 * i : 8 * i + 8], 32 * i, 1), folded)
    bulk_ref[BCOL:BULK] = folded


def columns_kernel(kap_ref, rr_ref, left_ref, right_ref, ends_ref):
    lane = iota((NY, NX), 1)
    left = jnp.zeros((NY, NX), F32)
    right = jnp.zeros((NY, NX), F32)
    for a in range(3):
        for zp in range(NZ):
            at = 2 + a * KROWS + 2 * zp
            moved = roll(kap_ref[a, zp + 1], at, 1)
            left = jnp.where(lane >= at, moved, left)
            right = jnp.where(lane >= at - 2, moved, right)
    for zp in range(NZ):
        at = RLANE + zp
        moved = roll(rr_ref[place(zp)], at, 1)
        left = jnp.where(lane >= at, moved, left)
        right = jnp.where(lane >= at - 1, moved, right)
    left_ref[...] = left
    right_ref[...] = right
    row = iota((8, NX), 0)
    ends_ref[...] = end_tile(*(jnp.where(row < 4, v[:8], v[NY - 8 :]) for v in (left, right)))


def columns_beyond(left, right, moved):
    lane = iota(left.shape, 1)
    for a in range(3):
        for s in range(2):
            at = 2 + a * KROWS + 2 * (NZ + s)
            values = moved(2 * a + s, at)
            left = jnp.where((lane == at) | (lane == at + 1), values, left)
            right = jnp.where((lane == at - 2) | (lane == at - 1), values, right)
    at = RLANE + NZ
    values = moved(6, at)
    return jnp.where(lane == at, values, left), jnp.where(lane == at - 1, values, right)


def columns_beyond_kernel(left_in, right_in, bulk_ref, after_ref, left_ref, right_ref):
    folded = bulk_ref[BCOL:BULK]
    columns = jnp.concatenate([roll(folded, -32 * i, 1) for i in range(NY // 8)], axis=0)
    left_ref[...], right_ref[...] = columns_beyond(
        left_in[...], right_in[...], lambda g, x0: roll(columns, x0 - 4 * g - 2, 1)
    )


def send_rows_kernel(far_ref, mine_ref, ends_ref, y0_in, y1_in, y2_in, after_ref, y0_ref, y1_ref, y2_ref, u2_ref):
    phase = lax.rem(lax.axis_index("gy"), 3)
    row, lane = iota((8, NX), 0), iota((8, NX), 1)
    low, high = far_ref[16:32], far_ref[32:48]
    for slot, ref in enumerate((y0_ref, y1_ref, y2_ref)):
        rows = jnp.where(phase == slot, high, low)
        for i in range(6):
            ref[i * GROUP + NZ : (i + 1) * GROUP] = rows[2 * i : 2 * i + 2]
        ref[RROW + NZ : RROW + NZ + 1] = rows[12:13]
    is_right = ((row >> 1) & 1) == 1
    at = lane - jnp.where(is_right, 0, 2)
    within = at - jnp.where(at >= 2 * KROWS, 2 * KROWS, jnp.where(at >= KROWS, KROWS, 0))
    beyond = (at < RROW) & (within >= 2 * NZ)
    beyond = beyond | (lane == RLANE + NZ - is_right.astype(jnp.int32))
    tile = jnp.where(beyond, far_ref[8:16], ends_ref[...])
    turned = roll(tile, 4, 0)
    coarse = jnp.where(row < CY, mine_ref[0:8], far_ref[0:8])
    for slot, (ref, at) in enumerate(((y0_ref, YPAY), (y1_ref, YPAY), (u2_ref, 0))):
        ref[at : at + 8] = coarse
        ref[at + 8 : at + 16] = jnp.where(phase == slot, turned, tile)


def neighbours(slots):
    gy = lax.axis_index("gy")
    phase = lax.rem(gy, 3)
    zero = jnp.zeros(slots[0].shape, F32)
    hi = jnp.where(phase == 0, slots[0], jnp.where(phase == 1, slots[1], slots[2]))
    lo = jnp.where(phase == 0, slots[2], jnp.where(phase == 1, slots[0], slots[1]))
    return jnp.where(gy > 0, lo, zero), jnp.where(gy < lax.axis_size("gy") - 1, hi, zero)


def columns_more_kernel(r0_ref, r1_ref, r2_ref, mine_ref, left_in, right_in, xa_ref, xb_ref, left_ref, right_ref, cor_ref):
    gx = lax.axis_index("gx")
    lo, hi = neighbours([r0_ref[YPAY:], r1_ref[YPAY:], r2_ref[...]])
    lane, row = iota((8, NX), 1), iota((8, NX), 0)

    def halo(shift):
        above, below = roll(hi[8:16], -shift, 0), roll(lo[8:16], 6 - shift, 0)
        return jnp.where(row < 2, above, jnp.where(row >= 6, below, 0.0))

    left_ref[0:NY] = left_in[...]
    right_ref[0:NY] = right_in[...]
    left_ref[NY : NY + 8] = halo(0)
    right_ref[NY : NY + 8] = halo(2)
    even_x = gx % 2 == 0
    xa_ref[0:40] = jnp.where(even_x, right_ref[...], left_ref[...])
    xb_ref[0:40] = jnp.where(even_x, left_ref[...], right_ref[...])

    tiles = [lo[0:8], mine_ref[0:8], hi[0:8]]
    zc, xs = lane >> 5, lane & 31
    pair = jnp.where(zc < 2, zc, 3 - zc)
    own = (xs >= 4) & (xs < 20)
    low_half, xs16 = lane < 64, iota((16, NX), 1) & 31
    sides = [jnp.zeros((16, NX), F32), jnp.zeros((16, NX), F32)]
    for q in range(4):
        at = (q * 2 + pair) * CX + jnp.clip(xs - 4, 0, CX - 1)
        below, mine, above = ((v, roll(v, 4, 0)) for v in (jnp.where(own, take(t, at), 0.0) for t in tiles))
        first = jnp.where(row < 4, jnp.where(low_half, below[0], below[1]), jnp.where(low_half, mine[1], mine[0]))
        second = jnp.where(row < 4, jnp.where(low_half, above[0], above[1]), 0.0)
        whole = jnp.concatenate([first, second], axis=0)
        cor_ref[q] = whole
        for i, start in enumerate((4, CX)):
            sides[i] = jnp.where((xs16 >= 4 * q) & (xs16 < 4 * q + 4), roll(whole, 4 * q - start, 1), sides[i])
    xa_ref[40:XPAY] = jnp.where(even_x, sides[1], sides[0])
    xb_ref[40:XPAY] = jnp.where(even_x, sides[0], sides[1])


def first_plane(to, zp, kap_ref, res, f_ref, p_ref, s1_ref, rim):
    below, k, above = ([kap_ref[a, zp + i] for a in range(3)] for i in range(3))
    part_0, part_y, part_x, part_yx = pair_stiffness(k, below, above)
    diag = SELF * (k[0] + k[1] + k[2]) + part_0 + both(part_y, 1, 0)
    inv = 1.0 / (diag + both(part_x + both(part_yx, 1, 0), 1, 1))
    f = jnp.where(rim, 0.0, WEIGHT_ONE * res * inv)
    f_ref[zp + 1] = f
    for a in range(3):
        p_ref[a, zp + 1] = k[a] * f
    if to < NZ if isinstance(to, int) else True:
        s1_ref[to] = WEIGHT_TWO * inv


def image_plane(to, zp, kap_ref, f_ref, p_ref, s1_ref, s2_ref, rim):
    k = [kap_ref[a, zp + 1] for a in range(3)]
    p = [p_ref[a, zp + 1] for a in range(3)]
    d0, d1, d2 = (p_ref[a, zp] + p_ref[a, zp + 2] for a in range(3))
    f, fz = f_ref[zp + 1], f_ref[zp] + f_ref[zp + 2]
    own_y = 0.5 * p[1] + 0.125 * (d0 + d1)
    own_yx = 0.125 * (p[1] + p[2]) + (1.0 / 24.0) * (d0 + d1 + d2)
    own_x = 0.5 * p[2] + 0.125 * (d0 + d2)
    fy, fyz = both(f, 1, 0), both(fz, 1, 0)
    t24, t8 = (1.0 / 24.0) * fyz, 0.125 * fyz
    total = 0.5 * d0 + both(own_y, 1, 0) + both(own_x + both(own_yx, 1, 0), 1, 1)
    total = total + k[0] * (0.5 * fz + t8 + both(0.125 * fz + t24, 1, 1))
    total = total + k[1] * (0.5 * fy + t8 + both(0.125 * fy + t24, 1, 1))
    total = total + k[2] * both(0.5 * f + 0.125 * (fz + fy) + t24, 1, 1)
    scaled = s1_ref[to]
    s1_ref[to] = jnp.where(rim, total, scaled)
    s2_ref[to] = jnp.where(rim, 0.0, KEEP * f + scaled * total)


def plane_rim():
    row, lane = iota((NY, NX), 0), iota((NY, NX), 1)
    return (row == 0) | (row == NY - 1) | (lane == 0) | (lane == NX - 1)


def inner_first_kernel(kap_ref, rr_ref, s1_ref, f_ref, p_ref):
    rim = plane_rim()
    f_ref[0] = jnp.zeros((NY, NX), F32)
    p_ref[:, 0] = jnp.zeros((3, NY, NX), F32)

    @pl.loop(0, 3)
    def _(i):
        for j in range(5):
            zp = i * 5 + j
            first_plane(zp, zp, kap_ref, rr_ref[place(zp)], f_ref, p_ref, s1_ref, rim)


def inner_image_kernel(kap_ref, f_ref, p_ref, s1_in, after_ref, s1_ref, s2_ref):
    rim = plane_rim()

    @pl.loop(0, 2)
    def _(i):
        for j in range(7):
            image_plane(i * 7 + j, i * 7 + j, kap_ref, f_ref, p_ref, s1_ref, s2_ref, rim)


def outer_kernel(kap_ref, rr_ref, bulk_ref, f_in, p_in, s1_in, s2_in, after_ref, s1_ref, s2_ref, k_ref, f_ref, p_ref):
    rim = plane_rim()
    for a in range(3):
        for i in range(3):
            k_ref[a, i] = kap_ref[a, NZ - 2 + i]
        for i in range(2):
            k_ref[a, 3 + i] = bulk_ref[(2 * a + i) * NY : (2 * a + i + 1) * NY]
            p_ref[a, i] = p_in[a, NZ - 2 + i]
    for i in range(2):
        f_ref[i] = f_in[NZ - 2 + i]
    first_plane(NZ - 1, 1, k_ref, rr_ref[place(NZ - 1)], f_ref, p_ref, s1_ref, rim)
    first_plane(NZ, 2, k_ref, bulk_ref[6 * NY : 7 * NY], f_ref, p_ref, s1_ref, rim)
    for i in range(2):
        image_plane(NZ - 2 + i, i, k_ref, f_ref, p_ref, s1_ref, s2_ref, rim)


def along_x(values):
    return both(values, 1, 1)


def edge_rows_kernel(y0_ref, y1_ref, y2_ref, r0_ref, r1_ref, r2_ref, s1_in, s2_in, s1_ref, s2_ref):
    size = 24
    row, lane = iota((size, NX), 0), iota((size, NX), 1)
    inner = (lane > 0) & (lane < NX - 1)
    near = inner & (row < NZ + 1)
    inner16 = inner[:NZ]
    sent = [y0_ref[0:YPAY], y1_ref[0:YPAY], y2_ref[...]]
    phase = lax.rem(lax.axis_index("gy"), 3)
    high = jnp.where(phase == 0, sent[0], jnp.where(phase == 1, sent[1], sent[2]))
    low = jnp.where(phase == 0, sent[2], jnp.where(phase == 1, sent[0], sent[1]))
    lo, hi = neighbours([r0_ref[0:YPAY], r1_ref[0:YPAY], r2_ref[...]])
    for other, mine, face, second in (
        (lo, low, 0, 1),
        (hi, high, NY - 1, NY - 2),
    ):

        def group(source, at):
            return jnp.where(row < GROUP, source[at : at + size], 0.0)

        k = [[group(other, a * KROWS + s * GROUP) for a in range(3)] for s in (0, 1)]
        k += [[group(mine, a * KROWS + s * GROUP) for a in range(3)] for s in (1, 0)]
        parts = [pair_stiffness(v, (None, None, None), [both(u, 1, 0) for u in v]) for v in k]
        res = [None] + [jnp.where(row < NZ + 1, v[YPAY - size :], 0.0) for v in (roll(other, 4 - 8, 0), roll(mine, 4 - 8, 0))]
        f, inv = [None] * 3, [None] * 3
        for c in (1, 2):
            diag = SELF * (k[c][0] + k[c][1] + k[c][2]) + parts[c][0] + parts[c - 1][1] + parts[c + 1][1]
            inv[c] = 1.0 / (diag + along_x(parts[c][2] + parts[c - 1][3] + parts[c + 1][3]))
            f[c] = jnp.where(near, WEIGHT_ONE * res[c] * inv[c], 0.0)
        p = [None] + [[v * f[c] for v in k[c]] for c in (1, 2)]
        d = [None] + [[both(v, 1, 0) for v in p[c]] for c in (1, 2)]
        fz = [None] + [both(f[c], 1, 0) for c in (1, 2)]

        def row_parts(c):
            return (
                0.5 * p[c][1] + 0.125 * (d[c][0] + d[c][1]),
                0.125 * (p[c][1] + p[c][2]) + (1.0 / 24.0) * (d[c][0] + d[c][1] + d[c][2]),
            )

        own_y, own_yx = row_parts(1)
        own_x = 0.5 * p[2][2] + 0.125 * (d[2][0] + d[2][2])
        t24, t8 = (1.0 / 24.0) * fz[1], 0.125 * fz[1]
        total = 0.5 * d[2][0] + own_y + along_x(own_x + own_yx)
        total = total + k[2][0] * (0.5 * fz[2] + t8 + along_x(0.125 * fz[2] + t24))
        total = total + k[2][1] * (0.5 * f[1] + t8 + along_x(0.125 * f[1] + t24))
        total = total + k[2][2] * along_x(0.5 * f[2] + 0.125 * (fz[2] + f[1]) + t24)
        total = total[:NZ] + s1_ref[:, face, :]
        scaled = WEIGHT_TWO * inv[2][:NZ]
        s1_ref[:, face, :] = jnp.where(inner16, scaled, total)
        s2_ref[:, face, :] = jnp.where(inner16, KEEP * f[2][:NZ] + scaled * total, 0.0)

        own_y, own_yx = row_parts(2)
        t24, t8 = (1.0 / 24.0) * fz[2], 0.125 * fz[2]
        total = own_y + along_x(own_yx) + k[3][0] * (t8 + along_x(t24))
        total = total + k[3][1] * (0.5 * f[2] + t8 + along_x(0.125 * f[2] + t24))
        total = (total + k[3][2] * along_x(0.125 * f[2] + t24))[:NZ]
        scaled = s1_ref[:, second, :]
        s1_ref[:, second, :] = jnp.where(inner16, scaled, scaled + total)
        s2_ref[:, second, :] = s2_ref[:, second, :] + jnp.where(inner16, scaled * total, 0.0)


def slab_lanes(left):
    lane = iota((8, NX), 1)
    zp, c = lane >> 2, lane & 3
    outer = c < 2 if left else c >= 2
    real = zp < GROUP
    near = ((c == 1) | (c == 2)) & (zp < NZ + 1)
    offset = jnp.where(outer, 0, 2) if left else jnp.where(outer, 2, 0)
    offset_r = jnp.where(outer, RLANE - 1, RLANE) if left else jnp.where(outer, RLANE, RLANE - 1)
    sources = [jnp.where(real, a * KROWS + 2 * zp + (c & 1) + offset, 0) for a in range(3)]
    sources.append(jnp.where(near, zp + offset_r, 0))
    return outer, [real] * 3 + [near], sources


def slab_kernel(left_ref, right_ref, after_ref, slab_ref):
    for side, pack in enumerate((left_ref, right_ref)):
        outer, keeps, sources = slab_lanes(side == 0)
        for q in range(4):
            for i in range(0, NY + 8, 8):
                piece = take(pack[i : i + 8], sources[q])
                slab_ref[side, q, i : i + 8] = jnp.where(keeps[q] & ~outer, piece, 0.0)


def rim_kernel(s1_ref, s2_ref, rim1_ref, rim2_ref):
    lane = iota((NY, NX), 1)
    for source, rim in ((s1_ref, rim1_ref), (s2_ref, rim2_ref)):
        values = jnp.zeros((NY, NX), F32)
        for zp in range(NZ):
            values = jnp.where(lane >= 4 * zp, roll(source[zp], 4 * zp + 2, 1), values)
        rim[...] = values


def slab_terms(mine, other, rim1, rim2, left):
    rows = NY + 8
    outer, keeps, sources = slab_lanes(left)

    def spread(q):
        pieces = []
        for i in range(0, rows, 8):
            pieces.append(jnp.where(keeps[q] & outer, take(other[i : i + 8], sources[q]), mine[q, i : i + 8]))
        return jnp.concatenate(pieces, axis=0)

    k = [spread(a) for a in range(3)]
    res = spread(3)
    c = iota((rows, NX), 1) & 3
    near = jnp.concatenate([keeps[3]] * (rows // 8), axis=0)

    dz = [both(v, 4, 1) for v in k]
    part_0, part_y, part_x, part_yx = pair_stiffness(k, (None, None, None), dz)
    diag = SELF * (k[0] + k[1] + k[2]) + part_0 + both(part_y, 1, 0)
    inv = 1.0 / (diag + both(part_x + both(part_yx, 1, 0), 1, 1))
    f = jnp.where(near, WEIGHT_ONE * res * inv, 0.0)

    def from_outer(values):
        return roll(values, 1 if left else -1, 1)

    p = [v * f for v in k]
    d0, d1, d2 = (both(v, 4, 1) for v in p)
    own_y = 0.5 * p[1] + 0.125 * (d0 + d1)
    own_yx = 0.125 * (p[1] + p[2]) + (1.0 / 24.0) * (d0 + d1 + d2)
    own_x = 0.5 * p[2] + 0.125 * (d0 + d2)
    fz = both(f, 4, 1)
    fy, fyz = both(f, 1, 0)[:NY], both(fz, 1, 0)[:NY]
    fc, fz = f[:NY], fz[:NY]
    k = [v[:NY] for v in k]
    t24, t8 = (1.0 / 24.0) * fyz, 0.125 * fyz
    total = 0.5 * d0[:NY] + both(own_y, 1, 0)[:NY] + from_outer(own_x[:NY] + both(own_yx, 1, 0)[:NY])
    total = total + k[0] * (0.5 * fz + t8 + from_outer(0.125 * fz + t24))
    total = total + k[1] * (0.5 * fy + t8 + from_outer(0.125 * fy + t24))
    total = total + k[2] * from_outer(0.5 * fc + 0.125 * (fz + fy) + t24)
    face = (c == 2 if left else c == 1)[:NY]
    return jnp.where(face, KEEP * fc + WEIGHT_TWO * inv[:NY] * (total + rim1), rim2 + rim1 * total)


def coarse_solve(cor_ref, lower, upper):
    xs = iota((16, NX), 1) & 31
    arrays = []
    for q in range(4):
        whole = jnp.where(xs < 4, roll(lower, -4 * q, 1), cor_ref[q])
        arrays.append(jnp.where((xs >= 20) & (xs < 24), roll(upper, 20 - 4 * q, 1), whole))
    kc, rhs = arrays[:3], arrays[3]
    lane = iota((16, NX), 1)

    def sides(values, axis):
        if axis == 0:
            return roll(values, 32, 1), roll(values, -32, 1)
        return roll(values, 1, axis - 1), roll(values, -1, axis - 1)

    within = [(lane >= 32, lane < 96), (None, None), (None, None)]
    diag = (1.0 + MASS / 3.0) * (kc[0] + kc[1] + kc[2])
    couple = []
    for a in range(3):
        for v, real in zip(sides(kc[a], a), within[a]):
            half = 0.5 * v if real is None else jnp.where(real, 0.5 * v, 0.0)
            diag = diag + half
            half = 0.5 * kc[a] + half
            couple.append(half if real is None else jnp.where(real, half, 0.0))
    inside = kc[0] > 0.0
    scaled = jnp.where(inside, OMEGA / jnp.where(inside, diag, 1.0), 0.0)
    couple = [scaled * v for v in couple]
    start = scaled * rhs
    estimate = start
    for _ in range(CITERS - 1):
        t = [v * u for v, u in zip(couple, [u for a in range(3) for u in sides(estimate, a)])]
        estimate = (start + (1.0 - OMEGA) * estimate) + (((t[0] + t[1]) + (t[2] + t[3])) + (t[4] + t[5]))
    return estimate[0:8]


def last_kernel(
    rb_ref, ra_ref, slab_ref, cor_ref, rim1_ref, rim2_ref, s2_ref, sel_ref, out_hbm, est_hbm, out_ref, est_ref, sems
):
    gx, gz = lax.axis_index("gx"), lax.axis_index("gz")
    even = gx % 2 == 0
    zero = jnp.zeros((XPAY, NX), F32)
    right = jnp.where(gx < lax.axis_size("gx") - 1, jnp.where(even, ra_ref[...], rb_ref[...]), zero)
    left = jnp.where(gx > 0, jnp.where(even, rb_ref[...], ra_ref[...]), zero)
    rim1, rim2 = rim1_ref[...], rim2_ref[...]
    from_left = slab_terms(slab_ref[0], left[:40], rim1, rim2, True)
    from_right = slab_terms(slab_ref[1], right[:40], rim1, rim2, False)
    lane = iota((NY, NX), 1)
    faces = jnp.where((lane & 3) < 2, from_right, from_left)

    estimate = coarse_solve(cor_ref, left[40:XPAY], right[40:XPAY])
    lane8 = iota((8, NX), 1)
    rim = (lane < 2) | (lane >= NX - 2)
    step = 4
    for zc in range(CZ):
        z_out = jnp.where(gz == 0, zc, CZ - 1 - zc)
        est_ref[z_out] = roll(estimate, -(zc * 32 + 4), 1)[4:8, 0:CX]
    copies = [pltpu.make_async_copy(est_ref, est_hbm, sems.at[NZ // step])]
    copies[0].start()
    for zc in range(CZ):
        wide = take(estimate, zc * 32 + 4 + (lane8 >> 3))
        fine = jnp.concatenate([jnp.broadcast_to(wide[4 + y : 5 + y], (BLK, NX)) for y in range(CY)], axis=0)
        for i in range(BLK):
            zp = zc * BLK + i
            z = jnp.where(gz == 0, zp, NZ - 1 - zp)
            out_ref[z] = jnp.where(rim, roll(faces, -(4 * zp + 2), 1), s2_ref[zp]) + sel_ref[z] * fine
            if zp % step == step - 1:
                planes = pl.ds(jnp.where(gz == 0, zp + 1 - step, NZ - 1 - zp), step)
                copies.append(pltpu.make_async_copy(out_ref.at[planes], out_hbm.at[planes], sems.at[zp // step]))
                copies[-1].start()
    for copy in copies:
        copy.wait()


def near(values):
    return pltpu.with_memory_space_constraint(values, pltpu.VMEM)


def call(kernel, inputs, outputs, scratch=(), aliases=None, us=0.1, name=None, in_space=pltpu.VMEM, out_spaces=None):
    return pl.pallas_call(
        kernel,
        out_shape=outputs,
        in_specs=[pl.BlockSpec(memory_space=in_space)] * len(inputs),
        out_specs=[pl.BlockSpec(memory_space=v) for v in out_spaces or [pltpu.VMEM] * len(outputs)],
        scratch_shapes=list(scratch),
        input_output_aliases=aliases or {},
        cost_estimate=pl.CostEstimate(flops=int(us * 1e9), bytes_accessed=0, transcendentals=0),
        compiler_params=pltpu.CompilerParams(vmem_limit_bytes=32 * 2**20),
        name=name,
    )(*inputs)


def vmem(*shape):
    return pltpu.VMEM(shape, F32)


def exchange(values, sizes, move):
    nx, ny, nz = sizes
    pairs = []
    for x in range(nx):
        for y in range(ny):
            for z in range(nz):
                a, b, c = move(x, y, z)
                pairs.append(((x * ny + y) * nz + z, (a * ny + b) * nz + c))
    return lax.ppermute(values, ("gx", "gy", "gz"), pairs)


def solution(mesh):
    sizes = (mesh.shape["gx"], mesh.shape["gy"], mesh.shape["gz"])
    nx, ny, nz = sizes

    def swap_z(values):
        return exchange(values, sizes, lambda x, y, z: (x, y, nz - 1 - z))

    def swap_y(values, slot):
        def move(x, y, z):
            b = y + 1 if y % 3 == slot else y - 1 if (y + 2) % 3 == slot else -1
            return (x, b, z) if 0 <= b < ny else (x ^ 1, y, z)

        return exchange(values, sizes, move)

    def swap_x(values, odd):
        return exchange(values, sizes, lambda x, y, z: ((x + 1 if x % 2 == odd else x - 1) % nx, y, z))

    def body(residual_in, labels, factor, basis, basis_index):
        inputs = [residual_in, labels, factor, basis, basis_index]
        kap, rr, sel, urgent = call(
            first_kernel,
            [pltpu.with_memory_space_constraint(v, pltpu.HBM) for v in inputs],
            [vmem(3, NZ + 1, NY, NX), vmem(NZ, NY, NX), vmem(NZ, NY, NX), vmem(ZURGENT, NX)],
            [
                pltpu.VMEM(labels.shape, jnp.int32),
                pltpu.VMEM(factor.shape, F32),
                pltpu.VMEM(basis.shape, F32),
                pltpu.VMEM(basis_index.shape, jnp.int32),
                pltpu.VMEM((4, BLK, BLK, NX), F32),
                pltpu.VMEM((64, NX), F32),
                pltpu.SemaphoreType.DMA((2,)),
                pltpu.SemaphoreType.DMA((len(PARTS), 3)),
            ],
            us=1.8,
            name="stiffness",
            in_space=pltpu.HBM,
        )
        kap, rr, sel, urgent = near(kap), near(rr), near(sel), near(urgent)
        zu = near(swap_z(urgent))
        payloads = [vmem(YPAY + URGENT, NX), vmem(YPAY + URGENT, NX), vmem(YPAY, NX)]
        y0, y1, y2, bulk = call(rows_kernel, [kap, rr], payloads + [vmem(BULK, NX)], name="rows")
        zb = near(swap_z(near(bulk)))
        left, right, ends = call(
            columns_kernel, [kap, rr], [vmem(NY, NX), vmem(NY, NX), vmem(8, NX)], us=0.4, name="columns"
        )
        s1, f, p = call(
            inner_first_kernel,
            [kap, rr],
            [vmem(NZ, NY, NX), vmem(NZ, NY, NX), vmem(3, NZ, NY, NX)],
            us=0.6,
            name="inner_first",
        )
        s1, f, p = near(s1), near(f), near(p)
        y0, y1, y2, u2 = call(
            send_rows_kernel,
            [zu, urgent, near(ends), near(y0), near(y1), near(y2), f],
            payloads + [vmem(URGENT, NX)],
            aliases={3: 0, 4: 1, 5: 2},
            us=10.0,
            name="send_rows",
        )
        y0, y1, y2, u2 = near(y0), near(y1), near(y2), near(u2)
        r0, r1, t2, r2 = near(swap_y(y0, 0)), near(swap_y(y1, 1)), near(swap_y(u2, 2)), near(swap_y(y2, 2))
        s1, s2 = call(
            inner_image_kernel,
            [kap, f, p, s1, u2],
            [vmem(NZ, NY, NX), vmem(NZ, NY, NX)],
            aliases={3: 0},
            us=0.7,
            name="inner_image",
        )
        s1, s2 = near(s1), near(s2)
        left, right = call(
            columns_beyond_kernel,
            [near(left), near(right), zb, s2],
            [vmem(NY, NX), vmem(NY, NX)],
            aliases={0: 0, 1: 1},
            us=100.0,
            name="columns_beyond",
        )
        xa, xb, left, right, cor = call(
            columns_more_kernel,
            [r0, r1, t2, u2, near(left), near(right)],
            [vmem(XPAY, NX), vmem(XPAY, NX), vmem(40, NX), vmem(40, NX), vmem(4, 16, NX)],
            us=1.0,
            name="columns_more",
        )
        xa, xb = near(xa), near(xb)
        vb, va = near(swap_x(xb, 1)), near(swap_x(xa, 0))
        s1, s2 = call(
            outer_kernel,
            [kap, rr, zb, f, p, s1, s2, xa],
            [vmem(NZ, NY, NX), vmem(NZ, NY, NX)],
            [pltpu.VMEM((3, 5, NY, NX), F32), pltpu.VMEM((4, NY, NX), F32), pltpu.VMEM((3, 4, NY, NX), F32)],
            aliases={5: 0, 6: 1},
            us=0.25,
            name="outer",
        )
        s1, s2 = call(
            edge_rows_kernel,
            [y0, y1, y2, r0, r1, r2, near(s1), near(s2)],
            [vmem(NZ, NY, NX), vmem(NZ, NY, NX)],
            aliases={6: 0, 7: 1},
            us=0.4,
            name="edge_rows",
        )
        (slab,) = call(slab_kernel, [near(left), near(right), xa], [vmem(2, 4, 40, NX)], us=0.1, name="slab")
        rim1, rim2 = call(rim_kernel, [near(s1), near(s2)], [vmem(NY, NX), vmem(NY, NX)], us=0.2, name="rim")
        out, estimate = call(
            last_kernel,
            [vb, va, near(slab), near(cor), near(rim1), near(rim2), near(s2), sel],
            [jax.ShapeDtypeStruct((NZ, NY, NX), F32), jax.ShapeDtypeStruct((CZ, CY, CX), F32)],
            [pltpu.VMEM((NZ, NY, NX), F32), pltpu.VMEM((CZ, CY, CX), F32), pltpu.SemaphoreType.DMA((5,))],
            us=1.5,
            name="last",
            out_spaces=[pltpu.HBM, pltpu.HBM],
        )
        return out, estimate

    in_specs = (
        P("gz", "gy", "gx"),
        P("gz", "gy", "gx"),
        P(None, "gz", "gy", "gx"),
        P(),
        P("gz", "gy", "gx"),
    )
    out_specs = (P("gz", "gy", "gx"), P("gz", "gy", "gx"))
    return jax.shard_map(body, mesh=mesh, in_specs=in_specs, out_specs=out_specs, check_vma=False)
```

```python
import math

import jax
import jax.numpy as jnp
from jax import lax
from jax.experimental import pallas as pl
from jax.experimental.pallas import tpu as pltpu
from jax.sharding import PartitionSpec as P

BLK = 8
CITERS = 4
BRICK = (0.6, 1.0, 1.0)
MORTAR = (0.25, 0.3, 0.3)
MASS = 0.05
OMEGA = 0.8
WEIGHT_ONE = 1.0 / (1.05 - 0.95 * math.cos(math.pi / 4))
WEIGHT_TWO = 1.0 / (1.05 + 0.95 * math.cos(math.pi / 4))
SELF = 1.0 + 1.0 + 1.0 / 3.0 + MASS / 3.0
KEEP = 1.0 + WEIGHT_TWO / WEIGHT_ONE - WEIGHT_TWO

NZ, NY, NX = 16, 32, 128
CZ, CY, CX = 2, 4, 16
PARTS = range(2)
F32 = jnp.float32
HIGHEST = lax.Precision.HIGHEST

BULK = 7 * NY + 8
BCOL = 7 * NY
URGENT = 16
ZURGENT = 48
KROWS = 36
GROUP = NZ + 2
RROW = 3 * KROWS
YPAY = 128
XPAY = 40 + 16
RLANE = 110


def iota(shape, dim):
    return lax.broadcasted_iota(jnp.int32, shape, dim)


def roll(values, shift, axis):
    size = values.shape[axis]
    shift = shift % size
    return values if shift == 0 else pltpu.roll(values, shift, axis)


def both(values, step, axis):
    return roll(values, step, axis) + roll(values, -step, axis)


def take(values, lanes):
    return jnp.take_along_axis(values, lanes, axis=1, mode="promise_in_bounds")


def pair_stiffness(own, below, above):
    k0, k1, k2 = own
    d0, d1, d2 = (a + b if a is not None else b for a, b in zip(below, above))
    part_y = 0.5 * k1 + 0.125 * (d0 + d1)
    part_yx = 0.125 * (k1 + k2) + (1.0 / 24.0) * (d0 + d1 + d2)
    part_0 = 0.5 * d0
    part_x = 0.5 * k2 + 0.125 * (d0 + d2)
    return part_0, part_y, part_x, part_yx


def first_kernel(
    r_hbm, lab_hbm, fac_hbm, bas_hbm, bix_hbm, kap_ref, rr_ref, sel_ref, urgent_ref,
    lab_ref, fac_ref, bas_ref, bix_ref, tile_ref, sum_ref, sems, more_sems
):
    gz = lax.axis_index("gz")
    parts = []
    small = [
        pltpu.make_async_copy(bas_hbm, bas_ref, sems.at[0]),
        pltpu.make_async_copy(bix_hbm, bix_ref, sems.at[1]),
    ]
    for copy in small:
        copy.start()
    step = NZ // len(PARTS)
    for part in PARTS:
        planes = pl.ds(jnp.where(gz == 0, part * step, NZ - step - part * step), step)
        parts.append(
            [
                pltpu.make_async_copy(lab_hbm.at[planes], lab_ref.at[planes], more_sems.at[part, 0]),
                pltpu.make_async_copy(fac_hbm.at[:, planes], fac_ref.at[:, planes], more_sems.at[part, 1]),
                pltpu.make_async_copy(r_hbm.at[planes], rr_ref.at[planes], more_sems.at[part, 2]),
            ]
        )
        for copy in parts[part]:
            copy.start()
    kap_ref[:, 0] = jnp.zeros((3, NY, NX), F32)
    for copy in small:
        copy.wait()
    tiled = lax.dot_general(
        bas_ref[...].reshape(4 * BLK * BLK, BLK),
        ((iota((BLK, NX), 1) & (BLK - 1)) == iota((BLK, NX), 0)).astype(F32),
        (((1,), (0,)), ((), ())),
        precision=HIGHEST,
        preferred_element_type=F32,
    )
    tile_ref[...] = tiled.reshape(4, BLK, BLK, NX)
    edges = [None] * 7
    spread = ((iota((CX, NX), 1) >> 3) == iota((CX, NX), 0)).astype(F32)
    indices = []
    for zc in range(CZ):
        index = lax.dot_general(
            bix_ref[jnp.where(gz == 0, zc, CZ - 1 - zc)].astype(F32),
            spread,
            (((1,), (0,)), ((), ())),
            precision=HIGHEST,
            preferred_element_type=F32,
        )
        indices.append(jnp.concatenate([jnp.broadcast_to(index[y : y + 1], (BLK, NX)) for y in range(CY)], axis=0))
    for zc in range(CZ):
        index = indices[zc]
        sums = [None] * 4
        for i in range(BLK):
            zp = zc * BLK + i
            if zp % step == 0:
                for copy in parts[zp // step]:
                    copy.wait()
            z = jnp.where(gz == 0, zp, NZ - 1 - zp)
            zi = jnp.where(gz == 0, i, BLK - 1 - i)
            mortar = lab_ref[z] == 1
            b0, b1, b2, b3 = (jnp.concatenate([tile_ref[n, zi]] * CY, axis=0) for n in range(4))
            basis = jnp.where(index < 1.5, jnp.where(index < 0.5, b0, b1), jnp.where(index < 2.5, b2, b3))
            res = rr_ref[z]
            sel_ref[z] = basis
            terms = []
            for a in range(3):
                k = jnp.where(mortar, MORTAR[a], BRICK[a]) * fac_ref[a, z]
                kap_ref[a, zp + 1] = k
                terms.append(k)
                if zp >= NZ - 2:
                    plane = 2 * a + NZ - 1 - zp
                    edges[plane] = k
            if zp == NZ - 1:
                edges[6] = res
            terms.append(basis * res)
            sums = [t if s is None else s + t for s, t in zip(sums, terms)]
        for q in range(4):
            total = sums[q].reshape(CY, BLK, NX).sum(axis=1)
            total = total if q == 3 else total * (1.0 / BLK**3)
            at = (q * 2 + zc) * 8
            sum_ref[at : at + CY] = total
            sum_ref[at + CY : at + 8] = total
    gather = ((iota((NX, NX), 0) >> 3) == (iota((NX, NX), 1) & (CX - 1))).astype(jnp.bfloat16)
    rest, bricks = sum_ref[...], None
    for _ in range(3):
        part = rest.astype(jnp.bfloat16)
        rest = rest - part.astype(F32)
        term = lax.dot_general(part, gather, (((1,), (0,)), ((), ())), preferred_element_type=F32)
        bricks = term if bricks is None else bricks + term
    group = iota((8, NX), 1) >> 4
    coarse = bricks[0:8]
    for g in range(1, 8):
        coarse = jnp.where(group == g, bricks[g * 8 : g * 8 + 8], coarse)
    urgent_ref[0:8] = coarse
    row = iota((8, NX), 0)

    def ends(plane):
        return jnp.where(row < 4, plane[:8], plane[NY - 8 :])

    left, right = columns_beyond(
        jnp.zeros((8, NX), F32), jnp.zeros((8, NX), F32), lambda g, x0: roll(ends(edges[g]), x0, 1)
    )
    urgent_ref[8:16] = end_tile(left, right)
    for g, plane in enumerate(edges):
        a, beyond = divmod(g, 2)
        for inner in range(2) if g < 6 else (1,):
            at = 12 if g == 6 else 4 * a + 2 * inner + beyond
            urgent_ref[16 + at : 17 + at] = plane[0:1] if inner else plane[1:2]
            urgent_ref[32 + at : 33 + at] = plane[NY - 1 : NY] if inner else plane[NY - 2 : NY - 1]


def end_tile(left, right):
    row = iota((8, NX), 0)
    low = jnp.where(row < 2, left, roll(right, 2, 0))
    high = jnp.where(row < 6, roll(left, -2, 0), right)
    return jnp.where(row < 4, low, high)


def place(zp):
    return jnp.where(lax.axis_index("gz") == 0, zp, NZ - 1 - zp)


def rows_kernel(kap_ref, rr_ref, ya_ref, yb_ref, bulk_ref):
    even = lax.rem(lax.axis_index("gy"), 2) == 0

    def put(at, low, high):
        ya_ref[at : at + 1] = jnp.where(even, high, low)
        yb_ref[at : at + 1] = jnp.where(even, low, high)

    for zp in range(NZ):
        for a in range(3):
            at = a * KROWS + zp
            put(at, kap_ref[a, zp + 1, 1:2], kap_ref[a, zp + 1, NY - 2 : NY - 1])
            put(at + GROUP, kap_ref[a, zp + 1, 0:1], kap_ref[a, zp + 1, NY - 1 : NY])
        put(RROW + zp, rr_ref[place(zp), 0:1], rr_ref[place(zp), NY - 1 : NY])
    for a in range(3):
        for s in range(2):
            bulk_ref[(2 * a + s) * NY : (2 * a + s + 1) * NY] = kap_ref[a, NZ - s]
    bulk_ref[6 * NY : 7 * NY] = rr_ref[place(NZ - 1)]
    planes = [kap_ref[a, NZ - s] for a in range(3) for s in range(2)] + [rr_ref[place(NZ - 1)]]
    lane = iota((NY, NX), 1)
    columns = jnp.zeros((NY, NX), F32)
    for g, plane in enumerate(planes):
        columns = jnp.where(lane >= 4 * g, roll(plane, 4 * g + 2, 1), columns)
    lane = iota((8, NX), 1)
    folded = columns[:8]
    for i in range(1, NY // 8):
        folded = jnp.where(lane >= 32 * i, roll(columns[8 * i : 8 * i + 8], 32 * i, 1), folded)
    bulk_ref[BCOL:BULK] = folded


def columns_kernel(kap_ref, rr_ref, left_ref, right_ref, ends_ref):
    lane = iota((NY, NX), 1)
    left = jnp.zeros((NY, NX), F32)
    right = jnp.zeros((NY, NX), F32)
    for a in range(3):
        for zp in range(NZ):
            at = 2 + a * KROWS + 2 * zp
            moved = roll(kap_ref[a, zp + 1], at, 1)
            left = jnp.where(lane >= at, moved, left)
            right = jnp.where(lane >= at - 2, moved, right)
    for zp in range(NZ):
        at = RLANE + zp
        moved = roll(rr_ref[place(zp)], at, 1)
        left = jnp.where(lane >= at, moved, left)
        right = jnp.where(lane >= at - 1, moved, right)
    left_ref[...] = left
    right_ref[...] = right
    row = iota((8, NX), 0)
    ends_ref[...] = end_tile(*(jnp.where(row < 4, v[:8], v[NY - 8 :]) for v in (left, right)))


def columns_beyond(left, right, moved):
    lane = iota(left.shape, 1)
    for a in range(3):
        for s in range(2):
            at = 2 + a * KROWS + 2 * (NZ + s)
            values = moved(2 * a + s, at)
            left = jnp.where((lane == at) | (lane == at + 1), values, left)
            right = jnp.where((lane == at - 2) | (lane == at - 1), values, right)
    at = RLANE + NZ
    values = moved(6, at)
    return jnp.where(lane == at, values, left), jnp.where(lane == at - 1, values, right)


def columns_beyond_kernel(left_in, right_in, bulk_ref, after_ref, left_ref, right_ref):
    folded = bulk_ref[BCOL:BULK]
    columns = jnp.concatenate([roll(folded, -32 * i, 1) for i in range(NY // 8)], axis=0)
    left_ref[...], right_ref[...] = columns_beyond(
        left_in[...], right_in[...], lambda g, x0: roll(columns, x0 - 4 * g - 2, 1)
    )


def send_rows_kernel(far_ref, mine_ref, ends_ref, ya_in, yb_in, after_ref, ya_ref, yb_ref, u0_ref, u1_ref, u2_ref):
    phase = lax.rem(lax.axis_index("gy"), 3)
    row, lane = iota((8, NX), 0), iota((8, NX), 1)
    low, high = far_ref[16:32], far_ref[32:48]
    even = lax.rem(lax.axis_index("gy"), 2) == 0
    for ref, rows in ((ya_ref, jnp.where(even, high, low)), (yb_ref, jnp.where(even, low, high))):
        for i in range(6):
            ref[i * GROUP + NZ : (i + 1) * GROUP] = rows[2 * i : 2 * i + 2]
        ref[RROW + NZ : RROW + NZ + 1] = rows[12:13]
    is_right = ((row >> 1) & 1) == 1
    at = lane - jnp.where(is_right, 0, 2)
    within = at - jnp.where(at >= 2 * KROWS, 2 * KROWS, jnp.where(at >= KROWS, KROWS, 0))
    beyond = (at < RROW) & (within >= 2 * NZ)
    beyond = beyond | (lane == RLANE + NZ - is_right.astype(jnp.int32))
    tile = jnp.where(beyond, far_ref[8:16], ends_ref[...])
    turned = roll(tile, 4, 0)
    coarse = jnp.where(row < CY, mine_ref[0:8], far_ref[0:8])
    for slot, ref in enumerate((u0_ref, u1_ref, u2_ref)):
        ref[0:8] = coarse
        ref[8:16] = jnp.where(phase == slot, turned, tile)


def neighbours(slots):
    gy = lax.axis_index("gy")
    phase = lax.rem(gy, 3)
    zero = jnp.zeros(slots[0].shape, F32)
    hi = jnp.where(phase == 0, slots[0], jnp.where(phase == 1, slots[1], slots[2]))
    lo = jnp.where(phase == 0, slots[2], jnp.where(phase == 1, slots[0], slots[1]))
    return jnp.where(gy > 0, lo, zero), jnp.where(gy < lax.axis_size("gy") - 1, hi, zero)


def columns_more_kernel(r0_ref, r1_ref, r2_ref, mine_ref, left_in, right_in, xa_ref, xb_ref, left_ref, right_ref, cor_ref):
    gx = lax.axis_index("gx")
    lo, hi = neighbours([r0_ref[...], r1_ref[...], r2_ref[...]])
    lane, row = iota((8, NX), 1), iota((8, NX), 0)

    def halo(shift):
        above, below = roll(hi[8:16], -shift, 0), roll(lo[8:16], 6 - shift, 0)
        return jnp.where(row < 2, above, jnp.where(row >= 6, below, 0.0))

    left_ref[0:NY] = left_in[...]
    right_ref[0:NY] = right_in[...]
    left_ref[NY : NY + 8] = halo(0)
    right_ref[NY : NY + 8] = halo(2)
    even_x = gx % 2 == 0
    xa_ref[0:40] = jnp.where(even_x, right_ref[...], left_ref[...])
    xb_ref[0:40] = jnp.where(even_x, left_ref[...], right_ref[...])

    tiles = [lo[0:8], mine_ref[0:8], hi[0:8]]
    zc, xs = lane >> 5, lane & 31
    pair = jnp.where(zc < 2, zc, 3 - zc)
    own = (xs >= 4) & (xs < 20)
    low_half, xs16 = lane < 64, iota((16, NX), 1) & 31
    sides = [jnp.zeros((16, NX), F32), jnp.zeros((16, NX), F32)]
    for q in range(4):
        at = (q * 2 + pair) * CX + jnp.clip(xs - 4, 0, CX - 1)
        below, mine, above = ((v, roll(v, 4, 0)) for v in (jnp.where(own, take(t, at), 0.0) for t in tiles))
        first = jnp.where(row < 4, jnp.where(low_half, below[0], below[1]), jnp.where(low_half, mine[1], mine[0]))
        second = jnp.where(row < 4, jnp.where(low_half, above[0], above[1]), 0.0)
        whole = jnp.concatenate([first, second], axis=0)
        cor_ref[q] = whole
        for i, start in enumerate((4, CX)):
            sides[i] = jnp.where((xs16 >= 4 * q) & (xs16 < 4 * q + 4), roll(whole, 4 * q - start, 1), sides[i])
    xa_ref[40:XPAY] = jnp.where(even_x, sides[1], sides[0])
    xb_ref[40:XPAY] = jnp.where(even_x, sides[0], sides[1])


def first_plane(to, zp, kap_ref, res, f_ref, p_ref, s1_ref, rim):
    below, k, above = ([kap_ref[a, zp + i] for a in range(3)] for i in range(3))
    part_0, part_y, part_x, part_yx = pair_stiffness(k, below, above)
    diag = SELF * (k[0] + k[1] + k[2]) + part_0 + both(part_y, 1, 0)
    inv = 1.0 / (diag + both(part_x + both(part_yx, 1, 0), 1, 1))
    f = jnp.where(rim, 0.0, WEIGHT_ONE * res * inv)
    f_ref[zp + 1] = f
    for a in range(3):
        p_ref[a, zp + 1] = k[a] * f
    if to < NZ if isinstance(to, int) else True:
        s1_ref[to] = WEIGHT_TWO * inv


def image_plane(to, zp, kap_ref, f_ref, p_ref, s1_ref, s2_ref, rim):
    k = [kap_ref[a, zp + 1] for a in range(3)]
    p = [p_ref[a, zp + 1] for a in range(3)]
    d0, d1, d2 = (p_ref[a, zp] + p_ref[a, zp + 2] for a in range(3))
    f, fz = f_ref[zp + 1], f_ref[zp] + f_ref[zp + 2]
    own_y = 0.5 * p[1] + 0.125 * (d0 + d1)
    own_yx = 0.125 * (p[1] + p[2]) + (1.0 / 24.0) * (d0 + d1 + d2)
    own_x = 0.5 * p[2] + 0.125 * (d0 + d2)
    fy, fyz = both(f, 1, 0), both(fz, 1, 0)
    t24, t8 = (1.0 / 24.0) * fyz, 0.125 * fyz
    total = 0.5 * d0 + both(own_y, 1, 0) + both(own_x + both(own_yx, 1, 0), 1, 1)
    total = total + k[0] * (0.5 * fz + t8 + both(0.125 * fz + t24, 1, 1))
    total = total + k[1] * (0.5 * fy + t8 + both(0.125 * fy + t24, 1, 1))
    total = total + k[2] * both(0.5 * f + 0.125 * (fz + fy) + t24, 1, 1)
    scaled = s1_ref[to]
    s1_ref[to] = jnp.where(rim, total, scaled)
    s2_ref[to] = jnp.where(rim, 0.0, KEEP * f + scaled * total)


def plane_rim():
    row, lane = iota((NY, NX), 0), iota((NY, NX), 1)
    return (row == 0) | (row == NY - 1) | (lane == 0) | (lane == NX - 1)


def inner_first_kernel(kap_ref, rr_ref, s1_ref, f_ref, p_ref):
    rim = plane_rim()
    f_ref[0] = jnp.zeros((NY, NX), F32)
    p_ref[:, 0] = jnp.zeros((3, NY, NX), F32)

    @pl.loop(0, 3)
    def _(i):
        for j in range(5):
            zp = i * 5 + j
            first_plane(zp, zp, kap_ref, rr_ref[place(zp)], f_ref, p_ref, s1_ref, rim)


def inner_image_kernel(kap_ref, f_ref, p_ref, s1_in, s1_ref, s2_ref):
    rim = plane_rim()

    @pl.loop(0, 2)
    def _(i):
        for j in range(7):
            image_plane(i * 7 + j, i * 7 + j, kap_ref, f_ref, p_ref, s1_ref, s2_ref, rim)


def outer_kernel(kap_ref, rr_ref, bulk_ref, f_in, p_in, s1_in, s2_in, after_ref, s1_ref, s2_ref, k_ref, f_ref, p_ref):
    rim = plane_rim()
    for a in range(3):
        for i in range(3):
            k_ref[a, i] = kap_ref[a, NZ - 2 + i]
        for i in range(2):
            k_ref[a, 3 + i] = bulk_ref[(2 * a + i) * NY : (2 * a + i + 1) * NY]
            p_ref[a, i] = p_in[a, NZ - 2 + i]
    for i in range(2):
        f_ref[i] = f_in[NZ - 2 + i]
    first_plane(NZ - 1, 1, k_ref, rr_ref[place(NZ - 1)], f_ref, p_ref, s1_ref, rim)
    first_plane(NZ, 2, k_ref, bulk_ref[6 * NY : 7 * NY], f_ref, p_ref, s1_ref, rim)
    for i in range(2):
        image_plane(NZ - 2 + i, i, k_ref, f_ref, p_ref, s1_ref, s2_ref, rim)


def along_x(values):
    return both(values, 1, 1)


def edge_rows_kernel(ya_ref, yb_ref, ra_ref, rb_ref, s1_in, s2_in, s1_ref, s2_ref):
    size = 24
    row, lane = iota((size, NX), 0), iota((size, NX), 1)
    inner = (lane > 0) & (lane < NX - 1)
    near = inner & (row < NZ + 1)
    inner16 = inner[:NZ]
    gy = lax.axis_index("gy")
    even = lax.rem(gy, 2) == 0
    ya, yb, ra, rb = ya_ref[...], yb_ref[...], ra_ref[...], rb_ref[...]
    low, high = jnp.where(even, yb, ya), jnp.where(even, ya, yb)
    zero = jnp.zeros((YPAY, NX), F32)
    lo = jnp.where(gy > 0, jnp.where(even, rb, ra), zero)
    hi = jnp.where(gy < lax.axis_size("gy") - 1, jnp.where(even, ra, rb), zero)
    for other, mine, face, second in (
        (lo, low, 0, 1),
        (hi, high, NY - 1, NY - 2),
    ):

        def group(source, at):
            return jnp.where(row < GROUP, source[at : at + size], 0.0)

        k = [[group(other, a * KROWS + s * GROUP) for a in range(3)] for s in (0, 1)]
        k += [[group(mine, a * KROWS + s * GROUP) for a in range(3)] for s in (1, 0)]
        parts = [pair_stiffness(v, (None, None, None), [both(u, 1, 0) for u in v]) for v in k]
        res = [None] + [jnp.where(row < NZ + 1, v[YPAY - size :], 0.0) for v in (roll(other, 4 - 8, 0), roll(mine, 4 - 8, 0))]
        f, inv = [None] * 3, [None] * 3
        for c in (1, 2):
            diag = SELF * (k[c][0] + k[c][1] + k[c][2]) + parts[c][0] + parts[c - 1][1] + parts[c + 1][1]
            inv[c] = 1.0 / (diag + along_x(parts[c][2] + parts[c - 1][3] + parts[c + 1][3]))
            f[c] = jnp.where(near, WEIGHT_ONE * res[c] * inv[c], 0.0)
        p = [None] + [[v * f[c] for v in k[c]] for c in (1, 2)]
        d = [None] + [[both(v, 1, 0) for v in p[c]] for c in (1, 2)]
        fz = [None] + [both(f[c], 1, 0) for c in (1, 2)]

        def row_parts(c):
            return (
                0.5 * p[c][1] + 0.125 * (d[c][0] + d[c][1]),
                0.125 * (p[c][1] + p[c][2]) + (1.0 / 24.0) * (d[c][0] + d[c][1] + d[c][2]),
            )

        own_y, own_yx = row_parts(1)
        own_x = 0.5 * p[2][2] + 0.125 * (d[2][0] + d[2][2])
        t24, t8 = (1.0 / 24.0) * fz[1], 0.125 * fz[1]
        total = 0.5 * d[2][0] + own_y + along_x(own_x + own_yx)
        total = total + k[2][0] * (0.5 * fz[2] + t8 + along_x(0.125 * fz[2] + t24))
        total = total + k[2][1] * (0.5 * f[1] + t8 + along_x(0.125 * f[1] + t24))
        total = total + k[2][2] * along_x(0.5 * f[2] + 0.125 * (fz[2] + f[1]) + t24)
        total = total[:NZ] + s1_ref[:, face, :]
        scaled = WEIGHT_TWO * inv[2][:NZ]
        s1_ref[:, face, :] = jnp.where(inner16, scaled, total)
        s2_ref[:, face, :] = jnp.where(inner16, KEEP * f[2][:NZ] + scaled * total, 0.0)

        own_y, own_yx = row_parts(2)
        t24, t8 = (1.0 / 24.0) * fz[2], 0.125 * fz[2]
        total = own_y + along_x(own_yx) + k[3][0] * (t8 + along_x(t24))
        total = total + k[3][1] * (0.5 * f[2] + t8 + along_x(0.125 * f[2] + t24))
        total = (total + k[3][2] * along_x(0.125 * f[2] + t24))[:NZ]
        scaled = s1_ref[:, second, :]
        s1_ref[:, second, :] = jnp.where(inner16, scaled, scaled + total)
        s2_ref[:, second, :] = s2_ref[:, second, :] + jnp.where(inner16, scaled * total, 0.0)


def slab_lanes(left):
    lane = iota((8, NX), 1)
    zp, c = lane >> 2, lane & 3
    outer = c < 2 if left else c >= 2
    real = zp < GROUP
    near = ((c == 1) | (c == 2)) & (zp < NZ + 1)
    offset = jnp.where(outer, 0, 2) if left else jnp.where(outer, 2, 0)
    offset_r = jnp.where(outer, RLANE - 1, RLANE) if left else jnp.where(outer, RLANE, RLANE - 1)
    sources = [jnp.where(real, a * KROWS + 2 * zp + (c & 1) + offset, 0) for a in range(3)]
    sources.append(jnp.where(near, zp + offset_r, 0))
    return outer, [real] * 3 + [near], sources


def slab_kernel(left_ref, right_ref, after_ref, slab_ref):
    for side, pack in enumerate((left_ref, right_ref)):
        outer, keeps, sources = slab_lanes(side == 0)
        for q in range(4):
            for i in range(0, NY + 8, 8):
                piece = take(pack[i : i + 8], sources[q])
                slab_ref[side, q, i : i + 8] = jnp.where(keeps[q] & ~outer, piece, 0.0)


def rim_kernel(s1_ref, s2_ref, rim1_ref, rim2_ref):
    lane = iota((NY, NX), 1)
    for source, rim in ((s1_ref, rim1_ref), (s2_ref, rim2_ref)):
        values = jnp.zeros((NY, NX), F32)
        for zp in range(NZ):
            values = jnp.where(lane >= 4 * zp, roll(source[zp], 4 * zp + 2, 1), values)
        rim[...] = values


def slab_terms(mine, other, rim1, rim2, left):
    rows = NY + 8
    outer, keeps, sources = slab_lanes(left)

    def spread(q):
        pieces = []
        for i in range(0, rows, 8):
            pieces.append(jnp.where(keeps[q] & outer, take(other[i : i + 8], sources[q]), mine[q, i : i + 8]))
        return jnp.concatenate(pieces, axis=0)

    k = [spread(a) for a in range(3)]
    res = spread(3)
    c = iota((rows, NX), 1) & 3
    near = jnp.concatenate([keeps[3]] * (rows // 8), axis=0)

    dz = [both(v, 4, 1) for v in k]
    part_0, part_y, part_x, part_yx = pair_stiffness(k, (None, None, None), dz)
    diag = SELF * (k[0] + k[1] + k[2]) + part_0 + both(part_y, 1, 0)
    inv = 1.0 / (diag + both(part_x + both(part_yx, 1, 0), 1, 1))
    f = jnp.where(near, WEIGHT_ONE * res * inv, 0.0)

    def from_outer(values):
        return roll(values, 1 if left else -1, 1)

    p = [v * f for v in k]
    d0, d1, d2 = (both(v, 4, 1) for v in p)
    own_y = 0.5 * p[1] + 0.125 * (d0 + d1)
    own_yx = 0.125 * (p[1] + p[2]) + (1.0 / 24.0) * (d0 + d1 + d2)
    own_x = 0.5 * p[2] + 0.125 * (d0 + d2)
    fz = both(f, 4, 1)
    fy, fyz = both(f, 1, 0)[:NY], both(fz, 1, 0)[:NY]
    fc, fz = f[:NY], fz[:NY]
    k = [v[:NY] for v in k]
    t24, t8 = (1.0 / 24.0) * fyz, 0.125 * fyz
    total = 0.5 * d0[:NY] + both(own_y, 1, 0)[:NY] + from_outer(own_x[:NY] + both(own_yx, 1, 0)[:NY])
    total = total + k[0] * (0.5 * fz + t8 + from_outer(0.125 * fz + t24))
    total = total + k[1] * (0.5 * fy + t8 + from_outer(0.125 * fy + t24))
    total = total + k[2] * from_outer(0.5 * fc + 0.125 * (fz + fy) + t24)
    face = (c == 2 if left else c == 1)[:NY]
    return jnp.where(face, KEEP * fc + WEIGHT_TWO * inv[:NY] * (total + rim1), rim2 + rim1 * total)


def coarse_solve(cor_ref, lower, upper):
    xs = iota((16, NX), 1) & 31
    arrays = []
    for q in range(4):
        whole = jnp.where(xs < 4, roll(lower, -4 * q, 1), cor_ref[q])
        arrays.append(jnp.where((xs >= 20) & (xs < 24), roll(upper, 20 - 4 * q, 1), whole))
    kc, rhs = arrays[:3], arrays[3]
    lane = iota((16, NX), 1)

    def sides(values, axis):
        if axis == 0:
            return roll(values, 32, 1), roll(values, -32, 1)
        return roll(values, 1, axis - 1), roll(values, -1, axis - 1)

    within = [(lane >= 32, lane < 96), (None, None), (None, None)]
    diag = (1.0 + MASS / 3.0) * (kc[0] + kc[1] + kc[2])
    couple = []
    for a in range(3):
        for v, real in zip(sides(kc[a], a), within[a]):
            half = 0.5 * v if real is None else jnp.where(real, 0.5 * v, 0.0)
            diag = diag + half
            half = 0.5 * kc[a] + half
            couple.append(half if real is None else jnp.where(real, half, 0.0))
    inside = kc[0] > 0.0
    scaled = jnp.where(inside, OMEGA / jnp.where(inside, diag, 1.0), 0.0)
    couple = [scaled * v for v in couple]
    start = scaled * rhs
    estimate = start
    for _ in range(CITERS - 1):
        t = [v * u for v, u in zip(couple, [u for a in range(3) for u in sides(estimate, a)])]
        estimate = (start + (1.0 - OMEGA) * estimate) + (((t[0] + t[1]) + (t[2] + t[3])) + (t[4] + t[5]))
    return estimate[0:8]


def last_kernel(
    rb_ref, ra_ref, slab_ref, cor_ref, rim1_ref, rim2_ref, s2_ref, sel_ref, out_hbm, est_hbm, out_ref, est_ref, sems
):
    gx, gz = lax.axis_index("gx"), lax.axis_index("gz")
    even = gx % 2 == 0
    zero = jnp.zeros((XPAY, NX), F32)
    right = jnp.where(gx < lax.axis_size("gx") - 1, jnp.where(even, ra_ref[...], rb_ref[...]), zero)
    left = jnp.where(gx > 0, jnp.where(even, rb_ref[...], ra_ref[...]), zero)
    rim1, rim2 = rim1_ref[...], rim2_ref[...]
    from_left = slab_terms(slab_ref[0], left[:40], rim1, rim2, True)
    from_right = slab_terms(slab_ref[1], right[:40], rim1, rim2, False)
    lane = iota((NY, NX), 1)
    faces = jnp.where((lane & 3) < 2, from_right, from_left)

    estimate = coarse_solve(cor_ref, left[40:XPAY], right[40:XPAY])
    lane8 = iota((8, NX), 1)
    rim = (lane < 2) | (lane >= NX - 2)
    step = 4
    for zc in range(CZ):
        z_out = jnp.where(gz == 0, zc, CZ - 1 - zc)
        est_ref[z_out] = roll(estimate, -(zc * 32 + 4), 1)[4:8, 0:CX]
    copies = [pltpu.make_async_copy(est_ref, est_hbm, sems.at[NZ // step])]
    copies[0].start()
    for zc in range(CZ):
        wide = take(estimate, zc * 32 + 4 + (lane8 >> 3))
        fine = jnp.concatenate([jnp.broadcast_to(wide[4 + y : 5 + y], (BLK, NX)) for y in range(CY)], axis=0)
        for i in range(BLK):
            zp = zc * BLK + i
            z = jnp.where(gz == 0, zp, NZ - 1 - zp)
            out_ref[z] = jnp.where(rim, roll(faces, -(4 * zp + 2), 1), s2_ref[zp]) + sel_ref[z] * fine
            if zp % step == step - 1:
                planes = pl.ds(jnp.where(gz == 0, zp + 1 - step, NZ - 1 - zp), step)
                copies.append(pltpu.make_async_copy(out_ref.at[planes], out_hbm.at[planes], sems.at[zp // step]))
                copies[-1].start()
    for copy in copies:
        copy.wait()


def near(values):
    return pltpu.with_memory_space_constraint(values, pltpu.VMEM)


def call(kernel, inputs, outputs, scratch=(), aliases=None, us=0.1, name=None, in_space=pltpu.VMEM, out_spaces=None):
    return pl.pallas_call(
        kernel,
        out_shape=outputs,
        in_specs=[pl.BlockSpec(memory_space=in_space)] * len(inputs),
        out_specs=[pl.BlockSpec(memory_space=v) for v in out_spaces or [pltpu.VMEM] * len(outputs)],
        scratch_shapes=list(scratch),
        input_output_aliases=aliases or {},
        cost_estimate=pl.CostEstimate(flops=int(us * 1e9), bytes_accessed=0, transcendentals=0),
        compiler_params=pltpu.CompilerParams(vmem_limit_bytes=32 * 2**20),
        name=name,
    )(*inputs)


def vmem(*shape):
    return pltpu.VMEM(shape, F32)


def exchange(values, sizes, move):
    nx, ny, nz = sizes
    pairs = []
    for x in range(nx):
        for y in range(ny):
            for z in range(nz):
                a, b, c = move(x, y, z)
                pairs.append(((x * ny + y) * nz + z, (a * ny + b) * nz + c))
    return lax.ppermute(values, ("gx", "gy", "gz"), pairs)


def solution(mesh):
    sizes = (mesh.shape["gx"], mesh.shape["gy"], mesh.shape["gz"])
    nx, ny, nz = sizes

    def swap_z(values):
        return exchange(values, sizes, lambda x, y, z: (x, y, nz - 1 - z))

    def swap_y(values, slots, slot):
        def move(x, y, z):
            b = y + 1 if y % slots == slot else y - 1 if (y - 1) % slots == slot else -1
            return (x, b, z) if 0 <= b < ny else (x ^ 1, y, z)

        return exchange(values, sizes, move)

    def swap_x(values, odd):
        return exchange(values, sizes, lambda x, y, z: ((x + 1 if x % 2 == odd else x - 1) % nx, y, z))

    def body(residual_in, labels, factor, basis, basis_index):
        inputs = [residual_in, labels, factor, basis, basis_index]
        kap, rr, sel, urgent = call(
            first_kernel,
            [pltpu.with_memory_space_constraint(v, pltpu.HBM) for v in inputs],
            [vmem(3, NZ + 1, NY, NX), vmem(NZ, NY, NX), vmem(NZ, NY, NX), vmem(ZURGENT, NX)],
            [
                pltpu.VMEM(labels.shape, jnp.int32),
                pltpu.VMEM(factor.shape, F32),
                pltpu.VMEM(basis.shape, F32),
                pltpu.VMEM(basis_index.shape, jnp.int32),
                pltpu.VMEM((4, BLK, BLK, NX), F32),
                pltpu.VMEM((64, NX), F32),
                pltpu.SemaphoreType.DMA((2,)),
                pltpu.SemaphoreType.DMA((len(PARTS), 3)),
            ],
            us=1.8,
            name="stiffness",
            in_space=pltpu.HBM,
        )
        kap, rr, sel, urgent = near(kap), near(rr), near(sel), near(urgent)
        zu = near(swap_z(urgent))
        payloads = [vmem(YPAY, NX)] * 2
        ya, yb, bulk = call(rows_kernel, [kap, rr], payloads + [vmem(BULK, NX)], name="rows")
        zb = near(swap_z(near(bulk)))
        left, right, ends = call(
            columns_kernel, [kap, rr], [vmem(NY, NX), vmem(NY, NX), vmem(8, NX)], us=0.4, name="columns"
        )
        s1, f, p = call(
            inner_first_kernel,
            [kap, rr],
            [vmem(NZ, NY, NX), vmem(NZ, NY, NX), vmem(3, NZ, NY, NX)],
            us=0.6,
            name="inner_first",
        )
        s1, f, p = near(s1), near(f), near(p)
        s1, s2 = call(
            inner_image_kernel,
            [kap, f, p, s1],
            [vmem(NZ, NY, NX), vmem(NZ, NY, NX)],
            aliases={3: 0},
            us=0.7,
            name="inner_image",
        )
        s1, s2 = near(s1), near(s2)
        sent = call(
            send_rows_kernel,
            [zu, urgent, near(ends), near(ya), near(yb), s2],
            payloads + [vmem(URGENT, NX)] * 3,
            aliases={3: 0, 4: 1},
            us=10.0,
            name="send_rows",
        )
        sent = [near(v) for v in sent]
        first, last = sent[2:], sent[:2]
        first_in = [near(swap_y(v, 3, slot)) for slot, v in enumerate(first)]
        last_in = [near(swap_y(v, 2, slot)) for slot, v in enumerate(last)]
        left, right = call(
            columns_beyond_kernel,
            [near(left), near(right), zb, first[2]],
            [vmem(NY, NX), vmem(NY, NX)],
            aliases={0: 0, 1: 1},
            us=100.0,
            name="columns_beyond",
        )
        xa, xb, left, right, cor = call(
            columns_more_kernel,
            first_in + [first[2], near(left), near(right)],
            [vmem(XPAY, NX), vmem(XPAY, NX), vmem(40, NX), vmem(40, NX), vmem(4, 16, NX)],
            us=1.0,
            name="columns_more",
        )
        xa, xb = near(xa), near(xb)
        vb, va = near(swap_x(xb, 1)), near(swap_x(xa, 0))
        s1, s2 = call(
            outer_kernel,
            [kap, rr, zb, f, p, s1, s2, xa],
            [vmem(NZ, NY, NX), vmem(NZ, NY, NX)],
            [pltpu.VMEM((3, 5, NY, NX), F32), pltpu.VMEM((4, NY, NX), F32), pltpu.VMEM((3, 4, NY, NX), F32)],
            aliases={5: 0, 6: 1},
            us=0.25,
            name="outer",
        )
        s1, s2 = call(
            edge_rows_kernel,
            last + last_in + [near(s1), near(s2)],
            [vmem(NZ, NY, NX), vmem(NZ, NY, NX)],
            aliases={4: 0, 5: 1},
            us=0.4,
            name="edge_rows",
        )
        (slab,) = call(slab_kernel, [near(left), near(right), xa], [vmem(2, 4, 40, NX)], us=0.1, name="slab")
        rim1, rim2 = call(rim_kernel, [near(s1), near(s2)], [vmem(NY, NX), vmem(NY, NX)], us=0.2, name="rim")
        out, estimate = call(
            last_kernel,
            [vb, va, near(slab), near(cor), near(rim1), near(rim2), near(s2), sel],
            [jax.ShapeDtypeStruct((NZ, NY, NX), F32), jax.ShapeDtypeStruct((CZ, CY, CX), F32)],
            [pltpu.VMEM((NZ, NY, NX), F32), pltpu.VMEM((CZ, CY, CX), F32), pltpu.SemaphoreType.DMA((5,))],
            us=1.5,
            name="last",
            out_spaces=[pltpu.HBM, pltpu.HBM],
        )
        return out, estimate

    in_specs = (
        P("gz", "gy", "gx"),
        P("gz", "gy", "gx"),
        P(None, "gz", "gy", "gx"),
        P(),
        P("gz", "gy", "gx"),
    )
    out_specs = (P("gz", "gy", "gx"), P("gz", "gy", "gx"))
    return jax.shard_map(body, mesh=mesh, in_specs=in_specs, out_specs=out_specs, check_vma=False)
```

```python
import math

import jax
import jax.numpy as jnp
from jax import lax
from jax.experimental import pallas as pl
from jax.experimental.pallas import tpu as pltpu
from jax.sharding import PartitionSpec as P

BLK = 8
CITERS = 4
BRICK = (0.6, 1.0, 1.0)
MORTAR = (0.25, 0.3, 0.3)
MASS = 0.05
OMEGA = 0.8
WEIGHT_ONE = 1.0 / (1.05 - 0.95 * math.cos(math.pi / 4))
WEIGHT_TWO = 1.0 / (1.05 + 0.95 * math.cos(math.pi / 4))
SELF = 1.0 + 1.0 + 1.0 / 3.0 + MASS / 3.0
KEEP = 1.0 + WEIGHT_TWO / WEIGHT_ONE - WEIGHT_TWO

NZ, NY, NX = 16, 32, 128
CZ, CY, CX = 2, 4, 16
PARTS = range(2)
F32 = jnp.float32
HIGHEST = lax.Precision.HIGHEST

BULK = 7 * NY + 8
BCOL = 7 * NY
URGENT = 16
ZURGENT = 48
KROWS = 36
GROUP = NZ + 2
RROW = 3 * KROWS
YPAY = 128
XPAY = 40 + 8
RLANE = 110


def iota(shape, dim):
    return lax.broadcasted_iota(jnp.int32, shape, dim)


def roll(values, shift, axis):
    size = values.shape[axis]
    shift = shift % size
    return values if shift == 0 else pltpu.roll(values, shift, axis)


def both(values, step, axis):
    return roll(values, step, axis) + roll(values, -step, axis)


def take(values, lanes):
    return jnp.take_along_axis(values, lanes, axis=1, mode="promise_in_bounds")


def pair_stiffness(own, below, above):
    k0, k1, k2 = own
    d0, d1, d2 = (a + b if a is not None else b for a, b in zip(below, above))
    part_y = 0.5 * k1 + 0.125 * (d0 + d1)
    part_yx = 0.125 * (k1 + k2) + (1.0 / 24.0) * (d0 + d1 + d2)
    part_0 = 0.5 * d0
    part_x = 0.5 * k2 + 0.125 * (d0 + d2)
    return part_0, part_y, part_x, part_yx


def first_kernel(
    r_hbm, lab_hbm, fac_hbm, bas_hbm, bix_hbm, kap_ref, rr_ref, sel_ref, urgent_ref,
    lab_ref, fac_ref, bas_ref, bix_ref, tile_ref, sum_ref, sems, more_sems
):
    gz = lax.axis_index("gz")
    parts = []
    small = [
        pltpu.make_async_copy(bas_hbm, bas_ref, sems.at[0]),
        pltpu.make_async_copy(bix_hbm, bix_ref, sems.at[1]),
    ]
    for copy in small:
        copy.start()
    step = NZ // len(PARTS)
    for part in PARTS:
        planes = pl.ds(jnp.where(gz == 0, part * step, NZ - step - part * step), step)
        parts.append(
            [
                pltpu.make_async_copy(lab_hbm.at[planes], lab_ref.at[planes], more_sems.at[part, 0]),
                pltpu.make_async_copy(fac_hbm.at[:, planes], fac_ref.at[:, planes], more_sems.at[part, 1]),
                pltpu.make_async_copy(r_hbm.at[planes], rr_ref.at[planes], more_sems.at[part, 2]),
            ]
        )
        for copy in parts[part]:
            copy.start()
    kap_ref[:, 0] = jnp.zeros((3, NY, NX), F32)
    for copy in small:
        copy.wait()
    tiled = lax.dot_general(
        bas_ref[...].reshape(4 * BLK * BLK, BLK),
        ((iota((BLK, NX), 1) & (BLK - 1)) == iota((BLK, NX), 0)).astype(F32),
        (((1,), (0,)), ((), ())),
        precision=HIGHEST,
        preferred_element_type=F32,
    )
    tile_ref[...] = tiled.reshape(4, BLK, BLK, NX)
    edges = [None] * 7
    spread = ((iota((CX, NX), 1) >> 3) == iota((CX, NX), 0)).astype(F32)
    indices = []
    for zc in range(CZ):
        index = lax.dot_general(
            bix_ref[jnp.where(gz == 0, zc, CZ - 1 - zc)].astype(F32),
            spread,
            (((1,), (0,)), ((), ())),
            precision=HIGHEST,
            preferred_element_type=F32,
        )
        indices.append(jnp.concatenate([jnp.broadcast_to(index[y : y + 1], (BLK, NX)) for y in range(CY)], axis=0))
    for zc in range(CZ):
        index = indices[zc]
        sums = [None] * 4
        for i in range(BLK):
            zp = zc * BLK + i
            if zp % step == 0:
                for copy in parts[zp // step]:
                    copy.wait()
            z = jnp.where(gz == 0, zp, NZ - 1 - zp)
            zi = jnp.where(gz == 0, i, BLK - 1 - i)
            mortar = lab_ref[z] == 1
            b0, b1, b2, b3 = (jnp.concatenate([tile_ref[n, zi]] * CY, axis=0) for n in range(4))
            basis = jnp.where(index < 1.5, jnp.where(index < 0.5, b0, b1), jnp.where(index < 2.5, b2, b3))
            res = rr_ref[z]
            sel_ref[z] = basis
            terms = []
            for a in range(3):
                k = jnp.where(mortar, MORTAR[a], BRICK[a]) * fac_ref[a, z]
                kap_ref[a, zp + 1] = k
                terms.append(k)
                if zp >= NZ - 2:
                    plane = 2 * a + NZ - 1 - zp
                    edges[plane] = k
            if zp == NZ - 1:
                edges[6] = res
            terms.append(basis * res)
            sums = [t if s is None else s + t for s, t in zip(sums, terms)]
        for q in range(4):
            total = sums[q].reshape(CY, BLK, NX).sum(axis=1)
            total = total if q == 3 else total * (1.0 / BLK**3)
            at = (q * 2 + zc) * 8
            sum_ref[at : at + CY] = total
            sum_ref[at + CY : at + 8] = total
    gather = ((iota((NX, NX), 0) >> 3) == (iota((NX, NX), 1) & (CX - 1))).astype(jnp.bfloat16)
    rest, bricks = sum_ref[...], None
    for _ in range(3):
        part = rest.astype(jnp.bfloat16)
        rest = rest - part.astype(F32)
        term = lax.dot_general(part, gather, (((1,), (0,)), ((), ())), preferred_element_type=F32)
        bricks = term if bricks is None else bricks + term
    group = iota((8, NX), 1) >> 4
    coarse = bricks[0:8]
    for g in range(1, 8):
        coarse = jnp.where(group == g, bricks[g * 8 : g * 8 + 8], coarse)
    urgent_ref[0:8] = coarse
    row = iota((8, NX), 0)

    def ends(plane):
        return jnp.where(row < 4, plane[:8], plane[NY - 8 :])

    left, right = columns_beyond(
        jnp.zeros((8, NX), F32), jnp.zeros((8, NX), F32), lambda g, x0: roll(ends(edges[g]), x0, 1)
    )
    urgent_ref[8:16] = end_tile(left, right)
    for g, plane in enumerate(edges):
        a, beyond = divmod(g, 2)
        for inner in range(2) if g < 6 else (1,):
            at = 12 if g == 6 else 4 * a + 2 * inner + beyond
            urgent_ref[16 + at : 17 + at] = plane[0:1] if inner else plane[1:2]
            urgent_ref[32 + at : 33 + at] = plane[NY - 1 : NY] if inner else plane[NY - 2 : NY - 1]


def end_tile(left, right):
    row = iota((8, NX), 0)
    low = jnp.where(row < 2, left, roll(right, 2, 0))
    high = jnp.where(row < 6, roll(left, -2, 0), right)
    return jnp.where(row < 4, low, high)


def place(zp):
    return jnp.where(lax.axis_index("gz") == 0, zp, NZ - 1 - zp)


def rows_kernel(kap_ref, rr_ref, ya_ref, yb_ref, bulk_ref):
    even = lax.rem(lax.axis_index("gy"), 2) == 0

    def put(at, low, high):
        ya_ref[at : at + 1] = jnp.where(even, high, low)
        yb_ref[at : at + 1] = jnp.where(even, low, high)

    for zp in range(NZ):
        for a in range(3):
            at = a * KROWS + zp
            put(at, kap_ref[a, zp + 1, 1:2], kap_ref[a, zp + 1, NY - 2 : NY - 1])
            put(at + GROUP, kap_ref[a, zp + 1, 0:1], kap_ref[a, zp + 1, NY - 1 : NY])
        put(RROW + zp, rr_ref[place(zp), 0:1], rr_ref[place(zp), NY - 1 : NY])
    for a in range(3):
        for s in range(2):
            bulk_ref[(2 * a + s) * NY : (2 * a + s + 1) * NY] = kap_ref[a, NZ - s]
    bulk_ref[6 * NY : 7 * NY] = rr_ref[place(NZ - 1)]
    planes = [kap_ref[a, NZ - s] for a in range(3) for s in range(2)] + [rr_ref[place(NZ - 1)]]
    lane = iota((NY, NX), 1)
    columns = jnp.zeros((NY, NX), F32)
    for g, plane in enumerate(planes):
        columns = jnp.where(lane >= 4 * g, roll(plane, 4 * g + 2, 1), columns)
    lane = iota((8, NX), 1)
    folded = columns[:8]
    for i in range(1, NY // 8):
        folded = jnp.where(lane >= 32 * i, roll(columns[8 * i : 8 * i + 8], 32 * i, 1), folded)
    bulk_ref[BCOL:BULK] = folded


def columns_kernel(kap_ref, rr_ref, left_ref, right_ref, ends_ref):
    lane = iota((NY, NX), 1)
    left = jnp.zeros((NY, NX), F32)
    right = jnp.zeros((NY, NX), F32)
    for a in range(3):
        for zp in range(NZ):
            at = 2 + a * KROWS + 2 * zp
            moved = roll(kap_ref[a, zp + 1], at, 1)
            left = jnp.where(lane >= at, moved, left)
            right = jnp.where(lane >= at - 2, moved, right)
    for zp in range(NZ):
        at = RLANE + zp
        moved = roll(rr_ref[place(zp)], at, 1)
        left = jnp.where(lane >= at, moved, left)
        right = jnp.where(lane >= at - 1, moved, right)
    left_ref[...] = left
    right_ref[...] = right
    row = iota((8, NX), 0)
    ends_ref[...] = end_tile(*(jnp.where(row < 4, v[:8], v[NY - 8 :]) for v in (left, right)))


def columns_beyond(left, right, moved):
    lane = iota(left.shape, 1)
    for a in range(3):
        for s in range(2):
            at = 2 + a * KROWS + 2 * (NZ + s)
            values = moved(2 * a + s, at)
            left = jnp.where((lane == at) | (lane == at + 1), values, left)
            right = jnp.where((lane == at - 2) | (lane == at - 1), values, right)
    at = RLANE + NZ
    values = moved(6, at)
    return jnp.where(lane == at, values, left), jnp.where(lane == at - 1, values, right)


def columns_beyond_kernel(left_in, right_in, bulk_ref, after_ref, left_ref, right_ref):
    folded = bulk_ref[BCOL:BULK]
    columns = jnp.concatenate([roll(folded, -32 * i, 1) for i in range(NY // 8)], axis=0)
    left_ref[...], right_ref[...] = columns_beyond(
        left_in[...], right_in[...], lambda g, x0: roll(columns, x0 - 4 * g - 2, 1)
    )


def send_rows_kernel(far_ref, mine_ref, ends_ref, ya_in, yb_in, after_ref, ya_ref, yb_ref, u0_ref, u1_ref, u2_ref):
    phase = lax.rem(lax.axis_index("gy"), 3)
    row, lane = iota((8, NX), 0), iota((8, NX), 1)
    low, high = far_ref[16:32], far_ref[32:48]
    even = lax.rem(lax.axis_index("gy"), 2) == 0
    for ref, rows in ((ya_ref, jnp.where(even, high, low)), (yb_ref, jnp.where(even, low, high))):
        for i in range(6):
            ref[i * GROUP + NZ : (i + 1) * GROUP] = rows[2 * i : 2 * i + 2]
        ref[RROW + NZ : RROW + NZ + 1] = rows[12:13]
    is_right = ((row >> 1) & 1) == 1
    at = lane - jnp.where(is_right, 0, 2)
    within = at - jnp.where(at >= 2 * KROWS, 2 * KROWS, jnp.where(at >= KROWS, KROWS, 0))
    beyond = (at < RROW) & (within >= 2 * NZ)
    beyond = beyond | (lane == RLANE + NZ - is_right.astype(jnp.int32))
    tile = jnp.where(beyond, far_ref[8:16], ends_ref[...])
    turned = roll(tile, 4, 0)
    coarse = jnp.where(row < CY, mine_ref[0:8], far_ref[0:8])
    for slot, ref in enumerate((u0_ref, u1_ref, u2_ref)):
        ref[0:8] = coarse
        ref[8:16] = jnp.where(phase == slot, turned, tile)


def neighbours(slots):
    gy = lax.axis_index("gy")
    phase = lax.rem(gy, 3)
    zero = jnp.zeros(slots[0].shape, F32)
    hi = jnp.where(phase == 0, slots[0], jnp.where(phase == 1, slots[1], slots[2]))
    lo = jnp.where(phase == 0, slots[2], jnp.where(phase == 1, slots[0], slots[1]))
    return jnp.where(gy > 0, lo, zero), jnp.where(gy < lax.axis_size("gy") - 1, hi, zero)


def columns_more_kernel(r0_ref, r1_ref, r2_ref, mine_ref, left_in, right_in, xa_ref, xb_ref, left_ref, right_ref, cor_ref):
    gx = lax.axis_index("gx")
    lo, hi = neighbours([r0_ref[...], r1_ref[...], r2_ref[...]])
    lane, row = iota((8, NX), 1), iota((8, NX), 0)

    def halo(shift):
        above, below = roll(hi[8:16], -shift, 0), roll(lo[8:16], 6 - shift, 0)
        return jnp.where(row < 2, above, jnp.where(row >= 6, below, 0.0))

    left_ref[0:NY] = left_in[...]
    right_ref[0:NY] = right_in[...]
    left_ref[NY : NY + 8] = halo(0)
    right_ref[NY : NY + 8] = halo(2)
    even_x = gx % 2 == 0
    xa_ref[0:40] = jnp.where(even_x, right_ref[...], left_ref[...])
    xb_ref[0:40] = jnp.where(even_x, left_ref[...], right_ref[...])

    tiles = [lo[0:8], mine_ref[0:8], hi[0:8]]
    zc, xs = lane >> 5, lane & 31
    pair = jnp.where(zc < 2, zc, 3 - zc)
    own = (xs >= 4) & (xs < 20)
    low_half = lane < 64
    sides = [jnp.zeros((8, NX), F32), jnp.zeros((8, NX), F32)]
    for q in range(4):
        at = (q * 2 + pair) * CX + jnp.clip(xs - 4, 0, CX - 1)
        below, mine, above = ((v, roll(v, 4, 0)) for v in (jnp.where(own, take(t, at), 0.0) for t in tiles))
        first = jnp.where(row < 4, jnp.where(low_half, below[0], below[1]), jnp.where(low_half, mine[1], mine[0]))
        second = jnp.where(row < 4, jnp.where(low_half, above[0], above[1]), 0.0)
        whole = jnp.concatenate([first, second], axis=0)
        cor_ref[q] = whole
        for i, start in enumerate((4, CX)):
            for half, to in ((first, 4 * q), (second, 4 * q + 16)):
                sides[i] = jnp.where((xs >= to) & (xs < to + 4), roll(half, to - start, 1), sides[i])
    xa_ref[40:XPAY] = jnp.where(even_x, sides[1], sides[0])
    xb_ref[40:XPAY] = jnp.where(even_x, sides[0], sides[1])


def first_plane(to, zp, kap_ref, res, f_ref, p_ref, s1_ref, rim):
    below, k, above = ([kap_ref[a, zp + i] for a in range(3)] for i in range(3))
    part_0, part_y, part_x, part_yx = pair_stiffness(k, below, above)
    diag = SELF * (k[0] + k[1] + k[2]) + part_0 + both(part_y, 1, 0)
    inv = 1.0 / (diag + both(part_x + both(part_yx, 1, 0), 1, 1))
    f = jnp.where(rim, 0.0, WEIGHT_ONE * res * inv)
    f_ref[zp + 1] = f
    for a in range(3):
        p_ref[a, zp + 1] = k[a] * f
    if to < NZ if isinstance(to, int) else True:
        s1_ref[to] = WEIGHT_TWO * inv


def image_plane(to, zp, kap_ref, f_ref, p_ref, s1_ref, s2_ref, rim):
    k = [kap_ref[a, zp + 1] for a in range(3)]
    p = [p_ref[a, zp + 1] for a in range(3)]
    d0, d1, d2 = (p_ref[a, zp] + p_ref[a, zp + 2] for a in range(3))
    f, fz = f_ref[zp + 1], f_ref[zp] + f_ref[zp + 2]
    own_y = 0.5 * p[1] + 0.125 * (d0 + d1)
    own_yx = 0.125 * (p[1] + p[2]) + (1.0 / 24.0) * (d0 + d1 + d2)
    own_x = 0.5 * p[2] + 0.125 * (d0 + d2)
    fy, fyz = both(f, 1, 0), both(fz, 1, 0)
    t24, t8 = (1.0 / 24.0) * fyz, 0.125 * fyz
    total = 0.5 * d0 + both(own_y, 1, 0) + both(own_x + both(own_yx, 1, 0), 1, 1)
    total = total + k[0] * (0.5 * fz + t8 + both(0.125 * fz + t24, 1, 1))
    total = total + k[1] * (0.5 * fy + t8 + both(0.125 * fy + t24, 1, 1))
    total = total + k[2] * both(0.5 * f + 0.125 * (fz + fy) + t24, 1, 1)
    scaled = s1_ref[to]
    s1_ref[to] = jnp.where(rim, total, scaled)
    s2_ref[to] = jnp.where(rim, 0.0, KEEP * f + scaled * total)


def plane_rim():
    row, lane = iota((NY, NX), 0), iota((NY, NX), 1)
    return (row == 0) | (row == NY - 1) | (lane == 0) | (lane == NX - 1)


def inner_first_kernel(kap_ref, rr_ref, s1_ref, f_ref, p_ref):
    rim = plane_rim()
    f_ref[0] = jnp.zeros((NY, NX), F32)
    p_ref[:, 0] = jnp.zeros((3, NY, NX), F32)

    @pl.loop(0, 3)
    def _(i):
        for j in range(5):
            zp = i * 5 + j
            first_plane(zp, zp, kap_ref, rr_ref[place(zp)], f_ref, p_ref, s1_ref, rim)


def inner_image_kernel(kap_ref, f_ref, p_ref, s1_in, s1_ref, s2_ref):
    rim = plane_rim()

    @pl.loop(0, 2)
    def _(i):
        for j in range(7):
            image_plane(i * 7 + j, i * 7 + j, kap_ref, f_ref, p_ref, s1_ref, s2_ref, rim)


def outer_kernel(kap_ref, rr_ref, bulk_ref, f_in, p_in, s1_in, s2_in, after_ref, s1_ref, s2_ref, k_ref, f_ref, p_ref):
    rim = plane_rim()
    for a in range(3):
        for i in range(3):
            k_ref[a, i] = kap_ref[a, NZ - 2 + i]
        for i in range(2):
            k_ref[a, 3 + i] = bulk_ref[(2 * a + i) * NY : (2 * a + i + 1) * NY]
            p_ref[a, i] = p_in[a, NZ - 2 + i]
    for i in range(2):
        f_ref[i] = f_in[NZ - 2 + i]
    first_plane(NZ - 1, 1, k_ref, rr_ref[place(NZ - 1)], f_ref, p_ref, s1_ref, rim)
    first_plane(NZ, 2, k_ref, bulk_ref[6 * NY : 7 * NY], f_ref, p_ref, s1_ref, rim)
    for i in range(2):
        image_plane(NZ - 2 + i, i, k_ref, f_ref, p_ref, s1_ref, s2_ref, rim)


def along_x(values):
    return both(values, 1, 1)


def edge_rows_kernel(ya_ref, yb_ref, ra_ref, rb_ref, s1_in, s2_in, s1_ref, s2_ref):
    size = 24
    row, lane = iota((size, NX), 0), iota((size, NX), 1)
    inner = (lane > 0) & (lane < NX - 1)
    near = inner & (row < NZ + 1)
    inner16 = inner[:NZ]
    gy = lax.axis_index("gy")
    even = lax.rem(gy, 2) == 0
    ya, yb, ra, rb = ya_ref[...], yb_ref[...], ra_ref[...], rb_ref[...]
    low, high = jnp.where(even, yb, ya), jnp.where(even, ya, yb)
    zero = jnp.zeros((YPAY, NX), F32)
    lo = jnp.where(gy > 0, jnp.where(even, rb, ra), zero)
    hi = jnp.where(gy < lax.axis_size("gy") - 1, jnp.where(even, ra, rb), zero)
    for other, mine, face, second in (
        (lo, low, 0, 1),
        (hi, high, NY - 1, NY - 2),
    ):

        def group(source, at):
            return jnp.where(row < GROUP, source[at : at + size], 0.0)

        k = [[group(other, a * KROWS + s * GROUP) for a in range(3)] for s in (0, 1)]
        k += [[group(mine, a * KROWS + s * GROUP) for a in range(3)] for s in (1, 0)]
        parts = [pair_stiffness(v, (None, None, None), [both(u, 1, 0) for u in v]) for v in k]
        res = [None] + [jnp.where(row < NZ + 1, v[YPAY - size :], 0.0) for v in (roll(other, 4 - 8, 0), roll(mine, 4 - 8, 0))]
        f, inv = [None] * 3, [None] * 3
        for c in (1, 2):
            diag = SELF * (k[c][0] + k[c][1] + k[c][2]) + parts[c][0] + parts[c - 1][1] + parts[c + 1][1]
            inv[c] = 1.0 / (diag + along_x(parts[c][2] + parts[c - 1][3] + parts[c + 1][3]))
            f[c] = jnp.where(near, WEIGHT_ONE * res[c] * inv[c], 0.0)
        p = [None] + [[v * f[c] for v in k[c]] for c in (1, 2)]
        d = [None] + [[both(v, 1, 0) for v in p[c]] for c in (1, 2)]
        fz = [None] + [both(f[c], 1, 0) for c in (1, 2)]

        def row_parts(c):
            return (
                0.5 * p[c][1] + 0.125 * (d[c][0] + d[c][1]),
                0.125 * (p[c][1] + p[c][2]) + (1.0 / 24.0) * (d[c][0] + d[c][1] + d[c][2]),
            )

        own_y, own_yx = row_parts(1)
        own_x = 0.5 * p[2][2] + 0.125 * (d[2][0] + d[2][2])
        t24, t8 = (1.0 / 24.0) * fz[1], 0.125 * fz[1]
        total = 0.5 * d[2][0] + own_y + along_x(own_x + own_yx)
        total = total + k[2][0] * (0.5 * fz[2] + t8 + along_x(0.125 * fz[2] + t24))
        total = total + k[2][1] * (0.5 * f[1] + t8 + along_x(0.125 * f[1] + t24))
        total = total + k[2][2] * along_x(0.5 * f[2] + 0.125 * (fz[2] + f[1]) + t24)
        total = total[:NZ] + s1_ref[:, face, :]
        scaled = WEIGHT_TWO * inv[2][:NZ]
        s1_ref[:, face, :] = jnp.where(inner16, scaled, total)
        s2_ref[:, face, :] = jnp.where(inner16, KEEP * f[2][:NZ] + scaled * total, 0.0)

        own_y, own_yx = row_parts(2)
        t24, t8 = (1.0 / 24.0) * fz[2], 0.125 * fz[2]
        total = own_y + along_x(own_yx) + k[3][0] * (t8 + along_x(t24))
        total = total + k[3][1] * (0.5 * f[2] + t8 + along_x(0.125 * f[2] + t24))
        total = (total + k[3][2] * along_x(0.125 * f[2] + t24))[:NZ]
        scaled = s1_ref[:, second, :]
        s1_ref[:, second, :] = jnp.where(inner16, scaled, scaled + total)
        s2_ref[:, second, :] = s2_ref[:, second, :] + jnp.where(inner16, scaled * total, 0.0)


def slab_lanes(left):
    lane = iota((8, NX), 1)
    zp, c = lane >> 2, lane & 3
    outer = c < 2 if left else c >= 2
    real = zp < GROUP
    near = ((c == 1) | (c == 2)) & (zp < NZ + 1)
    offset = jnp.where(outer, 0, 2) if left else jnp.where(outer, 2, 0)
    offset_r = jnp.where(outer, RLANE - 1, RLANE) if left else jnp.where(outer, RLANE, RLANE - 1)
    sources = [jnp.where(real, a * KROWS + 2 * zp + (c & 1) + offset, 0) for a in range(3)]
    sources.append(jnp.where(near, zp + offset_r, 0))
    return outer, [real] * 3 + [near], sources


def slab_kernel(left_ref, right_ref, after_ref, slab_ref):
    for side, pack in enumerate((left_ref, right_ref)):
        outer, keeps, sources = slab_lanes(side == 0)
        for q in range(4):
            for i in range(0, NY + 8, 8):
                piece = take(pack[i : i + 8], sources[q])
                slab_ref[side, q, i : i + 8] = jnp.where(keeps[q] & ~outer, piece, 0.0)


def rim_kernel(s1_ref, s2_ref, rim1_ref, rim2_ref):
    lane = iota((NY, NX), 1)
    for source, rim in ((s1_ref, rim1_ref), (s2_ref, rim2_ref)):
        values = jnp.zeros((NY, NX), F32)
        for zp in range(NZ):
            values = jnp.where(lane >= 4 * zp, roll(source[zp], 4 * zp + 2, 1), values)
        rim[...] = values


def slab_terms(mine, other, rim1, rim2, left):
    rows = NY + 8
    outer, keeps, sources = slab_lanes(left)

    def spread(q):
        pieces = []
        for i in range(0, rows, 8):
            pieces.append(jnp.where(keeps[q] & outer, take(other[i : i + 8], sources[q]), mine[q, i : i + 8]))
        return jnp.concatenate(pieces, axis=0)

    k = [spread(a) for a in range(3)]
    res = spread(3)
    c = iota((rows, NX), 1) & 3
    near = jnp.concatenate([keeps[3]] * (rows // 8), axis=0)

    dz = [both(v, 4, 1) for v in k]
    part_0, part_y, part_x, part_yx = pair_stiffness(k, (None, None, None), dz)
    diag = SELF * (k[0] + k[1] + k[2]) + part_0 + both(part_y, 1, 0)
    inv = 1.0 / (diag + both(part_x + both(part_yx, 1, 0), 1, 1))
    f = jnp.where(near, WEIGHT_ONE * res * inv, 0.0)

    def from_outer(values):
        return roll(values, 1 if left else -1, 1)

    p = [v * f for v in k]
    d0, d1, d2 = (both(v, 4, 1) for v in p)
    own_y = 0.5 * p[1] + 0.125 * (d0 + d1)
    own_yx = 0.125 * (p[1] + p[2]) + (1.0 / 24.0) * (d0 + d1 + d2)
    own_x = 0.5 * p[2] + 0.125 * (d0 + d2)
    fz = both(f, 4, 1)
    fy, fyz = both(f, 1, 0)[:NY], both(fz, 1, 0)[:NY]
    fc, fz = f[:NY], fz[:NY]
    k = [v[:NY] for v in k]
    t24, t8 = (1.0 / 24.0) * fyz, 0.125 * fyz
    total = 0.5 * d0[:NY] + both(own_y, 1, 0)[:NY] + from_outer(own_x[:NY] + both(own_yx, 1, 0)[:NY])
    total = total + k[0] * (0.5 * fz + t8 + from_outer(0.125 * fz + t24))
    total = total + k[1] * (0.5 * fy + t8 + from_outer(0.125 * fy + t24))
    total = total + k[2] * from_outer(0.5 * fc + 0.125 * (fz + fy) + t24)
    face = (c == 2 if left else c == 1)[:NY]
    return jnp.where(face, KEEP * fc + WEIGHT_TWO * inv[:NY] * (total + rim1), rim2 + rim1 * total)


def coarse_solve(cor_ref, lower, upper):
    xs = iota((8, NX), 1) & 31
    arrays = []
    for q in range(4):
        halves = []
        for i, from_ in enumerate((4 * q, 4 * q + 16)):
            half = jnp.where(xs < 4, roll(lower, -from_, 1), cor_ref[q, 8 * i : 8 * i + 8])
            halves.append(jnp.where((xs >= 20) & (xs < 24), roll(upper, 20 - from_, 1), half))
        arrays.append(jnp.concatenate(halves, axis=0))
    kc, rhs = arrays[:3], arrays[3]
    lane = iota((16, NX), 1)

    def sides(values, axis):
        if axis == 0:
            return roll(values, 32, 1), roll(values, -32, 1)
        return roll(values, 1, axis - 1), roll(values, -1, axis - 1)

    within = [(lane >= 32, lane < 96), (None, None), (None, None)]
    diag = (1.0 + MASS / 3.0) * (kc[0] + kc[1] + kc[2])
    couple = []
    for a in range(3):
        for v, real in zip(sides(kc[a], a), within[a]):
            half = 0.5 * v if real is None else jnp.where(real, 0.5 * v, 0.0)
            diag = diag + half
            half = 0.5 * kc[a] + half
            couple.append(half if real is None else jnp.where(real, half, 0.0))
    inside = kc[0] > 0.0
    scaled = jnp.where(inside, OMEGA / jnp.where(inside, diag, 1.0), 0.0)
    couple = [scaled * v for v in couple]
    start = scaled * rhs
    estimate = start
    for _ in range(CITERS - 1):
        t = [v * u for v, u in zip(couple, [u for a in range(3) for u in sides(estimate, a)])]
        estimate = (start + (1.0 - OMEGA) * estimate) + (((t[0] + t[1]) + (t[2] + t[3])) + (t[4] + t[5]))
    return estimate[0:8]


def last_kernel(
    rb_ref, ra_ref, slab_ref, cor_ref, rim1_ref, rim2_ref, s2_ref, sel_ref, out_hbm, est_hbm, out_ref, est_ref, sems
):
    gx, gz = lax.axis_index("gx"), lax.axis_index("gz")
    even = gx % 2 == 0
    zero = jnp.zeros((XPAY, NX), F32)
    right = jnp.where(gx < lax.axis_size("gx") - 1, jnp.where(even, ra_ref[...], rb_ref[...]), zero)
    left = jnp.where(gx > 0, jnp.where(even, rb_ref[...], ra_ref[...]), zero)
    rim1, rim2 = rim1_ref[...], rim2_ref[...]
    from_left = slab_terms(slab_ref[0], left[:40], rim1, rim2, True)
    from_right = slab_terms(slab_ref[1], right[:40], rim1, rim2, False)
    lane = iota((NY, NX), 1)
    faces = jnp.where((lane & 3) < 2, from_right, from_left)

    estimate = coarse_solve(cor_ref, left[40:XPAY], right[40:XPAY])
    lane8 = iota((8, NX), 1)
    rim = (lane < 2) | (lane >= NX - 2)
    step = 4
    for zc in range(CZ):
        z_out = jnp.where(gz == 0, zc, CZ - 1 - zc)
        est_ref[z_out] = roll(estimate, -(zc * 32 + 4), 1)[4:8, 0:CX]
    copies = [pltpu.make_async_copy(est_ref, est_hbm, sems.at[NZ // step])]
    copies[0].start()
    for zc in range(CZ):
        wide = take(estimate, zc * 32 + 4 + (lane8 >> 3))
        fine = jnp.concatenate([jnp.broadcast_to(wide[4 + y : 5 + y], (BLK, NX)) for y in range(CY)], axis=0)
        for i in range(BLK):
            zp = zc * BLK + i
            z = jnp.where(gz == 0, zp, NZ - 1 - zp)
            out_ref[z] = jnp.where(rim, roll(faces, -(4 * zp + 2), 1), s2_ref[zp]) + sel_ref[z] * fine
            if zp % step == step - 1:
                planes = pl.ds(jnp.where(gz == 0, zp + 1 - step, NZ - 1 - zp), step)
                copies.append(pltpu.make_async_copy(out_ref.at[planes], out_hbm.at[planes], sems.at[zp // step]))
                copies[-1].start()
    for copy in copies:
        copy.wait()


def near(values):
    return pltpu.with_memory_space_constraint(values, pltpu.VMEM)


def call(kernel, inputs, outputs, scratch=(), aliases=None, us=0.1, name=None, in_space=pltpu.VMEM, out_spaces=None):
    return pl.pallas_call(
        kernel,
        out_shape=outputs,
        in_specs=[pl.BlockSpec(memory_space=in_space)] * len(inputs),
        out_specs=[pl.BlockSpec(memory_space=v) for v in out_spaces or [pltpu.VMEM] * len(outputs)],
        scratch_shapes=list(scratch),
        input_output_aliases=aliases or {},
        cost_estimate=pl.CostEstimate(flops=int(us * 1e9), bytes_accessed=0, transcendentals=0),
        compiler_params=pltpu.CompilerParams(vmem_limit_bytes=32 * 2**20),
        name=name,
    )(*inputs)


def vmem(*shape):
    return pltpu.VMEM(shape, F32)


def exchange(values, sizes, move):
    nx, ny, nz = sizes
    pairs = []
    for x in range(nx):
        for y in range(ny):
            for z in range(nz):
                a, b, c = move(x, y, z)
                pairs.append(((x * ny + y) * nz + z, (a * ny + b) * nz + c))
    return lax.ppermute(values, ("gx", "gy", "gz"), pairs)


def solution(mesh):
    sizes = (mesh.shape["gx"], mesh.shape["gy"], mesh.shape["gz"])
    nx, ny, nz = sizes

    def swap_z(values):
        return exchange(values, sizes, lambda x, y, z: (x, y, nz - 1 - z))

    def swap_y(values, slots, slot):
        def move(x, y, z):
            b = y + 1 if y % slots == slot else y - 1 if (y - 1) % slots == slot else -1
            return (x, b, z) if 0 <= b < ny else (x ^ 1, y, z)

        return exchange(values, sizes, move)

    def swap_x(values, odd):
        return exchange(values, sizes, lambda x, y, z: ((x + 1 if x % 2 == odd else x - 1) % nx, y, z))

    def body(residual_in, labels, factor, basis, basis_index):
        inputs = [residual_in, labels, factor, basis, basis_index]
        kap, rr, sel, urgent = call(
            first_kernel,
            [pltpu.with_memory_space_constraint(v, pltpu.HBM) for v in inputs],
            [vmem(3, NZ + 1, NY, NX), vmem(NZ, NY, NX), vmem(NZ, NY, NX), vmem(ZURGENT, NX)],
            [
                pltpu.VMEM(labels.shape, jnp.int32),
                pltpu.VMEM(factor.shape, F32),
                pltpu.VMEM(basis.shape, F32),
                pltpu.VMEM(basis_index.shape, jnp.int32),
                pltpu.VMEM((4, BLK, BLK, NX), F32),
                pltpu.VMEM((64, NX), F32),
                pltpu.SemaphoreType.DMA((2,)),
                pltpu.SemaphoreType.DMA((len(PARTS), 3)),
            ],
            us=1.8,
            name="stiffness",
            in_space=pltpu.HBM,
        )
        kap, rr, sel, urgent = near(kap), near(rr), near(sel), near(urgent)
        zu = near(swap_z(urgent))
        payloads = [vmem(YPAY, NX)] * 2
        ya, yb, bulk = call(rows_kernel, [kap, rr], payloads + [vmem(BULK, NX)], name="rows")
        zb = near(swap_z(near(bulk)))
        left, right, ends = call(
            columns_kernel, [kap, rr], [vmem(NY, NX), vmem(NY, NX), vmem(8, NX)], us=0.4, name="columns"
        )
        s1, f, p = call(
            inner_first_kernel,
            [kap, rr],
            [vmem(NZ, NY, NX), vmem(NZ, NY, NX), vmem(3, NZ, NY, NX)],
            us=0.6,
            name="inner_first",
        )
        s1, f, p = near(s1), near(f), near(p)
        s1, s2 = call(
            inner_image_kernel,
            [kap, f, p, s1],
            [vmem(NZ, NY, NX), vmem(NZ, NY, NX)],
            aliases={3: 0},
            us=0.7,
            name="inner_image",
        )
        s1, s2 = near(s1), near(s2)
        sent = call(
            send_rows_kernel,
            [zu, urgent, near(ends), near(ya), near(yb), s2],
            payloads + [vmem(URGENT, NX)] * 3,
            aliases={3: 0, 4: 1},
            us=10.0,
            name="send_rows",
        )
        sent = [near(v) for v in sent]
        first, last = sent[2:], sent[:2]
        first_in = [near(swap_y(v, 3, slot)) for slot, v in enumerate(first)]
        last_in = [near(swap_y(v, 2, slot)) for slot, v in enumerate(last)]
        left, right = call(
            columns_beyond_kernel,
            [near(left), near(right), zb, first[2]],
            [vmem(NY, NX), vmem(NY, NX)],
            aliases={0: 0, 1: 1},
            us=100.0,
            name="columns_beyond",
        )
        xa, xb, left, right, cor = call(
            columns_more_kernel,
            first_in + [first[2], near(left), near(right)],
            [vmem(XPAY, NX), vmem(XPAY, NX), vmem(40, NX), vmem(40, NX), vmem(4, 16, NX)],
            us=1.0,
            name="columns_more",
        )
        xa, xb = near(xa), near(xb)
        vb, va = near(swap_x(xb, 1)), near(swap_x(xa, 0))
        s1, s2 = call(
            outer_kernel,
            [kap, rr, zb, f, p, s1, s2, xa],
            [vmem(NZ, NY, NX), vmem(NZ, NY, NX)],
            [pltpu.VMEM((3, 5, NY, NX), F32), pltpu.VMEM((4, NY, NX), F32), pltpu.VMEM((3, 4, NY, NX), F32)],
            aliases={5: 0, 6: 1},
            us=0.25,
            name="outer",
        )
        s1, s2 = call(
            edge_rows_kernel,
            last + last_in + [near(s1), near(s2)],
            [vmem(NZ, NY, NX), vmem(NZ, NY, NX)],
            aliases={4: 0, 5: 1},
            us=0.4,
            name="edge_rows",
        )
        (slab,) = call(slab_kernel, [near(left), near(right), xa], [vmem(2, 4, 40, NX)], us=0.1, name="slab")
        rim1, rim2 = call(rim_kernel, [near(s1), near(s2)], [vmem(NY, NX), vmem(NY, NX)], us=0.2, name="rim")
        out, estimate = call(
            last_kernel,
            [vb, va, near(slab), near(cor), near(rim1), near(rim2), near(s2), sel],
            [jax.ShapeDtypeStruct((NZ, NY, NX), F32), jax.ShapeDtypeStruct((CZ, CY, CX), F32)],
            [pltpu.VMEM((NZ, NY, NX), F32), pltpu.VMEM((CZ, CY, CX), F32), pltpu.SemaphoreType.DMA((5,))],
            us=1.5,
            name="last",
            out_spaces=[pltpu.HBM, pltpu.HBM],
        )
        return out, estimate

    in_specs = (
        P("gz", "gy", "gx"),
        P("gz", "gy", "gx"),
        P(None, "gz", "gy", "gx"),
        P(),
        P("gz", "gy", "gx"),
    )
    out_specs = (P("gz", "gy", "gx"), P("gz", "gy", "gx"))
    return jax.shard_map(body, mesh=mesh, in_specs=in_specs, out_specs=out_specs, check_vma=False)
```

```python
import math

import jax
import jax.numpy as jnp
from jax import lax
from jax.experimental import pallas as pl
from jax.experimental.pallas import tpu as pltpu
from jax.sharding import PartitionSpec as P

BLK = 8
CITERS = 4
BRICK = (0.6, 1.0, 1.0)
MORTAR = (0.25, 0.3, 0.3)
MASS = 0.05
OMEGA = 0.8
WEIGHT_ONE = 1.0 / (1.05 - 0.95 * math.cos(math.pi / 4))
WEIGHT_TWO = 1.0 / (1.05 + 0.95 * math.cos(math.pi / 4))
SELF = 1.0 + 1.0 + 1.0 / 3.0 + MASS / 3.0
KEEP = 1.0 + WEIGHT_TWO / WEIGHT_ONE - WEIGHT_TWO

NZ, NY, NX = 16, 32, 128
CZ, CY, CX = 2, 4, 16
PARTS = range(2)
F32 = jnp.float32
HIGHEST = lax.Precision.HIGHEST

BULK = 5 * NY + 8
BCOL = 5 * NY
URGENT = 16
ZURGENT = 48
KROWS = 36
GROUP = NZ + 2
RROW = 3 * KROWS
YPAY = 128
XPAY = 40 + 8
RLANE = 110


def iota(shape, dim):
    return lax.broadcasted_iota(jnp.int32, shape, dim)


def roll(values, shift, axis):
    size = values.shape[axis]
    shift = shift % size
    return values if shift == 0 else pltpu.roll(values, shift, axis)


def both(values, step, axis):
    return roll(values, step, axis) + roll(values, -step, axis)


def take(values, lanes):
    return jnp.take_along_axis(values, lanes, axis=1, mode="promise_in_bounds")


def pair_stiffness(own, below, above):
    k0, k1, k2 = own
    d0, d1, d2 = (a + b if a is not None else b for a, b in zip(below, above))
    part_y = 0.5 * k1 + 0.125 * (d0 + d1)
    part_yx = 0.125 * (k1 + k2) + (1.0 / 24.0) * (d0 + d1 + d2)
    part_0 = 0.5 * d0
    part_x = 0.5 * k2 + 0.125 * (d0 + d2)
    return part_0, part_y, part_x, part_yx


def first_kernel(
    r_hbm, lab_hbm, fac_hbm, bas_hbm, bix_hbm, kap_ref, rr_ref, sel_ref, urgent_ref,
    lab_ref, fac_ref, bas_ref, bix_ref, tile_ref, sum_ref, sems, more_sems
):
    gz = lax.axis_index("gz")
    parts = []
    small = [
        pltpu.make_async_copy(bas_hbm, bas_ref, sems.at[0]),
        pltpu.make_async_copy(bix_hbm, bix_ref, sems.at[1]),
    ]
    for copy in small:
        copy.start()
    step = NZ // len(PARTS)
    for part in PARTS:
        planes = pl.ds(jnp.where(gz == 0, part * step, NZ - step - part * step), step)
        parts.append(
            [
                pltpu.make_async_copy(lab_hbm.at[planes], lab_ref.at[planes], more_sems.at[part, 0]),
                pltpu.make_async_copy(fac_hbm.at[:, planes], fac_ref.at[:, planes], more_sems.at[part, 1]),
                pltpu.make_async_copy(r_hbm.at[planes], rr_ref.at[planes], more_sems.at[part, 2]),
            ]
        )
        for copy in parts[part]:
            copy.start()
    kap_ref[:, 0] = jnp.zeros((3, NY, NX), F32)
    for copy in small:
        copy.wait()
    tiled = lax.dot_general(
        bas_ref[...].reshape(4 * BLK * BLK, BLK),
        ((iota((BLK, NX), 1) & (BLK - 1)) == iota((BLK, NX), 0)).astype(F32),
        (((1,), (0,)), ((), ())),
        precision=HIGHEST,
        preferred_element_type=F32,
    )
    tile_ref[...] = tiled.reshape(4, BLK, BLK, NX)
    edges = [None] * 7
    spread = ((iota((CX, NX), 1) >> 3) == iota((CX, NX), 0)).astype(F32)
    indices = []
    for zc in range(CZ):
        index = lax.dot_general(
            bix_ref[jnp.where(gz == 0, zc, CZ - 1 - zc)].astype(F32),
            spread,
            (((1,), (0,)), ((), ())),
            precision=HIGHEST,
            preferred_element_type=F32,
        )
        indices.append(jnp.concatenate([jnp.broadcast_to(index[y : y + 1], (BLK, NX)) for y in range(CY)], axis=0))
    for zc in range(CZ):
        index = indices[zc]
        sums = [None] * 4
        for i in range(BLK):
            zp = zc * BLK + i
            if zp % step == 0:
                for copy in parts[zp // step]:
                    copy.wait()
            z = jnp.where(gz == 0, zp, NZ - 1 - zp)
            zi = jnp.where(gz == 0, i, BLK - 1 - i)
            mortar = lab_ref[z] == 1
            b0, b1, b2, b3 = (jnp.concatenate([tile_ref[n, zi]] * CY, axis=0) for n in range(4))
            basis = jnp.where(index < 1.5, jnp.where(index < 0.5, b0, b1), jnp.where(index < 2.5, b2, b3))
            res = rr_ref[z]
            sel_ref[z] = basis
            terms = []
            for a in range(3):
                k = jnp.where(mortar, MORTAR[a], BRICK[a]) * fac_ref[a, z]
                kap_ref[a, zp + 1] = k
                terms.append(k)
                if zp >= NZ - 2:
                    plane = 2 * a + NZ - 1 - zp
                    edges[plane] = k
            if zp == NZ - 1:
                edges[6] = res
            terms.append(basis * res)
            sums = [t if s is None else s + t for s, t in zip(sums, terms)]
        for q in range(4):
            total = sums[q].reshape(CY, BLK, NX).sum(axis=1)
            total = total if q == 3 else total * (1.0 / BLK**3)
            at = (q * 2 + zc) * 8
            sum_ref[at : at + CY] = total
            sum_ref[at + CY : at + 8] = total
    gather = ((iota((NX, NX), 0) >> 3) == (iota((NX, NX), 1) & (CX - 1))).astype(jnp.bfloat16)
    rest, bricks = sum_ref[...], None
    for _ in range(3):
        part = rest.astype(jnp.bfloat16)
        rest = rest - part.astype(F32)
        term = lax.dot_general(part, gather, (((1,), (0,)), ((), ())), preferred_element_type=F32)
        bricks = term if bricks is None else bricks + term
    group = iota((8, NX), 1) >> 4
    coarse = bricks[0:8]
    for g in range(1, 8):
        coarse = jnp.where(group == g, bricks[g * 8 : g * 8 + 8], coarse)
    urgent_ref[0:8] = coarse
    row = iota((8, NX), 0)

    def ends(plane):
        return jnp.where(row < 4, plane[:8], plane[NY - 8 :])

    left, right = columns_beyond(
        jnp.zeros((8, NX), F32), jnp.zeros((8, NX), F32), lambda g, x0: roll(ends(edges[g]), x0, 1)
    )
    urgent_ref[8:16] = end_tile(left, right)
    for g, plane in enumerate(edges):
        a, beyond = divmod(g, 2)
        for inner in range(2) if g < 6 else (1,):
            at = 12 if g == 6 else 4 * a + 2 * inner + beyond
            urgent_ref[16 + at : 17 + at] = plane[0:1] if inner else plane[1:2]
            urgent_ref[32 + at : 33 + at] = plane[NY - 1 : NY] if inner else plane[NY - 2 : NY - 1]


def end_tile(left, right):
    row = iota((8, NX), 0)
    low = jnp.where(row < 2, left, roll(right, 2, 0))
    high = jnp.where(row < 6, roll(left, -2, 0), right)
    return jnp.where(row < 4, low, high)


def place(zp):
    return jnp.where(lax.axis_index("gz") == 0, zp, NZ - 1 - zp)


def rows_kernel(kap_ref, rr_ref, ya_ref, yb_ref, bulk_ref):
    even = lax.rem(lax.axis_index("gy"), 2) == 0

    def put(at, low, high):
        ya_ref[at : at + 1] = jnp.where(even, high, low)
        yb_ref[at : at + 1] = jnp.where(even, low, high)

    for zp in range(NZ):
        for a in range(3):
            at = a * KROWS + zp
            put(at, kap_ref[a, zp + 1, 1:2], kap_ref[a, zp + 1, NY - 2 : NY - 1])
            put(at + GROUP, kap_ref[a, zp + 1, 0:1], kap_ref[a, zp + 1, NY - 1 : NY])
        put(RROW + zp, rr_ref[place(zp), 0:1], rr_ref[place(zp), NY - 1 : NY])
    face, second = ([kap_ref[a, NZ - s] for a in range(3)] for s in range(2))
    part_0, part_y, part_x, part_yx = pair_stiffness(face, (None, None, None), second)
    diag = SELF * (face[0] + face[1] + face[2]) + part_0 + both(part_y, 1, 0)
    for i, plane in enumerate(face + [rr_ref[place(NZ - 1)], diag + both(part_x + both(part_yx, 1, 0), 1, 1)]):
        bulk_ref[i * NY : (i + 1) * NY] = plane
    planes = [kap_ref[a, NZ - s] for a in range(3) for s in range(2)] + [rr_ref[place(NZ - 1)]]
    lane = iota((NY, NX), 1)
    columns = jnp.zeros((NY, NX), F32)
    for g, plane in enumerate(planes):
        columns = jnp.where(lane >= 4 * g, roll(plane, 4 * g + 2, 1), columns)
    lane = iota((8, NX), 1)
    folded = columns[:8]
    for i in range(1, NY // 8):
        folded = jnp.where(lane >= 32 * i, roll(columns[8 * i : 8 * i + 8], 32 * i, 1), folded)
    bulk_ref[BCOL:BULK] = folded


def columns_kernel(kap_ref, rr_ref, left_ref, right_ref, ends_ref):
    lane = iota((NY, NX), 1)
    left = jnp.zeros((NY, NX), F32)
    right = jnp.zeros((NY, NX), F32)
    for a in range(3):
        for zp in range(NZ):
            at = 2 + a * KROWS + 2 * zp
            moved = roll(kap_ref[a, zp + 1], at, 1)
            left = jnp.where(lane >= at, moved, left)
            right = jnp.where(lane >= at - 2, moved, right)
    for zp in range(NZ):
        at = RLANE + zp
        moved = roll(rr_ref[place(zp)], at, 1)
        left = jnp.where(lane >= at, moved, left)
        right = jnp.where(lane >= at - 1, moved, right)
    left_ref[...] = left
    right_ref[...] = right
    row = iota((8, NX), 0)
    ends_ref[...] = end_tile(*(jnp.where(row < 4, v[:8], v[NY - 8 :]) for v in (left, right)))


def columns_beyond(left, right, moved):
    lane = iota(left.shape, 1)
    for a in range(3):
        for s in range(2):
            at = 2 + a * KROWS + 2 * (NZ + s)
            values = moved(2 * a + s, at)
            left = jnp.where((lane == at) | (lane == at + 1), values, left)
            right = jnp.where((lane == at - 2) | (lane == at - 1), values, right)
    at = RLANE + NZ
    values = moved(6, at)
    return jnp.where(lane == at, values, left), jnp.where(lane == at - 1, values, right)


def columns_beyond_kernel(left_in, right_in, bulk_ref, after_ref, left_ref, right_ref):
    folded = bulk_ref[BCOL:BULK]
    columns = jnp.concatenate([roll(folded, -32 * i, 1) for i in range(NY // 8)], axis=0)
    left_ref[...], right_ref[...] = columns_beyond(
        left_in[...], right_in[...], lambda g, x0: roll(columns, x0 - 4 * g - 2, 1)
    )


def send_rows_kernel(far_ref, mine_ref, ends_ref, ya_in, yb_in, after_ref, ya_ref, yb_ref, u0_ref, u1_ref, u2_ref):
    phase = lax.rem(lax.axis_index("gy"), 3)
    row, lane = iota((8, NX), 0), iota((8, NX), 1)
    low, high = far_ref[16:32], far_ref[32:48]
    even = lax.rem(lax.axis_index("gy"), 2) == 0
    for ref, rows in ((ya_ref, jnp.where(even, high, low)), (yb_ref, jnp.where(even, low, high))):
        for i in range(6):
            ref[i * GROUP + NZ : (i + 1) * GROUP] = rows[2 * i : 2 * i + 2]
        ref[RROW + NZ : RROW + NZ + 1] = rows[12:13]
    is_right = ((row >> 1) & 1) == 1
    at = lane - jnp.where(is_right, 0, 2)
    within = at - jnp.where(at >= 2 * KROWS, 2 * KROWS, jnp.where(at >= KROWS, KROWS, 0))
    beyond = (at < RROW) & (within >= 2 * NZ)
    beyond = beyond | (lane == RLANE + NZ - is_right.astype(jnp.int32))
    tile = jnp.where(beyond, far_ref[8:16], ends_ref[...])
    turned = roll(tile, 4, 0)
    coarse = jnp.where(row < CY, mine_ref[0:8], far_ref[0:8])
    for slot, ref in enumerate((u0_ref, u1_ref, u2_ref)):
        ref[0:8] = coarse
        ref[8:16] = jnp.where(phase == slot, turned, tile)


def neighbours(slots):
    gy = lax.axis_index("gy")
    phase = lax.rem(gy, 3)
    zero = jnp.zeros(slots[0].shape, F32)
    hi = jnp.where(phase == 0, slots[0], jnp.where(phase == 1, slots[1], slots[2]))
    lo = jnp.where(phase == 0, slots[2], jnp.where(phase == 1, slots[0], slots[1]))
    return jnp.where(gy > 0, lo, zero), jnp.where(gy < lax.axis_size("gy") - 1, hi, zero)


def columns_more_kernel(r0_ref, r1_ref, r2_ref, mine_ref, left_in, right_in, xa_ref, xb_ref, left_ref, right_ref, cor_ref):
    gx = lax.axis_index("gx")
    lo, hi = neighbours([r0_ref[...], r1_ref[...], r2_ref[...]])
    lane, row = iota((8, NX), 1), iota((8, NX), 0)

    def halo(shift):
        above, below = roll(hi[8:16], -shift, 0), roll(lo[8:16], 6 - shift, 0)
        return jnp.where(row < 2, above, jnp.where(row >= 6, below, 0.0))

    left_ref[0:NY] = left_in[...]
    right_ref[0:NY] = right_in[...]
    left_ref[NY : NY + 8] = halo(0)
    right_ref[NY : NY + 8] = halo(2)
    even_x = gx % 2 == 0
    xa_ref[0:40] = jnp.where(even_x, right_ref[...], left_ref[...])
    xb_ref[0:40] = jnp.where(even_x, left_ref[...], right_ref[...])

    tiles = [lo[0:8], mine_ref[0:8], hi[0:8]]
    zc, xs = lane >> 5, lane & 31
    pair = jnp.where(zc < 2, zc, 3 - zc)
    own = (xs >= 4) & (xs < 20)
    low_half = lane < 64
    sides = [jnp.zeros((8, NX), F32), jnp.zeros((8, NX), F32)]
    for q in range(4):
        at = (q * 2 + pair) * CX + jnp.clip(xs - 4, 0, CX - 1)
        below, mine, above = ((v, roll(v, 4, 0)) for v in (jnp.where(own, take(t, at), 0.0) for t in tiles))
        first = jnp.where(row < 4, jnp.where(low_half, below[0], below[1]), jnp.where(low_half, mine[1], mine[0]))
        second = jnp.where(row < 4, jnp.where(low_half, above[0], above[1]), 0.0)
        whole = jnp.concatenate([first, second], axis=0)
        cor_ref[q] = whole
        for i, start in enumerate((4, CX)):
            for half, to in ((first, 4 * q), (second, 4 * q + 16)):
                sides[i] = jnp.where((xs >= to) & (xs < to + 4), roll(half, to - start, 1), sides[i])
    xa_ref[40:XPAY] = jnp.where(even_x, sides[1], sides[0])
    xb_ref[40:XPAY] = jnp.where(even_x, sides[0], sides[1])


def first_plane(to, zp, kap_ref, res, f_ref, p_ref, s1_ref, rim):
    below, k, above = ([kap_ref[a, zp + i] for a in range(3)] for i in range(3))
    part_0, part_y, part_x, part_yx = pair_stiffness(k, below, above)
    diag = SELF * (k[0] + k[1] + k[2]) + part_0 + both(part_y, 1, 0)
    inv = 1.0 / (diag + both(part_x + both(part_yx, 1, 0), 1, 1))
    f = jnp.where(rim, 0.0, WEIGHT_ONE * res * inv)
    f_ref[zp + 1] = f
    for a in range(3):
        p_ref[a, zp + 1] = k[a] * f
    s1_ref[to] = WEIGHT_TWO * inv


def image_plane(to, zp, kap_ref, f_ref, p_ref, s1_ref, s2_ref, rim):
    k = [kap_ref[a, zp + 1] for a in range(3)]
    p = [p_ref[a, zp + 1] for a in range(3)]
    d0, d1, d2 = (p_ref[a, zp] + p_ref[a, zp + 2] for a in range(3))
    f, fz = f_ref[zp + 1], f_ref[zp] + f_ref[zp + 2]
    own_y = 0.5 * p[1] + 0.125 * (d0 + d1)
    own_yx = 0.125 * (p[1] + p[2]) + (1.0 / 24.0) * (d0 + d1 + d2)
    own_x = 0.5 * p[2] + 0.125 * (d0 + d2)
    fy, fyz = both(f, 1, 0), both(fz, 1, 0)
    t24, t8 = (1.0 / 24.0) * fyz, 0.125 * fyz
    total = 0.5 * d0 + both(own_y, 1, 0) + both(own_x + both(own_yx, 1, 0), 1, 1)
    total = total + k[0] * (0.5 * fz + t8 + both(0.125 * fz + t24, 1, 1))
    total = total + k[1] * (0.5 * fy + t8 + both(0.125 * fy + t24, 1, 1))
    total = total + k[2] * both(0.5 * f + 0.125 * (fz + fy) + t24, 1, 1)
    scaled = s1_ref[to]
    s1_ref[to] = jnp.where(rim, total, scaled)
    s2_ref[to] = jnp.where(rim, 0.0, KEEP * f + scaled * total)


def plane_rim():
    row, lane = iota((NY, NX), 0), iota((NY, NX), 1)
    return (row == 0) | (row == NY - 1) | (lane == 0) | (lane == NX - 1)


def inner_first_kernel(kap_ref, rr_ref, s1_ref, f_ref, p_ref):
    rim = plane_rim()
    f_ref[0] = jnp.zeros((NY, NX), F32)
    p_ref[:, 0] = jnp.zeros((3, NY, NX), F32)

    @pl.loop(0, 3)
    def _(i):
        for j in range(5):
            zp = i * 5 + j
            first_plane(zp, zp, kap_ref, rr_ref[place(zp)], f_ref, p_ref, s1_ref, rim)


def inner_image_kernel(kap_ref, f_ref, p_ref, s1_in, s1_ref, s2_ref):
    rim = plane_rim()

    @pl.loop(0, 2)
    def _(i):
        for j in range(7):
            image_plane(i * 7 + j, i * 7 + j, kap_ref, f_ref, p_ref, s1_ref, s2_ref, rim)


def outer_kernel(kap_ref, rr_ref, bulk_ref, f_in, p_in, s1_in, s2_in, after_ref, s1_ref, s2_ref, k_ref, f_ref, p_ref):
    rim = plane_rim()
    for a in range(3):
        for i in range(3):
            k_ref[a, i] = kap_ref[a, NZ - 2 + i]
        k_ref[a, 3] = bulk_ref[a * NY : (a + 1) * NY]
        for i in range(2):
            p_ref[a, i] = p_in[a, NZ - 2 + i]
    for i in range(2):
        f_ref[i] = f_in[NZ - 2 + i]
    first_plane(NZ - 1, 1, k_ref, rr_ref[place(NZ - 1)], f_ref, p_ref, s1_ref, rim)
    k0, k1, k2 = (k_ref[a, 2] for a in range(3))
    diag = bulk_ref[4 * NY : 5 * NY] + 0.5 * k0 + both(0.125 * (k0 + k1), 1, 0)
    diag = diag + both(0.125 * (k0 + k2) + both((1.0 / 24.0) * (k0 + k1 + k2), 1, 0), 1, 1)
    f = jnp.where(rim, 0.0, WEIGHT_ONE * bulk_ref[3 * NY : 4 * NY] / diag)
    f_ref[3] = f
    for a in range(3):
        p_ref[a, 3] = k_ref[a, 3] * f
    for i in range(2):
        image_plane(NZ - 2 + i, i, k_ref, f_ref, p_ref, s1_ref, s2_ref, rim)


def along_x(values):
    return both(values, 1, 1)


def edge_rows_kernel(ya_ref, yb_ref, ra_ref, rb_ref, s1_in, s2_in, s1_ref, s2_ref):
    size = 24
    row, lane = iota((size, NX), 0), iota((size, NX), 1)
    inner = (lane > 0) & (lane < NX - 1)
    near = inner & (row < NZ + 1)
    inner16 = inner[:NZ]
    gy = lax.axis_index("gy")
    even = lax.rem(gy, 2) == 0
    ya, yb, ra, rb = ya_ref[...], yb_ref[...], ra_ref[...], rb_ref[...]
    low, high = jnp.where(even, yb, ya), jnp.where(even, ya, yb)
    zero = jnp.zeros((YPAY, NX), F32)
    lo = jnp.where(gy > 0, jnp.where(even, rb, ra), zero)
    hi = jnp.where(gy < lax.axis_size("gy") - 1, jnp.where(even, ra, rb), zero)
    for other, mine, face, second in (
        (lo, low, 0, 1),
        (hi, high, NY - 1, NY - 2),
    ):

        def group(source, at):
            return jnp.where(row < GROUP, source[at : at + size], 0.0)

        k = [[group(other, a * KROWS + s * GROUP) for a in range(3)] for s in (0, 1)]
        k += [[group(mine, a * KROWS + s * GROUP) for a in range(3)] for s in (1, 0)]
        parts = [pair_stiffness(v, (None, None, None), [both(u, 1, 0) for u in v]) for v in k]
        res = [None] + [jnp.where(row < NZ + 1, v[YPAY - size :], 0.0) for v in (roll(other, 4 - 8, 0), roll(mine, 4 - 8, 0))]
        f, inv = [None] * 3, [None] * 3
        for c in (1, 2):
            diag = SELF * (k[c][0] + k[c][1] + k[c][2]) + parts[c][0] + parts[c - 1][1] + parts[c + 1][1]
            inv[c] = 1.0 / (diag + along_x(parts[c][2] + parts[c - 1][3] + parts[c + 1][3]))
            f[c] = jnp.where(near, WEIGHT_ONE * res[c] * inv[c], 0.0)
        p = [None] + [[v * f[c] for v in k[c]] for c in (1, 2)]
        d = [None] + [[both(v, 1, 0) for v in p[c]] for c in (1, 2)]
        fz = [None] + [both(f[c], 1, 0) for c in (1, 2)]

        def row_parts(c):
            return (
                0.5 * p[c][1] + 0.125 * (d[c][0] + d[c][1]),
                0.125 * (p[c][1] + p[c][2]) + (1.0 / 24.0) * (d[c][0] + d[c][1] + d[c][2]),
            )

        own_y, own_yx = row_parts(1)
        own_x = 0.5 * p[2][2] + 0.125 * (d[2][0] + d[2][2])
        t24, t8 = (1.0 / 24.0) * fz[1], 0.125 * fz[1]
        total = 0.5 * d[2][0] + own_y + along_x(own_x + own_yx)
        total = total + k[2][0] * (0.5 * fz[2] + t8 + along_x(0.125 * fz[2] + t24))
        total = total + k[2][1] * (0.5 * f[1] + t8 + along_x(0.125 * f[1] + t24))
        total = total + k[2][2] * along_x(0.5 * f[2] + 0.125 * (fz[2] + f[1]) + t24)
        total = total[:NZ] + s1_ref[:, face, :]
        scaled = WEIGHT_TWO * inv[2][:NZ]
        s1_ref[:, face, :] = jnp.where(inner16, scaled, total)
        s2_ref[:, face, :] = jnp.where(inner16, KEEP * f[2][:NZ] + scaled * total, 0.0)

        own_y, own_yx = row_parts(2)
        t24, t8 = (1.0 / 24.0) * fz[2], 0.125 * fz[2]
        total = own_y + along_x(own_yx) + k[3][0] * (t8 + along_x(t24))
        total = total + k[3][1] * (0.5 * f[2] + t8 + along_x(0.125 * f[2] + t24))
        total = (total + k[3][2] * along_x(0.125 * f[2] + t24))[:NZ]
        scaled = s1_ref[:, second, :]
        s1_ref[:, second, :] = jnp.where(inner16, scaled, scaled + total)
        s2_ref[:, second, :] = s2_ref[:, second, :] + jnp.where(inner16, scaled * total, 0.0)


def slab_lanes(left):
    lane = iota((8, NX), 1)
    zp, c = lane >> 2, lane & 3
    outer = c < 2 if left else c >= 2
    real = zp < GROUP
    near = ((c == 1) | (c == 2)) & (zp < NZ + 1)
    offset = jnp.where(outer, 0, 2) if left else jnp.where(outer, 2, 0)
    offset_r = jnp.where(outer, RLANE - 1, RLANE) if left else jnp.where(outer, RLANE, RLANE - 1)
    sources = [jnp.where(real, a * KROWS + 2 * zp + (c & 1) + offset, 0) for a in range(3)]
    sources.append(jnp.where(near, zp + offset_r, 0))
    return outer, [real] * 3 + [near], sources


def slab_kernel(left_ref, right_ref, after_ref, slab_ref):
    for side, pack in enumerate((left_ref, right_ref)):
        outer, keeps, sources = slab_lanes(side == 0)
        for q in range(4):
            for i in range(0, NY + 8, 8):
                piece = take(pack[i : i + 8], sources[q])
                slab_ref[side, q, i : i + 8] = jnp.where(keeps[q] & ~outer, piece, 0.0)


def rim_kernel(s1_ref, s2_ref, rim1_ref, rim2_ref):
    lane = iota((NY, NX), 1)
    for source, rim in ((s1_ref, rim1_ref), (s2_ref, rim2_ref)):
        values = jnp.zeros((NY, NX), F32)
        for zp in range(NZ):
            values = jnp.where(lane >= 4 * zp, roll(source[zp], 4 * zp + 2, 1), values)
        rim[...] = values


def slab_terms(mine, other, rim1, rim2, left):
    rows = NY + 8
    outer, keeps, sources = slab_lanes(left)

    def spread(q):
        pieces = []
        for i in range(0, rows, 8):
            pieces.append(jnp.where(keeps[q] & outer, take(other[i : i + 8], sources[q]), mine[q, i : i + 8]))
        return jnp.concatenate(pieces, axis=0)

    k = [spread(a) for a in range(3)]
    res = spread(3)
    c = iota((rows, NX), 1) & 3
    near = jnp.concatenate([keeps[3]] * (rows // 8), axis=0)

    dz = [both(v, 4, 1) for v in k]
    part_0, part_y, part_x, part_yx = pair_stiffness(k, (None, None, None), dz)
    diag = SELF * (k[0] + k[1] + k[2]) + part_0 + both(part_y, 1, 0)
    inv = 1.0 / (diag + both(part_x + both(part_yx, 1, 0), 1, 1))
    f = jnp.where(near, WEIGHT_ONE * res * inv, 0.0)

    def from_outer(values):
        return roll(values, 1 if left else -1, 1)

    p = [v * f for v in k]
    d0, d1, d2 = (both(v, 4, 1) for v in p)
    own_y = 0.5 * p[1] + 0.125 * (d0 + d1)
    own_yx = 0.125 * (p[1] + p[2]) + (1.0 / 24.0) * (d0 + d1 + d2)
    own_x = 0.5 * p[2] + 0.125 * (d0 + d2)
    fz = both(f, 4, 1)
    fy, fyz = both(f, 1, 0)[:NY], both(fz, 1, 0)[:NY]
    fc, fz = f[:NY], fz[:NY]
    k = [v[:NY] for v in k]
    t24, t8 = (1.0 / 24.0) * fyz, 0.125 * fyz
    total = 0.5 * d0[:NY] + both(own_y, 1, 0)[:NY] + from_outer(own_x[:NY] + both(own_yx, 1, 0)[:NY])
    total = total + k[0] * (0.5 * fz + t8 + from_outer(0.125 * fz + t24))
    total = total + k[1] * (0.5 * fy + t8 + from_outer(0.125 * fy + t24))
    total = total + k[2] * from_outer(0.5 * fc + 0.125 * (fz + fy) + t24)
    face = (c == 2 if left else c == 1)[:NY]
    return jnp.where(face, KEEP * fc + WEIGHT_TWO * inv[:NY] * (total + rim1), rim2 + rim1 * total)


def coarse_solve(cor_ref, lower, upper):
    xs = iota((8, NX), 1) & 31
    arrays = []
    for q in range(4):
        halves = []
        for i, from_ in enumerate((4 * q, 4 * q + 16)):
            half = jnp.where(xs < 4, roll(lower, -from_, 1), cor_ref[q, 8 * i : 8 * i + 8])
            halves.append(jnp.where((xs >= 20) & (xs < 24), roll(upper, 20 - from_, 1), half))
        arrays.append(jnp.concatenate(halves, axis=0))
    kc, rhs = arrays[:3], arrays[3]
    lane = iota((16, NX), 1)

    def sides(values, axis):
        if axis == 0:
            return roll(values, 32, 1), roll(values, -32, 1)
        return roll(values, 1, axis - 1), roll(values, -1, axis - 1)

    within = [(lane >= 32, lane < 96), (None, None), (None, None)]
    diag = (1.0 + MASS / 3.0) * (kc[0] + kc[1] + kc[2])
    couple = []
    for a in range(3):
        for v, real in zip(sides(kc[a], a), within[a]):
            half = 0.5 * v if real is None else jnp.where(real, 0.5 * v, 0.0)
            diag = diag + half
            half = 0.5 * kc[a] + half
            couple.append(half if real is None else jnp.where(real, half, 0.0))
    inside = kc[0] > 0.0
    scaled = jnp.where(inside, OMEGA / jnp.where(inside, diag, 1.0), 0.0)
    couple = [scaled * v for v in couple]
    start = scaled * rhs
    estimate = start
    for _ in range(CITERS - 1):
        t = [v * u for v, u in zip(couple, [u for a in range(3) for u in sides(estimate, a)])]
        estimate = (start + (1.0 - OMEGA) * estimate) + (((t[0] + t[1]) + (t[2] + t[3])) + (t[4] + t[5]))
    return estimate[0:8]


def last_kernel(
    rb_ref, ra_ref, slab_ref, cor_ref, rim1_ref, rim2_ref, s2_ref, sel_ref, out_hbm, est_hbm, out_ref, est_ref, sems
):
    gx, gz = lax.axis_index("gx"), lax.axis_index("gz")
    even = gx % 2 == 0
    zero = jnp.zeros((XPAY, NX), F32)
    right = jnp.where(gx < lax.axis_size("gx") - 1, jnp.where(even, ra_ref[...], rb_ref[...]), zero)
    left = jnp.where(gx > 0, jnp.where(even, rb_ref[...], ra_ref[...]), zero)
    rim1, rim2 = rim1_ref[...], rim2_ref[...]
    from_left = slab_terms(slab_ref[0], left[:40], rim1, rim2, True)
    from_right = slab_terms(slab_ref[1], right[:40], rim1, rim2, False)
    lane = iota((NY, NX), 1)
    faces = jnp.where((lane & 3) < 2, from_right, from_left)

    estimate = coarse_solve(cor_ref, left[40:XPAY], right[40:XPAY])
    lane8 = iota((8, NX), 1)
    rim = (lane < 2) | (lane >= NX - 2)
    step = 4
    for zc in range(CZ):
        z_out = jnp.where(gz == 0, zc, CZ - 1 - zc)
        est_ref[z_out] = roll(estimate, -(zc * 32 + 4), 1)[4:8, 0:CX]
    copies = [pltpu.make_async_copy(est_ref, est_hbm, sems.at[NZ // step])]
    copies[0].start()
    for zc in range(CZ):
        wide = take(estimate, zc * 32 + 4 + (lane8 >> 3))
        fine = jnp.concatenate([jnp.broadcast_to(wide[4 + y : 5 + y], (BLK, NX)) for y in range(CY)], axis=0)
        for i in range(BLK):
            zp = zc * BLK + i
            z = jnp.where(gz == 0, zp, NZ - 1 - zp)
            out_ref[z] = jnp.where(rim, roll(faces, -(4 * zp + 2), 1), s2_ref[zp]) + sel_ref[z] * fine
            if zp % step == step - 1:
                planes = pl.ds(jnp.where(gz == 0, zp + 1 - step, NZ - 1 - zp), step)
                copies.append(pltpu.make_async_copy(out_ref.at[planes], out_hbm.at[planes], sems.at[zp // step]))
                copies[-1].start()
    for copy in copies:
        copy.wait()


def near(values):
    return pltpu.with_memory_space_constraint(values, pltpu.VMEM)


def call(kernel, inputs, outputs, scratch=(), aliases=None, us=0.1, name=None, in_space=pltpu.VMEM, out_spaces=None):
    return pl.pallas_call(
        kernel,
        out_shape=outputs,
        in_specs=[pl.BlockSpec(memory_space=in_space)] * len(inputs),
        out_specs=[pl.BlockSpec(memory_space=v) for v in out_spaces or [pltpu.VMEM] * len(outputs)],
        scratch_shapes=list(scratch),
        input_output_aliases=aliases or {},
        cost_estimate=pl.CostEstimate(flops=int(us * 1e9), bytes_accessed=0, transcendentals=0),
        compiler_params=pltpu.CompilerParams(vmem_limit_bytes=32 * 2**20),
        name=name,
    )(*inputs)


def vmem(*shape):
    return pltpu.VMEM(shape, F32)


def exchange(values, sizes, move):
    nx, ny, nz = sizes
    pairs = []
    for x in range(nx):
        for y in range(ny):
            for z in range(nz):
                a, b, c = move(x, y, z)
                pairs.append(((x * ny + y) * nz + z, (a * ny + b) * nz + c))
    return lax.ppermute(values, ("gx", "gy", "gz"), pairs)


def solution(mesh):
    sizes = (mesh.shape["gx"], mesh.shape["gy"], mesh.shape["gz"])
    nx, ny, nz = sizes

    def swap_z(values):
        return exchange(values, sizes, lambda x, y, z: (x, y, nz - 1 - z))

    def swap_y(values, slots, slot):
        def move(x, y, z):
            b = y + 1 if y % slots == slot else y - 1 if (y - 1) % slots == slot else -1
            return (x, b, z) if 0 <= b < ny else (x ^ 1, y, z)

        return exchange(values, sizes, move)

    def swap_x(values, odd):
        return exchange(values, sizes, lambda x, y, z: ((x + 1 if x % 2 == odd else x - 1) % nx, y, z))

    def body(residual_in, labels, factor, basis, basis_index):
        inputs = [residual_in, labels, factor, basis, basis_index]
        kap, rr, sel, urgent = call(
            first_kernel,
            [pltpu.with_memory_space_constraint(v, pltpu.HBM) for v in inputs],
            [vmem(3, NZ + 1, NY, NX), vmem(NZ, NY, NX), vmem(NZ, NY, NX), vmem(ZURGENT, NX)],
            [
                pltpu.VMEM(labels.shape, jnp.int32),
                pltpu.VMEM(factor.shape, F32),
                pltpu.VMEM(basis.shape, F32),
                pltpu.VMEM(basis_index.shape, jnp.int32),
                pltpu.VMEM((4, BLK, BLK, NX), F32),
                pltpu.VMEM((64, NX), F32),
                pltpu.SemaphoreType.DMA((2,)),
                pltpu.SemaphoreType.DMA((len(PARTS), 3)),
            ],
            us=1.8,
            name="stiffness",
            in_space=pltpu.HBM,
        )
        kap, rr, sel, urgent = near(kap), near(rr), near(sel), near(urgent)
        zu = near(swap_z(urgent))
        payloads = [vmem(YPAY, NX)] * 2
        ya, yb, bulk = call(rows_kernel, [kap, rr], payloads + [vmem(BULK, NX)], name="rows")
        zb = near(swap_z(near(bulk)))
        left, right, ends = call(
            columns_kernel, [kap, rr], [vmem(NY, NX), vmem(NY, NX), vmem(8, NX)], us=0.4, name="columns"
        )
        s1, f, p = call(
            inner_first_kernel,
            [kap, rr],
            [vmem(NZ, NY, NX), vmem(NZ, NY, NX), vmem(3, NZ, NY, NX)],
            us=0.6,
            name="inner_first",
        )
        s1, f, p = near(s1), near(f), near(p)
        s1, s2 = call(
            inner_image_kernel,
            [kap, f, p, s1],
            [vmem(NZ, NY, NX), vmem(NZ, NY, NX)],
            aliases={3: 0},
            us=0.7,
            name="inner_image",
        )
        s1, s2 = near(s1), near(s2)
        sent = call(
            send_rows_kernel,
            [zu, urgent, near(ends), near(ya), near(yb), s2],
            payloads + [vmem(URGENT, NX)] * 3,
            aliases={3: 0, 4: 1},
            us=10.0,
            name="send_rows",
        )
        sent = [near(v) for v in sent]
        first, last = sent[2:], sent[:2]
        first_in = [near(swap_y(v, 3, slot)) for slot, v in enumerate(first)]
        last_in = [near(swap_y(v, 2, slot)) for slot, v in enumerate(last)]
        left, right = call(
            columns_beyond_kernel,
            [near(left), near(right), zb, first[2]],
            [vmem(NY, NX), vmem(NY, NX)],
            aliases={0: 0, 1: 1},
            us=100.0,
            name="columns_beyond",
        )
        xa, xb, left, right, cor = call(
            columns_more_kernel,
            first_in + [first[2], near(left), near(right)],
            [vmem(XPAY, NX), vmem(XPAY, NX), vmem(40, NX), vmem(40, NX), vmem(4, 16, NX)],
            us=1.0,
            name="columns_more",
        )
        xa, xb = near(xa), near(xb)
        vb, va = near(swap_x(xb, 1)), near(swap_x(xa, 0))
        s1, s2 = call(
            outer_kernel,
            [kap, rr, zb, f, p, s1, s2, xa],
            [vmem(NZ, NY, NX), vmem(NZ, NY, NX)],
            [pltpu.VMEM((3, 4, NY, NX), F32), pltpu.VMEM((4, NY, NX), F32), pltpu.VMEM((3, 4, NY, NX), F32)],
            aliases={5: 0, 6: 1},
            us=0.25,
            name="outer",
        )
        s1, s2 = call(
            edge_rows_kernel,
            last + last_in + [near(s1), near(s2)],
            [vmem(NZ, NY, NX), vmem(NZ, NY, NX)],
            aliases={4: 0, 5: 1},
            us=0.4,
            name="edge_rows",
        )
        (slab,) = call(slab_kernel, [near(left), near(right), xa], [vmem(2, 4, 40, NX)], us=0.1, name="slab")
        rim1, rim2 = call(rim_kernel, [near(s1), near(s2)], [vmem(NY, NX), vmem(NY, NX)], us=0.2, name="rim")
        out, estimate = call(
            last_kernel,
            [vb, va, near(slab), near(cor), near(rim1), near(rim2), near(s2), sel],
            [jax.ShapeDtypeStruct((NZ, NY, NX), F32), jax.ShapeDtypeStruct((CZ, CY, CX), F32)],
            [pltpu.VMEM((NZ, NY, NX), F32), pltpu.VMEM((CZ, CY, CX), F32), pltpu.SemaphoreType.DMA((5,))],
            us=1.5,
            name="last",
            out_spaces=[pltpu.HBM, pltpu.HBM],
        )
        return out, estimate

    in_specs = (
        P("gz", "gy", "gx"),
        P("gz", "gy", "gx"),
        P(None, "gz", "gy", "gx"),
        P(),
        P("gz", "gy", "gx"),
    )
    out_specs = (P("gz", "gy", "gx"), P("gz", "gy", "gx"))
    return jax.shard_map(body, mesh=mesh, in_specs=in_specs, out_specs=out_specs, check_vma=False)
```
